32 devices in a mesh: cell: 8 (over y, x, core), lane: 4 (over z).
Axes of the slice: x: 2, y: 2, z: 4, core: 2. Of those that a mesh axis runs over, the one named last changes fastest.
Arguments:
- channel: float32 [8, 64, 2, 16, 256], P('cell', 'lane'), may hold values from -8 to 8
- symbols: bfloat16 [8, 16, 2, 2, 3072], P('cell'), may hold values from -4 to 4
- layers: int32 [8, 256], P('cell'), may hold values from 0 to 16, as said below
- user_ids: int32 [8, 16, 256], P('cell'), may hold values from 0 to 127
- user_power: float32 [8, 128], P('cell'), may hold values from 0.25 to 4
- neighbours: int32 [8, 6], replicated, may hold values from 0 to 7, as said below
- coupling: float32 [8, 6], replicated, may hold values from 0.05 to 0.5
Outputs:
- time_samples: float32 [8, 64, 2, 2, 4096], P('cell', 'lane')
The draws below stay inside these ranges and needn't reach their ends.
Inputs may be any that keep to these rules, and one draw needn't show every extreme that they name: Some block of some cell has all 16 layers granted; for every index of the cell axis and every group of 32 aligned blocks, the layers of that index's 1 cells over the group sum to at most 192, and to exactly 192 for some index and group. `neighbours`: a cell never lists itself.
All inputs are finite; a program needn't handle non-finite values.
Results may differ from the reference program's by a relative error of at most 0.0029.
Values may be sent and summed in bfloat16 or wider, within the bound.
No kernel may reach another device: no remote copies, remote signals or barrier semaphores. Data moves between devices by JAX's collectives and lax.ppermute only.
A program may use at most 64 MiB of HBM per device.

```python
import math
import jax
import jax.numpy as jnp
from jax import lax

TX_ANTENNA_COUNT = 64
MAX_LAYERS = 16
PRBS = 256
SUBC = 12
NFFT = 4096
SYMS = 2
USERS = 128
NEIGH = 6
NS_STEPS = 6
CELL_DEV = 1
POOL_CELL_COUNT = 8
SUBCARRIERS = 3072
BLOCK_GROUP = 32
PACK_CAP = 192


def draw_channel(key, part):
    base_station_key, row_key_split, antenna_key = jax.random.split(key, 3)
    shape = (POOL_CELL_COUNT, TX_ANTENNA_COUNT, 2, MAX_LAYERS, PRBS)
    base = jax.random.normal(base_station_key, shape, jnp.float32)
    row_scale = jnp.exp(jax.random.uniform(row_key_split, (POOL_CELL_COUNT, 1, 1, MAX_LAYERS, PRBS), jnp.float32, math.log(0.3), math.log(3.0)))
    antenna_gain_scale = jnp.exp(jax.random.uniform(antenna_key, (POOL_CELL_COUNT, TX_ANTENNA_COUNT, 1, 1, 1), jnp.float32, math.log(0.3), math.log(3.0)))
    values = base * row_scale * antenna_gain_scale * (0.5 / math.sqrt(TX_ANTENNA_COUNT))
    return jnp.clip(values, -8.0, 8.0).astype(jnp.float32)


def draw_layers(key, part):
    key_level, base_station_key, key_dev, key_group = jax.random.split(key, 4)
    level = jax.random.randint(key_level, (POOL_CELL_COUNT, 1), 2, MAX_LAYERS + 1)
    base = jax.random.randint(base_station_key, (POOL_CELL_COUNT, PRBS), 0, level + 1)
    groups = POOL_CELL_COUNT // CELL_DEV
    grouped = base.reshape(groups, CELL_DEV, groups, BLOCK_GROUP)
    totals = jnp.sum(grouped, axis=(1, 3), keepdims=True)
    capped = jnp.where(totals > PACK_CAP, grouped * PACK_CAP // jnp.maximum(totals, 1), grouped)
    entries = CELL_DEV * BLOCK_GROUP
    flat_pos = lax.broadcasted_iota(jnp.int32, (1, CELL_DEV, 1, BLOCK_GROUP), 1) * BLOCK_GROUP + lax.broadcasted_iota(jnp.int32, (1, CELL_DEV, 1, BLOCK_GROUP), 3)
    leftover = PACK_CAP - MAX_LAYERS
    spread_over = max(entries - 1, 1)
    share = leftover // spread_over
    extra = leftover % spread_over
    filled = jnp.where(flat_pos == 0, MAX_LAYERS, share + (flat_pos - 1 < extra).astype(jnp.int32))
    pick_dev = jax.random.randint(key_dev, (), 0, groups)
    pick_group = jax.random.randint(key_group, (), 0, groups)
    dev_iota = lax.broadcasted_iota(jnp.int32, (groups, 1, groups, 1), 0)
    group_iota = lax.broadcasted_iota(jnp.int32, (groups, 1, groups, 1), 2)
    chosen = jnp.logical_and(dev_iota == pick_dev, group_iota == pick_group)
    result = jnp.where(chosen, filled, capped)
    return result.reshape(POOL_CELL_COUNT, PRBS).astype(jnp.int32)


def draw_neighbours(key, part):
    offsets = jax.random.randint(key, (POOL_CELL_COUNT, NEIGH), 1, POOL_CELL_COUNT)
    rows = jnp.arange(POOL_CELL_COUNT, dtype=jnp.int32)[:, None]
    return ((rows + offsets) % POOL_CELL_COUNT).astype(jnp.int32)


def touch_ends(values, rng, smallest, high):
    longest = values.shape.index(max(values.shape))
    spots = []
    for shift in (0, 1):
        where = [jax.random.randint(jax.random.fold_in(rng, axis), (), 0, length) for axis, length in enumerate(values.shape)]
        where[longest] = (where[longest] + shift) % values.shape[longest]
        spots.append(tuple(where))
    return values.at[spots[0]].set(smallest).at[spots[1]].set(high)


def steps_of(own_key, shape, pieces, low, largest):
    factor_of = 1.0
    for position, parts in pieces:
        draws = jax.random.uniform(jax.random.fold_in(jax.random.fold_in(own_key, 6), position), (parts,), jnp.float32, low / len(pieces), largest / len(pieces))
        factor_of = factor_of * jnp.repeat(jnp.exp(draws), shape[position] // parts).reshape((-1,) + (1,) * (len(shape) - 1 - position))
    return factor_of


def normal_values(rng, shape, scale, reach, cuts=(), held_as=jnp.bfloat16):
    values = jax.random.normal(rng, shape, jnp.float32) * scale
    if len(cuts) > 0:
        values = steps_of(rng, shape, cuts, -0.22, 0.18) * values
    return jnp.clip(values, min=-reach, max=reach).astype(held_as)


def setup_inputs(seed: int = 0) -> dict:
    splits = jax.random.split(jax.random.key(seed), 8)
    channel = draw_channel(jax.random.fold_in(splits[7], 71), 0)
    symbols = normal_values(splits[1], (POOL_CELL_COUNT, MAX_LAYERS, 2, SYMS, SUBCARRIERS), 0.7, 4.0, ((0, 8),))
    layers = draw_layers(jax.random.fold_in(splits[7], 71), 0)
    user_ids = touch_ends(jax.random.randint(splits[3], (POOL_CELL_COUNT, MAX_LAYERS, PRBS), 0, USERS), jax.random.fold_in(splits[3], 1), 0, USERS - 1).astype(jnp.int32)
    user_power = jnp.clip(jnp.exp(math.log(4.0) - 2.7725887 * jax.random.uniform(splits[4], (POOL_CELL_COUNT, USERS), jnp.float32) ** steps_of(splits[4], (POOL_CELL_COUNT, USERS), ((0, 8),), -0.2, 0.2)), 0.25, 4.0)
    neighbours = draw_neighbours(jax.random.fold_in(splits[7], 71), 0)
    coupling = jnp.clip(jnp.exp(jax.random.uniform(splits[6], (POOL_CELL_COUNT, NEIGH), jnp.float32, math.log(0.05), math.log(0.5))), 0.05, 0.5)
    return {"channel": channel, "symbols": symbols, "layers": layers, "user_ids": user_ids, "user_power": user_power, "neighbours": neighbours, "coupling": coupling}


NORM_EPS = 1e-06
NOISE_FLOOR = 0.05
HIGHEST = lax.Precision.HIGHEST

def mix(form, left, right):
    return jnp.einsum(form, left, right, precision=HIGHEST)

def solve_cell(packed):
    chan, symbol_block, granted, amplitude, sigma = packed
    masked = chan * granted[None, None, :, :]
    chan_re = masked[:, 0]
    chan_im = masked[:, 1]
    gram_re = mix('alp,amp->lmp', chan_re, chan_re) + mix('alp,amp->lmp', chan_im, chan_im)
    gram_im = mix('alp,amp->lmp', chan_im, chan_re) - mix('alp,amp->lmp', chan_re, chan_im)
    identity = jnp.eye(MAX_LAYERS, dtype=jnp.float32)[:, :, None]
    reg_re = gram_re + identity * sigma[None, None, :]
    trace = lax.optimization_barrier(jnp.sum(jnp.diagonal(reg_re, axis1=0, axis2=1), axis=-1))
    inv_re = identity / trace[None, None, :]
    inv_im = jnp.zeros_like(inv_re)
    for iteration in range(NS_STEPS):
        prod_re = mix('lkp,kmp->lmp', reg_re, inv_re) - mix('lkp,kmp->lmp', gram_im, inv_im)
        prod_im = mix('lkp,kmp->lmp', reg_re, inv_im) + mix('lkp,kmp->lmp', gram_im, inv_re)
        fix_re = 2.0 * identity - prod_re
        fix_im = -prod_im
        next_re = mix('lkp,kmp->lmp', inv_re, fix_re) - mix('lkp,kmp->lmp', inv_im, fix_im)
        next_im = mix('lkp,kmp->lmp', inv_re, fix_im) + mix('lkp,kmp->lmp', inv_im, fix_re)
        inv_re, inv_im = (next_re, next_im)
    prec_re = mix('amp,mlp->alp', chan_re, inv_re) + mix('amp,mlp->alp', chan_im, inv_im)
    prec_im = mix('amp,mlp->alp', chan_re, inv_im) - mix('amp,mlp->alp', chan_im, inv_re)
    energy = lax.optimization_barrier(jnp.sum(prec_re * prec_re + prec_im * prec_im, axis=0))
    scale = amplitude / jnp.sqrt(energy + NORM_EPS)
    weights = jnp.stack([prec_re * scale[None], prec_im * scale[None]], 1).astype(jnp.bfloat16)
    weight_wide = weights.astype(jnp.float32)
    shaped = symbol_block.astype(jnp.float32).reshape(MAX_LAYERS, 2, SYMS, PRBS, SUBC)
    grid_re = jnp.einsum('alp,lspk->aspk', weight_wide[:, 0], shaped[:, 0]) - jnp.einsum('alp,lspk->aspk', weight_wide[:, 1], shaped[:, 1])
    grid_im = jnp.einsum('alp,lspk->aspk', weight_wide[:, 0], shaped[:, 1]) + jnp.einsum('alp,lspk->aspk', weight_wide[:, 1], shaped[:, 0])
    grid = lax.complex(grid_re, grid_im).reshape(TX_ANTENNA_COUNT, SYMS, SUBCARRIERS)
    half = SUBCARRIERS // 2
    filler = jnp.zeros((TX_ANTENNA_COUNT, SYMS, NFFT - SUBCARRIERS), grid.dtype)
    spectrum = jnp.concatenate([grid[..., half:], filler, grid[..., :half]], axis=-1)
    samples = jnp.fft.ifft(spectrum, axis=-1) * math.sqrt(NFFT)
    return jnp.stack([jnp.real(samples), jnp.imag(samples)], 1).astype(jnp.float32)

def reference(channel, symbols, layers, user_ids, user_power, neighbours, coupling):
    layer_iota = jnp.arange(MAX_LAYERS, dtype=jnp.int32)
    granted = (layer_iota[None, :, None] < layers[:, None, :]).astype(jnp.float32)
    cell_index = jnp.arange(POOL_CELL_COUNT, dtype=jnp.int32)
    power = user_power[cell_index[:, None, None], user_ids]
    amplitude = granted * jnp.sqrt(power)
    transmit = lax.optimization_barrier(jnp.sum(amplitude * amplitude, axis=1)) / MAX_LAYERS
    adjacency = lax.optimization_barrier(jnp.sum(jnp.where(neighbours[:, :, None] == cell_index[None, None, :], coupling[:, :, None], 0.0), axis=1))
    sigma = NOISE_FLOOR + jnp.dot(adjacency, transmit, precision=HIGHEST)
    return lax.map(solve_cell, (channel, symbols, granted, amplitude, sigma))
```

```python
import functools
import math

import jax
import jax.numpy as jnp
import numpy as np
from jax import lax
from jax.experimental import pallas as pl
from jax.experimental.pallas import tpu as pltpu
from jax.sharding import PartitionSpec as P

NFFT = 4096
NS_STEPS = 6
NORM_EPS = 1e-06
NOISE_FLOOR = 0.05
WIDE = 128
HALF = WIDE // 2
ROWS = 8

VMEM = pl.BlockSpec(memory_space=pltpu.VMEM)
SMEM = pl.BlockSpec(memory_space=pltpu.SMEM)


def lane_iota():
    return lax.broadcasted_iota(jnp.int32, (ROWS, WIDE), 1)


def row_iota():
    return lax.broadcasted_iota(jnp.int32, (ROWS, WIDE), 0)


def turn(value, shift):
    shift = shift % WIDE
    return value if shift == 0 else pltpu.roll(value, shift, 1)


def params(mib):
    return pltpu.CompilerParams(vmem_limit_bytes=mib * 1024 * 1024)


def power_kernel(layers_ref, ids_ref, power_ref, amp_ref, own_ref, *, chunk):
    order, blocks = ids_ref.shape
    users = power_ref.shape[1]
    rooted = jnp.sqrt(power_ref[...])
    sums = []
    for t in range(blocks // WIDE):
        spot = pl.ds(t * WIDE, WIDE)
        granted = layers_ref[:, spot]
        total = jnp.zeros((ROWS, WIDE), jnp.float32)
        for h in range(order // ROWS):
            ids = ids_ref[pl.ds(h * ROWS, ROWS), spot]
            picked = jnp.zeros((ROWS, WIDE), jnp.float32)
            for u in range(users // WIDE):
                table = jnp.broadcast_to(rooted[:, u * WIDE : (u + 1) * WIDE], (ROWS, WIDE))
                found = jnp.take_along_axis(table, ids % WIDE, axis=1, mode="promise_in_bounds")
                picked = jnp.where(ids // WIDE == u, found, picked)
            amp = jnp.where(row_iota() + h * ROWS < granted, picked, 0.0)
            amp_ref[pl.ds(h * ROWS, ROWS), spot] = amp
            total = total + amp * amp
        sums.append(jnp.sum(total, axis=0, keepdims=True) / order)
    start = lax.axis_index("lane") * chunk
    mine = jnp.broadcast_to(sums[0], (ROWS, WIDE))
    for t in range(1, len(sums)):
        mine = jnp.where(start // WIDE == t, jnp.broadcast_to(sums[t], (ROWS, WIDE)), mine)
    shift = lax.rem(start, WIDE)
    mine = pltpu.roll(mine, lax.rem(WIDE - shift, WIDE), 1)
    both = jnp.where(lane_iota() < HALF, mine, pltpu.roll(mine, HALF, 1))
    own_ref[...] = both[0:1]


def gram_kernel(channel_ref, layers_ref, out_ref, *, chunk):
    antennas, _, order, blocks = channel_ref.shape
    low = lane_iota() < HALF
    rows = row_iota()
    for t in range(blocks // WIDE):
        spot = pl.ds(t * WIDE, WIDE)
        granted = layers_ref[:, spot]
        inside = [rows + h * ROWS < granted for h in range(2)]
        for base in range(0, ROWS, 2):
            tops = (base, base + 1)
            acc = {}

            def add(key, value):
                acc[key] = value if key not in acc else acc[key] + value

            for a in range(antennas):
                re = [channel_ref[a, 0, pl.ds(h * ROWS, ROWS), spot] for h in range(2)]
                im = [channel_ref[a, 1, pl.ds(h * ROWS, ROWS), spot] for h in range(2)]
                for l in tops:
                    lre = channel_ref[a, 0, pl.ds(l, 1), spot]
                    lim = channel_ref[a, 1, pl.ds(l, 1), spot]
                    add((l, "re", 0), lre * re[0] + lim * im[0])
                    add((l, "re", 1), lre * re[1] + lim * im[1])
                    add((l, "im", 0), lim * re[0] - lre * im[0])
                    g = l + ROWS
                    gre = channel_ref[a, 0, pl.ds(g, 1), spot]
                    gim = channel_ref[a, 1, pl.ds(g, 1), spot]
                    add((g, "re", 1), gre * re[1] + gim * im[1])
                    add((g, "im", 0), gim * re[0] - gre * im[0])
                    add((g, "im", 1), gim * re[1] - gre * im[1])
            for l in tops:
                g = l + ROWS
                here = granted > l
                there = granted > g
                upper = [
                    jnp.where(rows >= l, acc[l, "re", 0], acc[l, "im", 0]),
                    acc[l, "re", 1],
                ]
                lower = [
                    acc[g, "im", 0],
                    jnp.where(rows >= l, acc[g, "re", 1], acc[g, "im", 1]),
                ]
                for h in range(2):
                    top = jnp.where(jnp.logical_and(inside[h], here), upper[h], 0.0)
                    bottom = jnp.where(jnp.logical_and(inside[h], there), lower[h], 0.0)
                    for z in range(t * WIDE // chunk, (t + 1) * WIDE // chunk):
                        off = z * chunk - t * WIDE
                        out_ref[z, pl.ds(l * 2 * ROWS + h * ROWS, ROWS), :] = jnp.where(
                            low, turn(top, -off), turn(bottom, HALF - off)
                        )


def solve_kernel(
    neigh_ref, coup_ref, parts_ref, trans_ref, out_ref, pack, gram, e_a, e_b, s_a, s_b, d_re, d_im
):
    order = 2 * ROWS
    low = lane_iota() < HALF
    rows = row_iota()
    sign = jnp.where(low, -1.0, 1.0)

    def at(l, h):
        return pl.ds(l * order + h * ROWS, ROWS)

    def column(l, h):
        return pl.ds(h * ROWS * order + l, ROWS, stride=order)

    def row(ref, l, k):
        return ref[pl.ds(l * order + k, 1), :]

    for l in range(ROWS):
        for h in range(2):
            value = parts_ref[0, at(l, h), :]
            for z in range(1, parts_ref.shape[0]):
                value = value + parts_ref[z, at(l, h), :]
            other = pltpu.roll(value, HALF, 1)
            pack[at(l, h), :] = jnp.where(low, value, other)
            pack[at(l + ROWS, h), :] = jnp.where(low, other, value)

    cell = lax.axis_index("cell")
    sigma = jnp.full((1, WIDE), NOISE_FLOOR, jnp.float32)
    for k in range(neigh_ref.shape[1]):
        sigma = sigma + coup_ref[cell, k] * trans_ref[pl.ds(neigh_ref[cell, k], 1), :]

    trace = order * sigma
    for l in range(order):
        trace = trace + row(pack, l, l)
    inverse = 1.0 / trace
    kept = 1.0 - sigma * inverse

    for l in range(order):
        for h in range(2):
            here = pack[at(l, h), :]
            across = pack[column(l, h), :]
            above = jnp.where(low, here, -across)
            below = jnp.where(low, across, here)
            if h * ROWS > l:
                value = above
            elif h * ROWS + ROWS - 1 < l:
                value = below
            else:
                value = jnp.where(rows + h * ROWS >= l, above, below)
                value = jnp.where(jnp.logical_and(rows + h * ROWS == l, ~low), 0.0, value)
            gram[at(l, h), :] = value
            error = -value * inverse
            total = error
            if h * ROWS <= l < h * ROWS + ROWS:
                spot = jnp.logical_and(rows + h * ROWS == l, low)
                error = error + jnp.where(spot, kept, 0.0)
                total = error + jnp.where(spot, 1.0, 0.0)
            e_a[at(l, h), :] = error
            s_a[at(l, h), :] = total

    def spread(ref):
        for l in range(order):
            for h in range(2):
                value = ref[at(l, h), :]
                other = pltpu.roll(value, HALF, 1)
                d_re[at(l, h), :] = jnp.where(low, value, other)
                d_im[at(l, h), :] = jnp.where(low, other, value)

    def products(jobs):
        for base in range(0, order, 2):
            halves = (0, 1) if base < ROWS else (1,)
            plain, crossed = {}, {}
            for l in (base, base + 1):
                for j, (_, _, start) in enumerate(jobs):
                    for h in halves:
                        if start is not None:
                            plain[l, j, h] = start[at(l, h), :]
            for k in range(order):
                right = {
                    (j, h): ref[at(k, h), :] for j, (ref, _, _) in enumerate(jobs) for h in halves
                }
                for l in (base, base + 1):
                    left_re = row(d_re, l, k)
                    left_im = row(d_im, l, k) if k != l else None
                    for (j, h), value in right.items():
                        key = (l, j, h)
                        term = left_re * value
                        plain[key] = plain[key] + term if key in plain else term
                        if left_im is not None:
                            term = left_im * value
                            crossed[key] = crossed[key] + term if key in crossed else term
            for (l, j, h), value in plain.items():
                cross = pltpu.roll(crossed[l, j, h], HALF, 1)
                jobs[j][1][at(l, h), :] = value + sign * cross
        for _, ref, _ in jobs:
            for l in range(ROWS, order):
                ref[at(l, 0), :] = -sign * ref[column(l, 0), :]

    spread(e_a)
    products([(e_a, e_b, None)])

    def two_steps(_, carry):
        spread(e_b)
        products([(e_b, e_a, None), (s_a, s_b, s_a)])
        spread(e_a)
        products([(e_a, e_b, None), (s_b, s_a, s_b)])
        return carry

    lax.fori_loop(0, (NS_STEPS - 2) // 2, two_steps, 0)
    spread(e_b)
    products([(s_a, s_b, s_a)])

    for l in range(order):
        for h in range(2):
            s_a[at(l, h), :] = s_b[at(l, h), :] * inverse
    spread(s_a)
    products([(gram, e_a, None)])

    energy = []
    for h in range(2):
        value = s_a[at(0, h), :] * e_a[at(0, h), :]
        for m in range(1, order):
            value = value + s_a[at(m, h), :] * e_a[at(m, h), :]
        energy.append(value + pltpu.roll(value, HALF, 1))
    last = jnp.where(low, energy[0], energy[1])
    for l in range(ROWS):
        for h in range(2):
            first = s_a[at(l, h), :]
            second = s_a[at(l + ROWS, h), :]
            where = rows + h * ROWS
            value = jnp.where(
                low,
                jnp.where(where >= l, first, pltpu.roll(first, HALF, 1)),
                jnp.where(where >= l + ROWS, pltpu.roll(second, HALF, 1), second),
            )
            for z in range(out_ref.shape[0]):
                out_ref[z, at(l, h), :] = value
    for z in range(out_ref.shape[0]):
        out_ref[z, pl.ds(order * ROWS, ROWS), :] = last


def arrange_kernel(symbols_ref, order_ref, channel_ref, sym_ref, chan_ref, stage):
    antennas, _, layers, blocks = channel_ref.shape
    tiles = blocks // WIDE
    span = symbols_ref.shape[1] // tiles
    for t in range(tiles):
        piece = symbols_ref[:, pl.ds(t * span, span)]
        for k in range(span // WIDE // 2):
            got = jnp.dot(
                piece,
                order_ref[:, pl.ds(k * 2 * WIDE, 2 * WIDE)],
                preferred_element_type=jnp.float32,
            )
            sym_ref[t, 2 * k] = got[:, :WIDE]
            sym_ref[t, 2 * k + 1] = got[:, WIDE:]
    for t in range(tiles):
        for a in range(antennas):
            for r in range(2):
                for h in range(layers // ROWS):
                    stage[t, pl.ds((a * 2 + r) * layers + h * ROWS, ROWS), :] = channel_ref[
                        a, r, pl.ds(h * ROWS, ROWS), pl.ds(t * WIDE, WIDE)
                    ]
        for r in range(2):
            for m in range(layers):
                for h in range(antennas // ROWS):
                    first = h * ROWS * 2 * layers + r * layers + m
                    chan_ref[t, r, m, pl.ds(h * ROWS, ROWS), :] = stage[
                        t, pl.ds(first, ROWS, stride=2 * layers), :
                    ]


def transmit_kernel(
    packs_ref,
    amp_ref,
    chan_ref,
    sym_ref,
    high_ref,
    rest_ref,
    twist_ref,
    out_ref,
    pack,
    scale,
    weight,
    grid_high,
    grid_rest,
    spec,
    *,
    chunk,
):
    tiles, _, order, antennas, _ = chan_ref.shape
    per_block, syms = sym_ref.shape[1], sym_ref.shape[2] // (2 * order)
    groups = antennas // ROWS
    lanes = lane_iota()

    for t in range(tiles):
        for i in range(2 * ROWS + 1):
            rows = pl.ds(i * ROWS, ROWS)
            first = second = None
            for z in range(t * WIDE // chunk, (t + 1) * WIDE // chunk):
                off = z * chunk - t * WIDE
                value = packs_ref[z, rows, :]
                if first is None:
                    first, second = value, pltpu.roll(value, HALF, 1)
                else:
                    first = jnp.where(lanes >= off, turn(value, off), first)
                    second = jnp.where(lanes >= off, turn(value, off - HALF), second)
            if i < 2 * ROWS:
                pack[t, rows, :] = first
                pack[t, pl.ds((i + 2 * ROWS) * ROWS, ROWS), :] = second
            else:
                for h, energy in enumerate((first, second)):
                    amp = amp_ref[pl.ds(h * ROWS, ROWS), pl.ds(t * WIDE, WIDE)]
                    scale[t, pl.ds(h * ROWS, ROWS), :] = amp / jnp.sqrt(energy + NORM_EPS)

    def row(t, l, m):
        return pack[t, pl.ds(l * order + m, 1), :]

    for t in range(tiles):
        for base in range(0, order, 4):
            acc = {}

            def add(key, value):
                acc[key] = value if key not in acc else acc[key] + value

            for m in range(order):
                chan = [
                    [chan_ref[t, r, m, pl.ds(g * ROWS, ROWS), :] for g in range(groups)]
                    for r in range(2)
                ]
                for l in range(base, base + 4):
                    inv_re = row(t, min(l, m), max(l, m))
                    inv_im = row(t, max(l, m), min(l, m)) if l != m else None
                    if l > m:
                        inv_im = -inv_im
                    for g in range(groups):
                        re, im = chan[0][g], chan[1][g]
                        if inv_im is None:
                            add((l, 0, g), re * inv_re)
                            add((l, 1, g), -(im * inv_re))
                        else:
                            add((l, 0, g), re * inv_re + im * inv_im)
                            add((l, 1, g), re * inv_im - im * inv_re)
            for (l, r, g), value in acc.items():
                value = value * scale[t, pl.ds(l, 1), :]
                weight[t, r, l, pl.ds(g * ROWS, ROWS), :] = value.astype(jnp.bfloat16).astype(
                    jnp.float32
                )

    def precode(k, carry):
        for t in range(tiles):
            acc = {}
            for l in range(order):
                w_re = [weight[t, 0, l, pl.ds(g * ROWS, ROWS), :] for g in range(groups)]
                w_im = [weight[t, 1, l, pl.ds(g * ROWS, ROWS), :] for g in range(groups)]
                for s in range(syms):
                    s_re = sym_ref[t, k, pl.ds((l * 2 + 0) * syms + s, 1), :]
                    s_im = sym_ref[t, k, pl.ds((l * 2 + 1) * syms + s, 1), :]
                    for g in range(groups):
                        re = w_re[g] * s_re - w_im[g] * s_im
                        im = w_re[g] * s_im + w_im[g] * s_re
                        if l == 0:
                            acc[s, g] = (re, im)
                        else:
                            old = acc[s, g]
                            acc[s, g] = (old[0] + re, old[1] + im)
            for r in range(2):
                whole = jnp.concatenate(
                    [acc[s, g][r] for s in range(syms) for g in range(groups)], axis=0
                )
                high = whole.astype(jnp.bfloat16)
                spot = pl.ds((r * tiles + t) * WIDE, WIDE)
                grid_high[k, :, spot] = high
                grid_rest[k, :, spot] = (whole - high.astype(jnp.float32)).astype(jnp.bfloat16)
        return carry

    lax.fori_loop(0, per_block, precode, 0)

    quarter = NFFT // 4
    height = syms * antennas

    def transform(n, carry):
        high = grid_high[...].reshape(per_block * height, 2 * tiles * WIDE)
        rest = grid_rest[...].reshape(per_block * height, 2 * tiles * WIDE)
        spec[...] = (
            jnp.dot(high, high_ref[n], preferred_element_type=jnp.float32)
            + jnp.dot(rest, high_ref[n], preferred_element_type=jnp.float32)
            + jnp.dot(high, rest_ref[n], preferred_element_type=jnp.float32)
        )
        for s in range(syms):
            for g in range(groups):
                part = [None] * 4
                for k in range(per_block):
                    rows = pl.ds(k * height + s * antennas + g * ROWS, ROWS)
                    re = spec[rows, pl.ds(0, WIDE)]
                    im = spec[rows, pl.ds(WIDE, WIDE)]
                    if k > 0:
                        cos = twist_ref[n, pl.ds(2 * k, 1), :]
                        sin = twist_ref[n, pl.ds(2 * k + 1, 1), :]
                        re, im = re * cos - im * sin, re * sin + im * cos
                    old = part[k % 4]
                    part[k % 4] = (re, im) if old is None else (old[0] + re, old[1] + im)
                (r0, i0), (r1, i1), (r2, i2), (r3, i3) = part
                even_re, even_im, odd_re, odd_im = r0 + r2, i0 + i2, r1 + r3, i1 + i3
                gap_re, gap_im, far_re, far_im = r0 - r2, i0 - i2, r1 - r3, i1 - i3
                outs = (
                    (even_re + odd_re, even_im + odd_im),
                    (gap_re - far_im, gap_im + far_re),
                    (even_re - odd_re, even_im - odd_im),
                    (gap_re + far_im, gap_im - far_re),
                )
                for q, pair in enumerate(outs):
                    spot = pl.ds(pl.multiple_of(q * quarter + n * WIDE, WIDE), WIDE)
                    for r in range(2):
                        out_ref[r, s, pl.ds(g * ROWS, ROWS), spot] = pair[r]
        return carry

    lax.fori_loop(0, quarter // WIDE, transform, 0)


def transform_tables(blocks, subcarriers):
    sub = subcarriers // blocks
    quarter = NFFT // 4
    p = np.arange(blocks)[:, None]
    n = np.arange(quarter)[None, :]
    angle = 2.0 * np.pi / NFFT * ((sub * p - subcarriers // 2) * n % NFFT)
    cos = np.cos(angle) / math.sqrt(NFFT)
    sin = np.sin(angle) / math.sqrt(NFFT)
    count = quarter // WIDE
    real = np.concatenate([cos, -sin], 0).reshape(2 * blocks, count, 1, WIDE)
    imag = np.concatenate([sin, cos], 0).reshape(2 * blocks, count, 1, WIDE)
    table = np.concatenate([real, imag], 2).transpose(1, 0, 2, 3)
    table = table.reshape(count, 2 * blocks, 2 * WIDE).astype(np.float32)
    high = table.astype(jnp.bfloat16)
    rest = (table - high.astype(np.float32)).astype(jnp.bfloat16)
    turns = 2.0 * np.pi / NFFT * (np.arange(sub)[:, None] * n)
    twist = np.stack([np.cos(turns), np.sin(turns)], 1).astype(np.float32)
    twist = twist.reshape(2 * sub, count, WIDE).transpose(1, 0, 2)
    return high, rest, np.ascontiguousarray(twist)


def reorder_table(sub):
    source = np.arange(sub * WIDE)
    table = np.zeros((sub * WIDE, sub * WIDE), np.float32)
    table[source, (source % sub) * WIDE + source // sub] = 1.0
    return table.astype(jnp.bfloat16)


def per_device(channel, symbols, layers, user_ids, user_power, neighbours, coupling):
    lanes = lax.axis_size("lane")
    cells = lax.axis_size("cell")
    _, antennas, _, order, blocks = channel.shape
    syms, subcarriers = symbols.shape[3:]
    sub = subcarriers // blocks
    chunk = blocks // lanes
    tiles = blocks // WIDE
    quarter = NFFT // 4
    f32 = jnp.float32
    high, rest, twist = transform_tables(blocks, subcarriers)
    chan = channel[0]

    amp, own = pl.pallas_call(
        functools.partial(power_kernel, chunk=chunk),
        out_shape=(
            jax.ShapeDtypeStruct((order, blocks), f32),
            jax.ShapeDtypeStruct((1, WIDE), f32),
        ),
        in_specs=[VMEM] * 3,
        out_specs=(VMEM, VMEM),
        name="power",
    )(layers, user_ids[0], user_power)
    transmit = lax.all_to_all(jnp.broadcast_to(own, (cells, WIDE)), "cell", 0, 0, tiled=True)

    parts = pl.pallas_call(
        functools.partial(gram_kernel, chunk=chunk),
        out_shape=jax.ShapeDtypeStruct((lanes, order * ROWS, WIDE), f32),
        in_specs=[VMEM] * 2,
        out_specs=VMEM,
        compiler_params=params(16),
        name="gram",
    )(chan, layers)
    parts = lax.all_to_all(parts, "lane", 0, 0, tiled=True)

    sym, turned = pl.pallas_call(
        arrange_kernel,
        out_shape=(
            jax.ShapeDtypeStruct((tiles, sub, order * 2 * syms, WIDE), f32),
            jax.ShapeDtypeStruct((tiles, 2, order, antennas, WIDE), f32),
        ),
        in_specs=[VMEM] * 3,
        out_specs=(VMEM, VMEM),
        scratch_shapes=[pltpu.VMEM((tiles, antennas * 2 * order, WIDE), f32)],
        compiler_params=params(24),
        cost_estimate=pl.CostEstimate(flops=10**9, bytes_accessed=8 * 10**6, transcendentals=0),
        name="arrange",
    )(symbols.reshape(order * 2 * syms, subcarriers), jnp.asarray(reorder_table(sub)), chan)

    packs = pl.pallas_call(
        solve_kernel,
        out_shape=jax.ShapeDtypeStruct((lanes, order * ROWS + ROWS, WIDE), f32),
        in_specs=[SMEM, SMEM, VMEM, VMEM],
        out_specs=VMEM,
        scratch_shapes=[pltpu.VMEM((order * order, WIDE), f32)] * 8,
        compiler_params=params(16),
        name="solve",
    )(neighbours, coupling, parts, transmit)
    packs = lax.all_to_all(packs, "lane", 0, 0, tiled=True)

    out = pl.pallas_call(
        functools.partial(transmit_kernel, chunk=chunk),
        out_shape=jax.ShapeDtypeStruct((2, syms, antennas, NFFT), f32),
        in_specs=[VMEM] * 7,
        out_specs=VMEM,
        scratch_shapes=[
            pltpu.VMEM((tiles, order * order, WIDE), f32),
            pltpu.VMEM((tiles, order, WIDE), f32),
            pltpu.VMEM((tiles, 2, order, antennas, WIDE), f32),
            pltpu.VMEM((sub, syms * antennas, 2 * tiles * WIDE), jnp.bfloat16),
            pltpu.VMEM((sub, syms * antennas, 2 * tiles * WIDE), jnp.bfloat16),
            pltpu.VMEM((sub * syms * antennas, 2 * WIDE), f32),
        ],
        compiler_params=params(32),
        name="transmit",
    )(packs, amp, turned, sym, jnp.asarray(high), jnp.asarray(rest), jnp.asarray(twist))
    return jnp.transpose(out, (2, 0, 1, 3))[None]


def solution(mesh):
    in_specs = (
        P("cell", "lane", None, None, None),
        P("cell", None, None, None, None),
        P("cell", None),
        P("cell", None, None),
        P("cell", None),
        P(),
        P(),
    )
    out_specs = P("cell", "lane", None, None, None)
    return jax.shard_map(
        per_device, mesh=mesh, in_specs=in_specs, out_specs=out_specs, check_vma=False
    )
```

```python
import functools
import math

import jax
import jax.numpy as jnp
import numpy as np
from jax import lax
from jax.experimental import pallas as pl
from jax.experimental.pallas import tpu as pltpu
from jax.sharding import PartitionSpec as P

NFFT = 4096
NS_STEPS = 6
NORM_EPS = 1e-06
NOISE_FLOOR = 0.05
WIDE = 128
HALF = WIDE // 2
ROWS = 8

VMEM = pl.BlockSpec(memory_space=pltpu.VMEM)
HBM = pl.BlockSpec(memory_space=pltpu.HBM)


def lane_iota():
    return lax.broadcasted_iota(jnp.int32, (ROWS, WIDE), 1)


def row_iota():
    return lax.broadcasted_iota(jnp.int32, (ROWS, WIDE), 0)


def turn(value, shift):
    shift = shift % WIDE
    return value if shift == 0 else pltpu.roll(value, shift, 1)


def params(mib):
    return pltpu.CompilerParams(vmem_limit_bytes=mib * 1024 * 1024)


def gram_kernel(*refs, lanes, chunk):
    ins, outs = refs[:6], refs[10 : 10 + lanes]
    amp_all, own, mix, turned = refs[6:10]
    channel, layers, ids_all, power, neigh, coup, pieces, stage, sems = refs[10 + lanes :]
    antennas, _, order, blocks = channel.shape
    users = power.shape[1]
    tiles = blocks // WIDE
    small = [
        pltpu.make_async_copy(src, dst, sems.at[i])
        for i, (src, dst) in enumerate(
            (
                (ins[1], layers),
                (ins[2].at[0], ids_all),
                (ins[3], power),
                (ins[4], neigh),
                (ins[5], coup),
            )
        )
    ]
    large = [
        pltpu.make_async_copy(
            ins[0].at[0, :, :, :, pl.ds(t * WIDE, WIDE)],
            channel.at[:, :, :, pl.ds(t * WIDE, WIDE)],
            sems.at[5 + t],
        )
        for t in range(tiles)
    ]
    for copy in small + large:
        copy.start()
    for copy in small:
        copy.wait()

    rooted = jnp.sqrt(power[...])
    sums = []
    for t in range(tiles):
        spot = pl.ds(t * WIDE, WIDE)
        granted = layers[:, spot]
        total = jnp.zeros((ROWS, WIDE), jnp.float32)
        for h in range(order // ROWS):
            ids = ids_all[pl.ds(h * ROWS, ROWS), spot]
            picked = jnp.zeros((ROWS, WIDE), jnp.float32)
            for u in range(users // WIDE):
                table = jnp.broadcast_to(rooted[:, u * WIDE : (u + 1) * WIDE], (ROWS, WIDE))
                found = jnp.take_along_axis(table, ids % WIDE, axis=1, mode="promise_in_bounds")
                picked = jnp.where(ids // WIDE == u, found, picked)
            amp = jnp.where(row_iota() + h * ROWS < granted, picked, 0.0)
            amp_all[t, pl.ds(h * ROWS, ROWS), :] = amp
            total = total + amp * amp
        sums.append(jnp.sum(total, axis=0, keepdims=True) / order)
    lane = lax.axis_index("lane")
    start = lane * chunk
    mine = jnp.broadcast_to(sums[0], (ROWS, WIDE))
    for t in range(1, tiles):
        mine = jnp.where(start // WIDE == t, jnp.broadcast_to(sums[t], (ROWS, WIDE)), mine)
    mine = pltpu.roll(mine, lax.rem(WIDE - lax.rem(start, WIDE), WIDE), 1)
    both = jnp.where(lane_iota() < HALF, mine, pltpu.roll(mine, HALF, 1))
    own[...] = jnp.broadcast_to(both[0:1][None], own.shape)
    cell = lax.axis_index("cell")
    mix[...] = jnp.zeros(mix.shape, jnp.float32)
    for k in range(neigh.shape[1]):
        spot = neigh[cell, k]
        mix[spot] = mix[spot] + coup[cell, k]
    low = lane_iota() < HALF
    rows = row_iota()
    for t in range(tiles):
        spot = pl.ds(t * WIDE, WIDE)
        granted = layers[:, spot]
        inside = [rows + h * ROWS < granted for h in range(2)]
        large[t].wait()
        for base in range(0, ROWS, 2):
            tops = (base, base + 1)
            acc = {}

            def add(key, value):
                acc[key] = value if key not in acc else acc[key] + value

            for a in range(antennas):
                re = [channel[a, 0, pl.ds(h * ROWS, ROWS), spot] for h in range(2)]
                im = [channel[a, 1, pl.ds(h * ROWS, ROWS), spot] for h in range(2)]
                for l in tops:
                    lre = channel[a, 0, pl.ds(l, 1), spot]
                    lim = channel[a, 1, pl.ds(l, 1), spot]
                    add((l, "re", 0), lre * re[0] + lim * im[0])
                    add((l, "re", 1), lre * re[1] + lim * im[1])
                    add((l, "im", 0), lim * re[0] - lre * im[0])
                    g = l + ROWS
                    gre = channel[a, 0, pl.ds(g, 1), spot]
                    gim = channel[a, 1, pl.ds(g, 1), spot]
                    add((g, "re", 1), gre * re[1] + gim * im[1])
                    add((g, "im", 0), gim * re[0] - gre * im[0])
                    add((g, "im", 1), gim * re[1] - gre * im[1])
            for l in tops:
                g = l + ROWS
                here = granted > l
                there = granted > g
                upper = [
                    jnp.where(rows >= l, acc[l, "re", 0], acc[l, "im", 0]),
                    acc[l, "re", 1],
                ]
                lower = [
                    acc[g, "im", 0],
                    jnp.where(rows >= l, acc[g, "re", 1], acc[g, "im", 1]),
                ]
                for h in range(2):
                    top = jnp.where(jnp.logical_and(inside[h], here), upper[h], 0.0)
                    bottom = jnp.where(jnp.logical_and(inside[h], there), lower[h], 0.0)
                    for z in range(t * WIDE // chunk, (t + 1) * WIDE // chunk):
                        off = z * chunk - t * WIDE
                        where = pl.ds(l * 2 * ROWS + h * ROWS, ROWS)
                        pieces[lane ^ z, where, :] = jnp.where(
                            low, turn(top, -off), turn(bottom, HALF - off)
                        )
    for s in range(lanes):
        outs[s][...] = pieces[s]
    for t in range(tiles):
        for a in range(antennas):
            for r in range(2):
                for h in range(order // ROWS):
                    stage[t, pl.ds((a * 2 + r) * order + h * ROWS, ROWS), :] = channel[
                        a, r, pl.ds(h * ROWS, ROWS), pl.ds(t * WIDE, WIDE)
                    ]
        for r in range(2):
            for m in range(order):
                for h in range(antennas // ROWS):
                    first = h * ROWS * 2 * order + r * order + m
                    turned[t, r, m, pl.ds(h * ROWS, ROWS), :] = stage[
                        t, pl.ds(first, ROWS, stride=2 * order), :
                    ]


def solve_kernel(*refs, lanes):
    trans, mix = refs[:2]
    parts, out = refs[2 : 2 + lanes], refs[3 + lanes]
    pack, gram, e_a, e_b, s_a, s_b, d_re, d_im = refs[4 + lanes :]
    order = 2 * ROWS
    low = lane_iota() < HALF
    rows = row_iota()
    sign = jnp.where(low, -1.0, 1.0)

    def at(l, h):
        return pl.ds(l * order + h * ROWS, ROWS)

    def column(l, h):
        return pl.ds(h * ROWS * order + l, ROWS, stride=order)

    def row(ref, l, k):
        return ref[pl.ds(l * order + k, 1), :]

    for l in range(ROWS):
        for h in range(2):
            value = parts[0][at(l, h), :]
            for s in range(1, lanes):
                value = value + parts[s][at(l, h), :]
            other = pltpu.roll(value, HALF, 1)
            pack[at(l, h), :] = jnp.where(low, value, other)
            pack[at(l + ROWS, h), :] = jnp.where(low, other, value)

    sigma = jnp.full((1, WIDE), NOISE_FLOOR, jnp.float32)
    for c in range(trans.shape[0]):
        sigma = sigma + mix[c] * trans[c]

    trace = order * sigma
    for l in range(order):
        trace = trace + row(pack, l, l)
    inverse = 1.0 / trace
    kept = 1.0 - sigma * inverse

    for l in range(order):
        for h in range(2):
            here = pack[at(l, h), :]
            across = pack[column(l, h), :]
            above = jnp.where(low, here, -across)
            below = jnp.where(low, across, here)
            if h * ROWS > l:
                value = above
            elif h * ROWS + ROWS - 1 < l:
                value = below
            else:
                value = jnp.where(rows + h * ROWS >= l, above, below)
                value = jnp.where(jnp.logical_and(rows + h * ROWS == l, ~low), 0.0, value)
            gram[at(l, h), :] = value
            error = -value * inverse
            total = error
            if h * ROWS <= l < h * ROWS + ROWS:
                spot = jnp.logical_and(rows + h * ROWS == l, low)
                error = error + jnp.where(spot, kept, 0.0)
                total = error + jnp.where(spot, 1.0, 0.0)
            e_a[at(l, h), :] = error
            s_a[at(l, h), :] = total

    def spread(ref):
        for l in range(order):
            for h in range(2):
                value = ref[at(l, h), :]
                other = pltpu.roll(value, HALF, 1)
                d_re[at(l, h), :] = jnp.where(low, value, other)
                d_im[at(l, h), :] = jnp.where(low, other, value)

    def products(jobs):
        for base in range(0, order, 2):
            halves = (0, 1) if base < ROWS else (1,)
            plain, crossed = {}, {}
            for l in (base, base + 1):
                for j, (_, _, start) in enumerate(jobs):
                    for h in halves:
                        if start is not None:
                            plain[l, j, h] = start[at(l, h), :]
            for k in range(order):
                right = {
                    (j, h): ref[at(k, h), :] for j, (ref, _, _) in enumerate(jobs) for h in halves
                }
                for l in (base, base + 1):
                    left_re = row(d_re, l, k)
                    left_im = row(d_im, l, k) if k != l else None
                    for (j, h), value in right.items():
                        key = (l, j, h)
                        term = left_re * value
                        plain[key] = plain[key] + term if key in plain else term
                        if left_im is not None:
                            term = left_im * value
                            crossed[key] = crossed[key] + term if key in crossed else term
            for (l, j, h), value in plain.items():
                cross = pltpu.roll(crossed[l, j, h], HALF, 1)
                jobs[j][1][at(l, h), :] = value + sign * cross
        for _, ref, _ in jobs:
            for l in range(ROWS, order):
                ref[at(l, 0), :] = -sign * ref[column(l, 0), :]

    spread(e_a)
    products([(e_a, e_b, None)])

    def two_steps(_, carry):
        spread(e_b)
        products([(e_b, e_a, None), (s_a, s_b, s_a)])
        spread(e_a)
        products([(e_a, e_b, None), (s_b, s_a, s_b)])
        return carry

    lax.fori_loop(0, (NS_STEPS - 2) // 2, two_steps, 0)
    spread(e_b)
    products([(s_a, s_b, s_a)])

    for l in range(order):
        for h in range(2):
            s_a[at(l, h), :] = s_b[at(l, h), :] * inverse
    spread(s_a)
    products([(gram, e_a, None)])

    energy = []
    for h in range(2):
        value = s_a[at(0, h), :] * e_a[at(0, h), :]
        for m in range(1, order):
            value = value + s_a[at(m, h), :] * e_a[at(m, h), :]
        energy.append(value + pltpu.roll(value, HALF, 1))
    last = jnp.where(low, energy[0], energy[1])
    for l in range(ROWS):
        for h in range(2):
            first = s_a[at(l, h), :]
            second = s_a[at(l + ROWS, h), :]
            where = rows + h * ROWS
            value = jnp.where(
                low,
                jnp.where(where >= l, first, pltpu.roll(first, HALF, 1)),
                jnp.where(where >= l + ROWS, pltpu.roll(second, HALF, 1), second),
            )
            out[at(l, h), :] = value
    out[pl.ds(order * ROWS, ROWS), :] = last


def arrange_kernel(far_ref, sym_ref, mark_ref, symbols_ref, sem, flat, stacked, moved):
    copy = pltpu.make_async_copy(far_ref, symbols_ref, sem)
    copy.start()
    copy.wait()
    _, layers, parts, syms, subcarriers = symbols_ref.shape
    tiles, sub, height, _ = sym_ref.shape
    few = 32
    span = sub * few
    quads = WIDE // few
    lanes = lane_iota()
    for l in range(layers):
        for r in range(parts):
            flat[pl.ds((l * parts + r) * syms, syms), :] = symbols_ref[0, l, r].astype(jnp.float32)
    for i in range(tiles * quads):
        stacked[pl.ds(i * height, height), :] = flat[:, pl.ds(i * span, span)].astype(jnp.bfloat16)
    source = lax.broadcasted_iota(jnp.int32, (span, span), 0)
    target = lax.broadcasted_iota(jnp.int32, (span, span), 1)
    table = jnp.where(source == target % few * sub + target // few, 1.0, 0.0).astype(jnp.bfloat16)
    moved[...] = jnp.dot(stacked[...], table, preferred_element_type=jnp.float32)
    for t in range(tiles):
        for k in range(sub):
            for g in range(height // ROWS):
                value = None
                for b in range(quads):
                    rows = pl.ds((t * quads + b) * height + g * ROWS, ROWS)
                    piece = moved[rows, pl.ds(k // quads * WIDE, WIDE)]
                    piece = turn(piece, (b - k % quads) * few)
                    value = piece if b == 0 else jnp.where(lanes >= b * few, piece, value)
                sym_ref[t, k, pl.ds(g * ROWS, ROWS), :] = value
    mark_ref[...] = jnp.zeros(mark_ref.shape, jnp.float32)


def transmit_kernel(*refs, which, last, chunk):
    per_tile = WIDE // chunk
    ins, rest = refs[:per_tile], refs[per_tile:]
    amp, chan, sym, table_ref, twist = rest[:5]
    before = rest[5] if which else None
    out_ref = out = rest[5 + which]
    packs, pack, scale, weight, mixed, grid, table, spec_a, spec_b, sems = rest[
        6 + which : 16 + which
    ]
    if last:
        out, out_sems = rest[16 + which :]
    tiles, _, order, antennas, _ = chan.shape
    per_block, syms = sym.shape[1], sym.shape[2] // (2 * order)
    groups = antennas // ROWS
    lanes = lane_iota()
    lane = lax.axis_index("lane")
    tile = (lane // per_tile) ^ which
    halves = [
        pltpu.make_async_copy(
            table_ref.at[tile], table.at[:, pl.ds(h * 2 * WIDE, 2 * WIDE), :], sems.at[h]
        )
        for h in range(2)
    ]
    for copy in halves:
        copy.start()

    for s, ref in enumerate(ins):
        packs[lane % per_tile ^ s] = ref[...]
    for i in range(2 * ROWS + 1):
        rows = pl.ds(i * ROWS, ROWS)
        value = packs[0, rows, :]
        first, second = value, pltpu.roll(value, HALF, 1)
        for z in range(1, per_tile):
            off = z * chunk
            value = packs[z, rows, :]
            first = jnp.where(lanes >= off, turn(value, off), first)
            second = jnp.where(lanes >= off, turn(value, off - HALF), second)
        if i < 2 * ROWS:
            pack[rows, :] = first
            pack[pl.ds((i + 2 * ROWS) * ROWS, ROWS), :] = second
        else:
            for h, energy in enumerate((first, second)):
                spot = pl.ds(h * ROWS, ROWS)
                scale[spot, :] = amp[tile, spot, :] / jnp.sqrt(energy + NORM_EPS)

    def row(l, m):
        return pack[pl.ds(l * order + m, 1), :]

    for base in range(0, order, 4):
        acc = {}

        def add(key, value):
            acc[key] = value if key not in acc else acc[key] + value

        for m in range(order):
            here = [
                [chan[tile, r, m, pl.ds(g * ROWS, ROWS), :] for g in range(groups)]
                for r in range(2)
            ]
            for l in range(base, base + 4):
                inv_re = row(min(l, m), max(l, m))
                inv_im = row(max(l, m), min(l, m)) if l != m else None
                if l > m:
                    inv_im = -inv_im
                for g in range(groups):
                    re, im = here[0][g], here[1][g]
                    if inv_im is None:
                        add((l, 0, g), re * inv_re)
                        add((l, 1, g), -(im * inv_re))
                    else:
                        add((l, 0, g), re * inv_re + im * inv_im)
                        add((l, 1, g), re * inv_im - im * inv_re)
        for (l, r, g), value in acc.items():
            value = value * scale[pl.ds(l, 1), :]
            weight[r, l, pl.ds(g * ROWS, ROWS), :] = value.astype(jnp.bfloat16).astype(jnp.float32)

    def precode(k, carry):
        acc = {}
        for l in range(order):
            w_re = [weight[0, l, pl.ds(g * ROWS, ROWS), :] for g in range(groups)]
            w_im = [weight[1, l, pl.ds(g * ROWS, ROWS), :] for g in range(groups)]
            for s in range(syms):
                s_re = sym[tile, k, pl.ds((l * 2 + 0) * syms + s, 1), :]
                s_im = sym[tile, k, pl.ds((l * 2 + 1) * syms + s, 1), :]
                for g in range(groups):
                    re = w_re[g] * s_re - w_im[g] * s_im
                    im = w_re[g] * s_im + w_im[g] * s_re
                    if l == 0:
                        acc[s, g] = (re, im)
                    else:
                        old = acc[s, g]
                        acc[s, g] = (old[0] + re, old[1] + im)
        for r in range(2):
            for s in range(syms):
                for g in range(groups):
                    spot = pl.ds(g * ROWS * syms + s, ROWS, stride=syms)
                    mixed[r, spot, :] = acc[s, g][r]
        for r in range(2):
            whole = mixed[r]
            high = whole.astype(jnp.bfloat16)
            grid[k, :, pl.ds(r * WIDE, WIDE)] = high
            grid[k, :, pl.ds((2 + r) * WIDE, WIDE)] = (whole - high.astype(jnp.float32)).astype(
                jnp.bfloat16
            )
        return carry

    lax.fori_loop(0, per_block, precode, 0)

    height = syms * antennas
    count = NFFT // WIDE // 4
    for copy in halves:
        copy.wait()
    left = grid[...].reshape(per_block * height, 4 * WIDE)
    specs = (spec_a, spec_b)

    def product(n):
        specs[n % 2][...] = jnp.dot(left, table[n], preferred_element_type=jnp.float32)

    def combine(n):
        spec = specs[n % 2]
        for g in range(height // ROWS):
            part = [None] * 4
            for k in range(per_block):
                rows = pl.ds(k * height + g * ROWS, ROWS)
                re = spec[rows, pl.ds(0, WIDE)]
                im = spec[rows, pl.ds(WIDE, WIDE)]
                if k > 0:
                    cos = twist[n, pl.ds(2 * k, 1), :]
                    sin = twist[n, pl.ds(2 * k + 1, 1), :]
                    re, im = re * cos - im * sin, re * sin + im * cos
                old = part[k % 4]
                part[k % 4] = (re, im) if old is None else (old[0] + re, old[1] + im)
            (r0, i0), (r1, i1), (r2, i2), (r3, i3) = part
            even_re, even_im, odd_re, odd_im = r0 + r2, i0 + i2, r1 + r3, i1 + i3
            gap_re, gap_im, far_re, far_im = r0 - r2, i0 - i2, r1 - r3, i1 - i3
            outs = (
                (even_re + odd_re, even_im + odd_im),
                (gap_re - far_im, gap_im + far_re),
                (even_re - odd_re, even_im - odd_im),
                (gap_re + far_im, gap_im - far_re),
            )
            spot = pl.ds(g * ROWS, ROWS)
            for q, pair in enumerate(outs):
                for r in range(2):
                    value = pair[r]
                    if which:
                        value = value + before[n, q, r, spot, :]
                    out[n, q, r, spot, :] = value

    done = []
    product(0)
    for n in range(count):
        if n + 1 < count:
            product(n + 1)
        combine(n)
        if not last:
            continue
        for q in range(4):
            for r in range(2):
                copy = pltpu.make_async_copy(
                    out.at[n, q, r].reshape(antennas, syms, WIDE),
                    out_ref.at[:, r, q * count + n],
                    out_sems.at[n, q, r],
                )
                copy.start()
                done.append(copy)
    for copy in done:
        copy.wait()


def transform_tables(blocks, subcarriers):
    sub = subcarriers // blocks
    tiles = blocks // WIDE
    quarter = NFFT // 4
    p = np.arange(blocks)[:, None]
    n = np.arange(quarter)[None, :]
    angle = 2.0 * np.pi / NFFT * ((sub * p - subcarriers // 2) * n % NFFT)
    cos = np.cos(angle) / math.sqrt(NFFT)
    sin = np.sin(angle) / math.sqrt(NFFT)
    count = quarter // WIDE
    table = np.stack([np.stack([cos, sin]), np.stack([-sin, cos])])
    table = table.reshape(2, 2, tiles, WIDE, count, WIDE).transpose(2, 4, 0, 3, 1, 5)
    table = table.reshape(tiles, count, 2 * WIDE, 2 * WIDE).astype(jnp.bfloat16)
    turns = 2.0 * np.pi / NFFT * (np.arange(sub)[:, None] * n)
    twist = np.stack([np.cos(turns), np.sin(turns)], 1).astype(np.float32)
    twist = twist.reshape(2 * sub, count, WIDE).transpose(1, 0, 2)
    return table, np.ascontiguousarray(twist)


def far(value):
    return pltpu.with_memory_space_constraint(value, pltpu.HBM)


def near(value):
    return pltpu.with_memory_space_constraint(value, pltpu.VMEM)


def swap(pieces):
    lanes = lax.axis_size("lane")
    return [pieces[0]] + [
        lax.ppermute(pieces[s], "lane", [(j, j ^ s) for j in range(lanes)]) for s in range(1, lanes)
    ]


def per_device(channel, symbols, layers, user_ids, user_power, neighbours, coupling):
    lanes = lax.axis_size("lane")
    cells = lax.axis_size("cell")
    _, antennas, _, order, blocks = channel.shape
    syms, subcarriers = symbols.shape[3:]
    sub = subcarriers // blocks
    chunk = blocks // lanes
    tiles = blocks // WIDE
    f32, bf16 = jnp.float32, jnp.bfloat16
    shape = jax.ShapeDtypeStruct
    table, twist = transform_tables(blocks, subcarriers)
    table, twist = jnp.asarray(table), jnp.asarray(twist)
    dma = pltpu.SemaphoreType.DMA

    amp, own, mix, turned, *pieces = pl.pallas_call(
        functools.partial(gram_kernel, lanes=lanes, chunk=chunk),
        out_shape=[pltpu.VMEM((tiles, order, WIDE), f32)]
        + [pltpu.VMEM((cells, 1, WIDE), f32)] * 2
        + [pltpu.VMEM((tiles, 2, order, antennas, WIDE), f32)]
        + [pltpu.VMEM((order * ROWS, WIDE), f32)] * lanes,
        in_specs=[HBM] * 6,
        out_specs=[VMEM] * (4 + lanes),
        scratch_shapes=[
            pltpu.VMEM((antennas, 2, order, blocks), f32),
            pltpu.VMEM((1, blocks), jnp.int32),
            pltpu.VMEM((order, blocks), jnp.int32),
            pltpu.VMEM(user_power.shape, f32),
            pltpu.SMEM(neighbours.shape, jnp.int32),
            pltpu.SMEM(coupling.shape, f32),
            pltpu.VMEM((lanes, order * ROWS, WIDE), f32),
            pltpu.VMEM((tiles, antennas * 2 * order, WIDE), f32),
            dma((5 + tiles,)),
        ],
        compiler_params=params(16),
        name="gram",
    )(*map(far, (channel, layers, user_ids, user_power, neighbours, coupling)))
    parts = swap(pieces)
    transmit = lax.all_to_all(own, "cell", 0, 0, tiled=True)

    sym, mark = pl.pallas_call(
        arrange_kernel,
        out_shape=(
            pltpu.VMEM((tiles, sub, order * 2 * syms, WIDE), f32),
            pltpu.VMEM((ROWS, WIDE), f32),
        ),
        in_specs=[HBM],
        out_specs=(VMEM, VMEM),
        scratch_shapes=[
            pltpu.VMEM(symbols.shape, bf16),
            pltpu.SemaphoreType.DMA,
            pltpu.VMEM((order * 2 * syms, subcarriers), f32),
            pltpu.VMEM((subcarriers // (sub * 32) * order * 2 * syms, sub * 32), bf16),
            pltpu.VMEM((subcarriers // (sub * 32) * order * 2 * syms, sub * 32), f32),
        ],
        compiler_params=params(16),
        cost_estimate=pl.CostEstimate(flops=10**9, bytes_accessed=8 * 10**6, transcendentals=0),
        name="arrange",
    )(far(symbols))

    packed = pl.pallas_call(
        functools.partial(solve_kernel, lanes=lanes),
        out_shape=pltpu.VMEM((order * ROWS + ROWS, WIDE), f32),
        in_specs=[VMEM] * (3 + lanes),
        out_specs=VMEM,
        scratch_shapes=[pltpu.VMEM((order * order, WIDE), f32)] * 8,
        compiler_params=params(16),
        name="solve",
    )(near(transmit), near(mix), *map(near, parts), near(mark))
    packs = swap([packed] * lanes)

    per_tile = WIDE // chunk
    height = syms * antennas
    count = NFFT // WIDE // 4
    out = ()
    for which in range(tiles):
        last = which == tiles - 1
        result = (count, 4, 2, height, WIDE)
        final = (antennas, 2, NFFT // WIDE, syms, WIDE)
        out = pl.pallas_call(
            functools.partial(transmit_kernel, which=which, last=last, chunk=chunk),
            out_shape=[shape(final, f32) if last else pltpu.VMEM(result, f32)],
            in_specs=[VMEM] * (per_tile + 3) + [HBM, VMEM] + [VMEM] * which,
            out_specs=[HBM if last else VMEM],
            scratch_shapes=[
                pltpu.VMEM((per_tile, order * ROWS + ROWS, WIDE), f32),
                pltpu.VMEM((order * order, WIDE), f32),
                pltpu.VMEM((order, WIDE), f32),
                pltpu.VMEM((2, order, antennas, WIDE), f32),
                pltpu.VMEM((2, height, WIDE), f32),
                pltpu.VMEM((sub, height, 4 * WIDE), bf16),
                pltpu.VMEM((count, 4 * WIDE, 2 * WIDE), bf16),
                pltpu.VMEM((sub * height, 2 * WIDE), f32),
                pltpu.VMEM((sub * height, 2 * WIDE), f32),
                dma((2,)),
            ]
            + [pltpu.VMEM(result, f32), dma((count, 4, 2))] * last,
            compiler_params=params(16),
            cost_estimate=pl.CostEstimate(
                flops=10**9, bytes_accessed=4 * 10**6, transcendentals=0
            ),
            name="transmit",
        )(
            *map(near, packs[which * per_tile : (which + 1) * per_tile]),
            near(amp),
            near(turned),
            near(sym),
            far(table),
            near(twist),
            *map(near, out),
        )
    out = out[0].transpose(0, 1, 3, 2, 4)
    return out.reshape(1, antennas, 2, syms, NFFT)


def solution(mesh):
    in_specs = (
        P("cell", "lane", None, None, None),
        P("cell", None, None, None, None),
        P("cell", None),
        P("cell", None, None),
        P("cell", None),
        P(),
        P(),
    )
    out_specs = P("cell", "lane", None, None, None)
    return jax.shard_map(
        per_device, mesh=mesh, in_specs=in_specs, out_specs=out_specs, check_vma=False
    )
```

```python
import functools
import math

import jax
import jax.numpy as jnp
import numpy as np
from jax import lax
from jax.experimental import pallas as pl
from jax.experimental.pallas import tpu as pltpu
from jax.sharding import PartitionSpec as P

NFFT = 4096
NS_STEPS = 6
NORM_EPS = 1e-06
NOISE_FLOOR = 0.05
WIDE = 128
HALF = WIDE // 2
ROWS = 8
FULL = 32760.0
OFFSET = 32768
ROOT_UNIT = 2.0**24
LOG_UNIT = 2.0**23

VMEM = pl.BlockSpec(memory_space=pltpu.VMEM)
HBM = pl.BlockSpec(memory_space=pltpu.HBM)


def lane_iota():
    return lax.broadcasted_iota(jnp.int32, (ROWS, WIDE), 1)


def row_iota():
    return lax.broadcasted_iota(jnp.int32, (ROWS, WIDE), 0)


def turn(value, shift):
    shift = shift % WIDE
    return value if shift == 0 else pltpu.roll(value, shift, 1)


def mirrored(index, lanes):
    bits = lanes.bit_length() - 1
    total = 0
    for b in range(bits):
        total = total + ((index >> b) % 2) * (1 << (bits - 1 - b))
    return total


def split(value, unit):
    whole = jnp.round(value * unit).astype(jnp.int32)
    high = whole >> 16
    return jnp.concatenate([high, whole - (high << 16) - OFFSET], 0).astype(jnp.int16)


def joined(halves, unit):
    high = halves[:ROWS].astype(jnp.float32) * (65536.0 / unit)
    return high + (halves[ROWS:] + OFFSET).astype(jnp.float32) * (1.0 / unit)


def unpacked(piece):
    order = 2 * ROWS
    low, rows = lane_iota() < HALF, row_iota()
    root = joined(piece[pl.ds(order * ROWS, order), :].astype(jnp.int32), ROOT_UNIT)
    other = pltpu.roll(root, HALF, 1)
    both = (jnp.where(low, root, other), jnp.where(low, other, root))
    values = {}
    for l in range(ROWS):
        held = piece[pl.ds(l * order, order), :].astype(jnp.int32).astype(jnp.float32)
        for h in range(2):
            whole = jnp.logical_and(rows == l, low if h == 0 else ~low)
            part = jnp.where(whole, 1.0, held[h * ROWS : (h + 1) * ROWS] * (1.0 / FULL))
            values[l, h] = root[l : l + 1] * both[h] * part
    return values


def params(mib):
    return pltpu.CompilerParams(vmem_limit_bytes=mib * 1024 * 1024)


def gram_kernel(*refs, lanes, chunk):
    ins, outs = refs[:6], refs[10 : 10 + lanes]
    amp_all, own, mix, turned = refs[6:10]
    channel, layers, ids_all, power, neigh, coup, pieces, inverses, stage, sems = refs[10 + lanes :]
    antennas, _, order, blocks = channel.shape
    users = power.shape[1]
    tiles = blocks // WIDE
    small = [
        pltpu.make_async_copy(src, dst, sems.at[i])
        for i, (src, dst) in enumerate(
            (
                (ins[1], layers),
                (ins[2].at[0], ids_all),
                (ins[3], power),
                (ins[4], neigh),
                (ins[5], coup),
            )
        )
    ]
    large = [
        pltpu.make_async_copy(
            ins[0].at[0, :, :, :, pl.ds(t * WIDE, WIDE)],
            channel.at[:, :, :, pl.ds(t * WIDE, WIDE)],
            sems.at[5 + t],
        )
        for t in range(tiles)
    ]
    for copy in small + large:
        copy.start()
    for copy in small:
        copy.wait()

    rooted = jnp.sqrt(power[...])
    sums = []
    for t in range(tiles):
        spot = pl.ds(t * WIDE, WIDE)
        granted = layers[:, spot]
        total = jnp.zeros((ROWS, WIDE), jnp.float32)
        for h in range(order // ROWS):
            ids = ids_all[pl.ds(h * ROWS, ROWS), spot]
            picked = jnp.zeros((ROWS, WIDE), jnp.float32)
            for u in range(users // WIDE):
                table = jnp.broadcast_to(rooted[:, u * WIDE : (u + 1) * WIDE], (ROWS, WIDE))
                found = jnp.take_along_axis(table, ids % WIDE, axis=1, mode="promise_in_bounds")
                picked = jnp.where(ids // WIDE == u, found, picked)
            amp = jnp.where(row_iota() + h * ROWS < granted, picked, 0.0)
            amp_all[t, pl.ds(h * ROWS, ROWS), :] = amp
            total = total + amp * amp
        sums.append(jnp.sum(total, axis=0, keepdims=True) / order)
    lane = lax.axis_index("lane")
    start = mirrored(lane, lanes) * chunk
    mine = jnp.broadcast_to(sums[0], (ROWS, WIDE))
    for t in range(1, tiles):
        mine = jnp.where(start // WIDE == t, jnp.broadcast_to(sums[t], (ROWS, WIDE)), mine)
    mine = pltpu.roll(mine, lax.rem(WIDE - lax.rem(start, WIDE), WIDE), 1)
    both = jnp.where(lane_iota() < HALF, mine, pltpu.roll(mine, HALF, 1))
    own[...] = jnp.broadcast_to(both[0:1][None], own.shape)
    cell = lax.axis_index("cell")
    mix[...] = jnp.zeros(mix.shape, jnp.float32)
    for k in range(neigh.shape[1]):
        spot = neigh[cell, k]
        mix[spot] = mix[spot] + coup[cell, k]
    low = lane_iota() < HALF
    rows = row_iota()
    for t in range(tiles):
        spot = pl.ds(t * WIDE, WIDE)
        granted = layers[:, spot]
        inside = [rows + h * ROWS < granted for h in range(2)]
        large[t].wait()
        inverse, root = [], []
        for h in range(2):
            part = pl.ds(h * ROWS, ROWS)
            total = jnp.zeros((ROWS, WIDE), jnp.float32)
            for a in range(antennas):
                re, im = channel[a, 0, part, spot], channel[a, 1, part, spot]
                total = total + (re * re + im * im)
            total = jnp.where(inside[h], total, 0.0)
            inverse.append(jnp.where(total > 0.0, lax.rsqrt(total), 0.0))
            root.append(total * inverse[h])
            inverses[part, :] = inverse[h] * FULL
        chunks = range(t * WIDE // chunk, (t + 1) * WIDE // chunk)

        def packed(top, bottom, z):
            off = z * chunk - t * WIDE
            return jnp.where(low, turn(top, -off), turn(bottom, HALF - off))

        for z in chunks:
            pieces[lane ^ mirrored(z, lanes), pl.ds(order * ROWS, order), :] = split(
                packed(root[0], root[1], z), ROOT_UNIT
            )
        for base in range(0, ROWS, 2):
            tops = (base, base + 1)
            acc = {}

            def add(key, value):
                acc[key] = value if key not in acc else acc[key] + value

            for a in range(antennas):
                re = [channel[a, 0, pl.ds(h * ROWS, ROWS), spot] for h in range(2)]
                im = [channel[a, 1, pl.ds(h * ROWS, ROWS), spot] for h in range(2)]
                for l in tops:
                    lre = channel[a, 0, pl.ds(l, 1), spot]
                    lim = channel[a, 1, pl.ds(l, 1), spot]
                    add((l, "re", 0), lre * re[0] + lim * im[0])
                    add((l, "re", 1), lre * re[1] + lim * im[1])
                    add((l, "im", 0), lim * re[0] - lre * im[0])
                    g = l + ROWS
                    gre = channel[a, 0, pl.ds(g, 1), spot]
                    gim = channel[a, 1, pl.ds(g, 1), spot]
                    add((g, "re", 1), gre * re[1] + gim * im[1])
                    add((g, "im", 0), gim * re[0] - gre * im[0])
                    add((g, "im", 1), gim * re[1] - gre * im[1])
            for l in tops:
                g = l + ROWS
                here = granted > l
                there = granted > g
                upper = [
                    jnp.where(rows >= l, acc[l, "re", 0], acc[l, "im", 0]),
                    acc[l, "re", 1],
                ]
                lower = [
                    acc[g, "im", 0],
                    jnp.where(rows >= l, acc[g, "re", 1], acc[g, "im", 1]),
                ]
                tops_out, bottoms_out = [], []
                for h in range(2):
                    top = jnp.where(jnp.logical_and(inside[h], here), upper[h], 0.0)
                    bottom = jnp.where(jnp.logical_and(inside[h], there), lower[h], 0.0)
                    tops_out.append(top * inverses[pl.ds(l, 1), :] * inverse[h])
                    bottoms_out.append(bottom * inverses[pl.ds(g, 1), :] * inverse[h])
                for z in chunks:
                    value = jnp.concatenate(
                        [packed(tops_out[h], bottoms_out[h], z) for h in range(2)], 0
                    )
                    pieces[lane ^ mirrored(z, lanes), pl.ds(l * order, order), :] = (
                        jnp.round(value).astype(jnp.int32).astype(jnp.int16)
                    )
    for s in range(lanes):
        outs[s][...] = pieces[s]
    for t in range(tiles):
        for a in range(antennas):
            for r in range(2):
                for h in range(order // ROWS):
                    stage[t, pl.ds((a * 2 + r) * order + h * ROWS, ROWS), :] = channel[
                        a, r, pl.ds(h * ROWS, ROWS), pl.ds(t * WIDE, WIDE)
                    ]
        for r in range(2):
            for m in range(order):
                for h in range(antennas // ROWS):
                    first = h * ROWS * 2 * order + r * order + m
                    turned[t, r, m, pl.ds(h * ROWS, ROWS), :] = stage[
                        t, pl.ds(first, ROWS, stride=2 * order), :
                    ]


def solve_kernel(*refs, count):
    trans, mix = refs[:2]
    parts, out = refs[2 : 2 + count], refs[2 + count]
    pack, gram, e_a, e_b, s_a, s_b, d_re, d_im = refs[3 + count :]
    order = 2 * ROWS
    low = lane_iota() < HALF
    rows = row_iota()
    sign = jnp.where(low, -1.0, 1.0)

    def at(l, h):
        return pl.ds(l * order + h * ROWS, ROWS)

    def column(l, h):
        return pl.ds(h * ROWS * order + l, ROWS, stride=order)

    def row(ref, l, k):
        return ref[pl.ds(l * order + k, 1), :]

    others = [unpacked(part) for part in parts[1:]]
    for l in range(ROWS):
        for h in range(2):
            value = parts[0][at(l, h), :]
            for other in others:
                value = value + other[l, h]
            other = pltpu.roll(value, HALF, 1)
            pack[at(l, h), :] = jnp.where(low, value, other)
            pack[at(l + ROWS, h), :] = jnp.where(low, other, value)

    sigma = jnp.full((1, WIDE), NOISE_FLOOR, jnp.float32)
    for c in range(trans.shape[0]):
        sigma = sigma + mix[c] * trans[c]

    trace = order * sigma
    for l in range(order):
        trace = trace + row(pack, l, l)
    inverse = 1.0 / trace
    kept = 1.0 - sigma * inverse

    for l in range(order):
        for h in range(2):
            here = pack[at(l, h), :]
            across = pack[column(l, h), :]
            above = jnp.where(low, here, -across)
            below = jnp.where(low, across, here)
            if h * ROWS > l:
                value = above
            elif h * ROWS + ROWS - 1 < l:
                value = below
            else:
                value = jnp.where(rows + h * ROWS >= l, above, below)
                value = jnp.where(jnp.logical_and(rows + h * ROWS == l, ~low), 0.0, value)
            gram[at(l, h), :] = value
            error = -value * inverse
            total = error
            if h * ROWS <= l < h * ROWS + ROWS:
                spot = jnp.logical_and(rows + h * ROWS == l, low)
                error = error + jnp.where(spot, kept, 0.0)
                total = error + jnp.where(spot, 1.0, 0.0)
            e_a[at(l, h), :] = error
            s_a[at(l, h), :] = total

    def spread(ref):
        for l in range(order):
            for h in range(2):
                value = ref[at(l, h), :]
                other = pltpu.roll(value, HALF, 1)
                d_re[at(l, h), :] = jnp.where(low, value, other)
                d_im[at(l, h), :] = jnp.where(low, other, value)

    def products(jobs):
        for base in range(0, order, 2):
            halves = (0, 1) if base < ROWS else (1,)
            plain, crossed = {}, {}
            for l in (base, base + 1):
                for j, (_, _, start) in enumerate(jobs):
                    for h in halves:
                        if start is not None:
                            plain[l, j, h] = start[at(l, h), :]
            for k in range(order):
                right = {
                    (j, h): ref[at(k, h), :] for j, (ref, _, _) in enumerate(jobs) for h in halves
                }
                for l in (base, base + 1):
                    left_re = row(d_re, l, k)
                    left_im = row(d_im, l, k) if k != l else None
                    for (j, h), value in right.items():
                        key = (l, j, h)
                        term = left_re * value
                        plain[key] = plain[key] + term if key in plain else term
                        if left_im is not None:
                            term = left_im * value
                            crossed[key] = crossed[key] + term if key in crossed else term
            for (l, j, h), value in plain.items():
                cross = pltpu.roll(crossed[l, j, h], HALF, 1)
                jobs[j][1][at(l, h), :] = value + sign * cross
        for _, ref, _ in jobs:
            for l in range(ROWS, order):
                ref[at(l, 0), :] = -sign * ref[column(l, 0), :]

    spread(e_a)
    products([(e_a, e_b, None)])

    def two_steps(_, carry):
        spread(e_b)
        products([(e_b, e_a, None), (s_a, s_b, s_a)])
        spread(e_a)
        products([(e_a, e_b, None), (s_b, s_a, s_b)])
        return carry

    lax.fori_loop(0, (NS_STEPS - 2) // 2, two_steps, 0)
    spread(e_b)
    products([(s_a, s_b, s_a)])

    for l in range(order):
        for h in range(2):
            s_a[at(l, h), :] = s_b[at(l, h), :] * inverse
    spread(s_a)
    products([(gram, e_a, None)])

    logs, norms = [], []
    for h in range(2):
        value = s_a[at(0, h), :] * e_a[at(0, h), :]
        for m in range(1, order):
            value = value + s_a[at(m, h), :] * e_a[at(m, h), :]
        energy = value + pltpu.roll(value, HALF, 1)
        norms.append(lax.rsqrt(jnp.maximum(energy, 0.0) + NORM_EPS))
        logs.append(jnp.log2(norms[h]))
        d_re[pl.ds(h * ROWS, ROWS), :] = norms[h]
    peak = jnp.zeros((ROWS, WIDE), jnp.float32)
    diagonal = [peak, peak]
    for l in range(order):
        for h in range(2) if l < ROWS else (1,):
            value = s_a[at(l, h), :] * d_re[pl.ds(l, 1), :] * norms[h]
            if h * ROWS <= l < h * ROWS + ROWS:
                spot = rows + h * ROWS == l
                diagonal[h] = jnp.where(spot, value, diagonal[h])
                value = jnp.where(spot, 0.0, value)
            peak = jnp.maximum(peak, jnp.abs(value))
    peak = jnp.max(peak, axis=0, keepdims=True)
    peak = jnp.maximum(jnp.broadcast_to(peak, (ROWS, WIDE)), 1e-18)
    level = jnp.ceil(jnp.log2(jnp.maximum(peak, pltpu.roll(peak, HALF, 1))) * 128.0) + 1.0
    shrink = jnp.exp2(level * (-1.0 / 128.0))
    norms = [norm * shrink for norm in norms]
    for l in range(ROWS):
        values = []
        for h in range(2):
            first = s_a[at(l, h), :]
            second = s_a[at(l + ROWS, h), :]
            where = rows + h * ROWS
            first = jnp.where(where >= l, first, pltpu.roll(first, HALF, 1))
            second = jnp.where(where >= l + ROWS, pltpu.roll(second, HALF, 1), second)
            value = jnp.where(
                low, first * d_re[pl.ds(l, 1), :], second * d_re[pl.ds(l + ROWS, 1), :]
            )
            value = jnp.round(value * norms[h] * FULL)
            here = jnp.logical_and(rows == l, low if h == 0 else ~low)
            values.append(jnp.where(here, level, value))
        out[pl.ds(l * order, order), :] = (
            jnp.concatenate(values, 0).astype(jnp.int32).astype(jnp.int16)
        )
    diagonal = [jnp.where(low, d, pltpu.roll(d, HALF, 1)) for d in diagonal]
    diagonal = [jnp.log2(jnp.maximum(d * shrink, 1e-30)) for d in diagonal]
    out[pl.ds(order * ROWS, order), :] = split(jnp.where(low, *diagonal), LOG_UNIT)
    out[pl.ds(order * ROWS + order, order), :] = split(jnp.where(low, *logs), LOG_UNIT)


def arrange_kernel(
    far_ref, own_ref, other_ref, sym_ref, sum_ref, symbols_ref, sem, flat, stacked, moved
):
    copy = pltpu.make_async_copy(far_ref, symbols_ref, sem)
    copy.start()
    copy.wait()
    _, layers, parts, syms, subcarriers = symbols_ref.shape
    tiles, sub, height, _ = sym_ref.shape
    few = 32
    span = sub * few
    quads = WIDE // few
    lanes = lane_iota()
    for l in range(layers):
        for r in range(parts):
            flat[pl.ds((l * parts + r) * syms, syms), :] = symbols_ref[0, l, r].astype(jnp.float32)
    for i in range(tiles * quads):
        stacked[pl.ds(i * height, height), :] = flat[:, pl.ds(i * span, span)].astype(jnp.bfloat16)
    source = lax.broadcasted_iota(jnp.int32, (span, span), 0)
    target = lax.broadcasted_iota(jnp.int32, (span, span), 1)
    table = jnp.where(source == target % few * sub + target // few, 1.0, 0.0).astype(jnp.bfloat16)
    moved[...] = jnp.dot(stacked[...], table, preferred_element_type=jnp.float32)
    for t in range(tiles):
        for k in range(sub):
            for g in range(height // ROWS):
                value = None
                for b in range(quads):
                    rows = pl.ds((t * quads + b) * height + g * ROWS, ROWS)
                    piece = moved[rows, pl.ds(k // quads * WIDE, WIDE)]
                    piece = turn(piece, (b - k % quads) * few)
                    value = piece if b == 0 else jnp.where(lanes >= b * few, piece, value)
                sym_ref[t, k, pl.ds(g * ROWS, ROWS), :] = value
    own, other = unpacked(own_ref), unpacked(other_ref)
    for (l, h), value in own.items():
        sum_ref[pl.ds((l * 2 + h) * ROWS, ROWS), :] = value + other[l, h]


def transmit_kernel(*refs, which, last, lanes_count, chunk):
    per_tile = WIDE // chunk
    ins, rest = refs[:per_tile], refs[per_tile:]
    amp, chan, sym, table_ref, twist = rest[:5]
    before = rest[5] if which else None
    out_ref = out = rest[5 + which]
    packs, pack, whole, norm, scale, scaled, weight, mixed, grid, table, spec_a, spec_b, sems = rest[
        6 + which : 19 + which
    ]
    if last:
        out, out_sems = rest[19 + which :]
    tiles, _, order, antennas, _ = chan.shape
    per_block, syms = sym.shape[1], sym.shape[2] // (2 * order)
    groups = antennas // ROWS
    lanes = lane_iota()
    lane = mirrored(lax.axis_index("lane"), lanes_count)
    tile = (lane // per_tile) ^ which
    halves = [
        pltpu.make_async_copy(
            table_ref.at[tile], table.at[:, pl.ds(h * 2 * WIDE, 2 * WIDE), :], sems.at[h]
        )
        for h in range(2)
    ]
    for copy in halves:
        copy.start()

    for s, ref in enumerate(ins):
        packs[lane % per_tile ^ s] = ref[...]

    def merged(values):
        first, second = values[0], pltpu.roll(values[0], HALF, 1)
        for z in range(1, per_tile):
            off = z * chunk
            first = jnp.where(lanes >= off, turn(values[z], off), first)
            second = jnp.where(lanes >= off, turn(values[z], off - HALF), second)
        return first, second

    for l in range(ROWS):
        held = [
            packs[z, pl.ds(l * order, order), :].astype(jnp.int32).astype(jnp.float32)
            for z in range(per_tile)
        ]
        for h in range(2):
            both = merged([value[h * ROWS : (h + 1) * ROWS] for value in held])
            for i, value in enumerate(both):
                pack[pl.ds((l + i * ROWS) * order + h * ROWS, ROWS), :] = value
    grow = jnp.exp2(pack[pl.ds(0, 1), :] * (1.0 / 128.0)) * (1.0 / FULL)
    tails = [
        merged(
            [
                joined(
                    packs[z, pl.ds(order * ROWS + i * order, order), :].astype(jnp.int32), LOG_UNIT
                )
                for z in range(per_tile)
            ]
        )
        for i in range(2)
    ]
    for h in range(2):
        spot = pl.ds(h * ROWS, ROWS)
        whole[spot, :] = jnp.exp2(tails[0][h]) * FULL
        norm[spot, :] = jnp.exp2(-tails[1][h])
        scale[spot, :] = amp[tile, spot, :] * grow
    for r in range(2):
        for m in range(order):
            for g in range(groups):
                spot = pl.ds(g * ROWS, ROWS)
                scaled[r, m, spot, :] = chan[tile, r, m, spot, :] * norm[pl.ds(m, 1), :]

    def row(l, m):
        return pack[pl.ds(l * order + m, 1), :]

    for base in range(0, order, 4):
        acc = {}

        def add(key, value):
            acc[key] = value if key not in acc else acc[key] + value

        for m in range(order):
            here = [
                [scaled[r, m, pl.ds(g * ROWS, ROWS), :] for g in range(groups)] for r in range(2)
            ]
            for l in range(base, base + 4):
                inv_re = row(min(l, m), max(l, m)) if l != m else whole[pl.ds(l, 1), :]
                inv_im = row(max(l, m), min(l, m)) if l != m else None
                if l > m:
                    inv_im = -inv_im
                for g in range(groups):
                    re, im = here[0][g], here[1][g]
                    if inv_im is None:
                        add((l, 0, g), re * inv_re)
                        add((l, 1, g), -(im * inv_re))
                    else:
                        add((l, 0, g), re * inv_re + im * inv_im)
                        add((l, 1, g), re * inv_im - im * inv_re)
        for (l, r, g), value in acc.items():
            value = value * scale[pl.ds(l, 1), :]
            weight[r, l, pl.ds(g * ROWS, ROWS), :] = value.astype(jnp.bfloat16).astype(jnp.float32)

    def precode(k, carry):
        acc = {}
        for l in range(order):
            w_re = [weight[0, l, pl.ds(g * ROWS, ROWS), :] for g in range(groups)]
            w_im = [weight[1, l, pl.ds(g * ROWS, ROWS), :] for g in range(groups)]
            for s in range(syms):
                s_re = sym[tile, k, pl.ds((l * 2 + 0) * syms + s, 1), :]
                s_im = sym[tile, k, pl.ds((l * 2 + 1) * syms + s, 1), :]
                for g in range(groups):
                    re = w_re[g] * s_re - w_im[g] * s_im
                    im = w_re[g] * s_im + w_im[g] * s_re
                    if l == 0:
                        acc[s, g] = (re, im)
                    else:
                        old = acc[s, g]
                        acc[s, g] = (old[0] + re, old[1] + im)
        for r in range(2):
            for s in range(syms):
                for g in range(groups):
                    spot = pl.ds(g * ROWS * syms + s, ROWS, stride=syms)
                    mixed[r, spot, :] = acc[s, g][r]
        for r in range(2):
            exact = mixed[r]
            high = exact.astype(jnp.bfloat16)
            grid[k, :, pl.ds(r * WIDE, WIDE)] = high
            grid[k, :, pl.ds((2 + r) * WIDE, WIDE)] = (exact - high.astype(jnp.float32)).astype(
                jnp.bfloat16
            )
        return carry

    lax.fori_loop(0, per_block, precode, 0)

    height = syms * antennas
    count = NFFT // WIDE // 4
    for copy in halves:
        copy.wait()
    left = grid[...].reshape(per_block * height, 4 * WIDE)
    specs = (spec_a, spec_b)

    def product(n):
        specs[n % 2][...] = jnp.dot(left, table[n], preferred_element_type=jnp.float32)

    def combine(n):
        spec = specs[n % 2]
        for g in range(height // ROWS):
            part = [None] * 4
            for k in range(per_block):
                rows = pl.ds(k * height + g * ROWS, ROWS)
                re = spec[rows, pl.ds(0, WIDE)]
                im = spec[rows, pl.ds(WIDE, WIDE)]
                if k > 0:
                    cos = twist[n, pl.ds(2 * k, 1), :]
                    sin = twist[n, pl.ds(2 * k + 1, 1), :]
                    re, im = re * cos - im * sin, re * sin + im * cos
                old = part[k % 4]
                part[k % 4] = (re, im) if old is None else (old[0] + re, old[1] + im)
            (r0, i0), (r1, i1), (r2, i2), (r3, i3) = part
            even_re, even_im, odd_re, odd_im = r0 + r2, i0 + i2, r1 + r3, i1 + i3
            gap_re, gap_im, far_re, far_im = r0 - r2, i0 - i2, r1 - r3, i1 - i3
            outs = (
                (even_re + odd_re, even_im + odd_im),
                (gap_re - far_im, gap_im + far_re),
                (even_re - odd_re, even_im - odd_im),
                (gap_re + far_im, gap_im - far_re),
            )
            spot = pl.ds(g * ROWS, ROWS)
            for q, pair in enumerate(outs):
                for r in range(2):
                    value = pair[r]
                    if which:
                        value = value + before[n, q, r, spot, :]
                    out[n, q, r, spot, :] = value

    done = []
    product(0)
    for n in range(count):
        if n + 1 < count:
            product(n + 1)
        combine(n)
        if not last:
            continue
        for q in range(4):
            for r in range(2):
                copy = pltpu.make_async_copy(
                    out.at[n, q, r].reshape(antennas, syms, WIDE),
                    out_ref.at[:, r, q * count + n],
                    out_sems.at[n, q, r],
                )
                copy.start()
                done.append(copy)
    for copy in done:
        copy.wait()


def transform_tables(blocks, subcarriers):
    sub = subcarriers // blocks
    tiles = blocks // WIDE
    quarter = NFFT // 4
    p = np.arange(blocks)[:, None]
    n = np.arange(quarter)[None, :]
    angle = 2.0 * np.pi / NFFT * ((sub * p - subcarriers // 2) * n % NFFT)
    cos = np.cos(angle) / math.sqrt(NFFT)
    sin = np.sin(angle) / math.sqrt(NFFT)
    count = quarter // WIDE
    table = np.stack([np.stack([cos, sin]), np.stack([-sin, cos])])
    table = table.reshape(2, 2, tiles, WIDE, count, WIDE).transpose(2, 4, 0, 3, 1, 5)
    table = table.reshape(tiles, count, 2 * WIDE, 2 * WIDE).astype(jnp.bfloat16)
    turns = 2.0 * np.pi / NFFT * (np.arange(sub)[:, None] * n)
    twist = np.stack([np.cos(turns), np.sin(turns)], 1).astype(np.float32)
    twist = twist.reshape(2 * sub, count, WIDE).transpose(1, 0, 2)
    return table, np.ascontiguousarray(twist)


def far(value):
    return pltpu.with_memory_space_constraint(value, pltpu.HBM)


def near(value):
    return pltpu.with_memory_space_constraint(value, pltpu.VMEM)


def swap(pieces):
    lanes = lax.axis_size("lane")
    return [pieces[0]] + [
        lax.ppermute(pieces[s], "lane", [(j, j ^ s) for j in range(lanes)]) for s in range(1, lanes)
    ]


def per_device(channel, symbols, layers, user_ids, user_power, neighbours, coupling):
    lanes = lax.axis_size("lane")
    cells = lax.axis_size("cell")
    _, antennas, _, order, blocks = channel.shape
    syms, subcarriers = symbols.shape[3:]
    sub = subcarriers // blocks
    chunk = blocks // lanes
    tiles = blocks // WIDE
    f32, bf16 = jnp.float32, jnp.bfloat16
    shape = jax.ShapeDtypeStruct
    table, twist = transform_tables(blocks, subcarriers)
    table, twist = jnp.asarray(table), jnp.asarray(twist)
    dma = pltpu.SemaphoreType.DMA

    amp, own, mix, turned, *pieces = pl.pallas_call(
        functools.partial(gram_kernel, lanes=lanes, chunk=chunk),
        out_shape=[pltpu.VMEM((tiles, order, WIDE), f32)]
        + [pltpu.VMEM((cells, 1, WIDE), f32)] * 2
        + [pltpu.VMEM((tiles, 2, order, antennas, WIDE), f32)]
        + [pltpu.VMEM((order * ROWS + order, WIDE), jnp.int16)] * lanes,
        in_specs=[HBM] * 6,
        out_specs=[VMEM] * (4 + lanes),
        scratch_shapes=[
            pltpu.VMEM((antennas, 2, order, blocks), f32),
            pltpu.VMEM((1, blocks), jnp.int32),
            pltpu.VMEM((order, blocks), jnp.int32),
            pltpu.VMEM(user_power.shape, f32),
            pltpu.SMEM(neighbours.shape, jnp.int32),
            pltpu.SMEM(coupling.shape, f32),
            pltpu.VMEM((lanes, order * ROWS + order, WIDE), jnp.int16),
            pltpu.VMEM((order, WIDE), f32),
            pltpu.VMEM((tiles, antennas * 2 * order, WIDE), f32),
            dma((5 + tiles,)),
        ],
        compiler_params=params(16),
        name="gram",
    )(*map(far, (channel, layers, user_ids, user_power, neighbours, coupling)))
    parts = swap(pieces)
    transmit = lax.all_to_all(own, "cell", 0, 0, tiled=True)

    sym, pair = pl.pallas_call(
        arrange_kernel,
        out_shape=(
            pltpu.VMEM((tiles, sub, order * 2 * syms, WIDE), f32),
            pltpu.VMEM((order * ROWS, WIDE), f32),
        ),
        in_specs=[HBM, VMEM, VMEM],
        out_specs=(VMEM, VMEM),
        scratch_shapes=[
            pltpu.VMEM(symbols.shape, bf16),
            pltpu.SemaphoreType.DMA,
            pltpu.VMEM((order * 2 * syms, subcarriers), f32),
            pltpu.VMEM((subcarriers // (sub * 32) * order * 2 * syms, sub * 32), bf16),
            pltpu.VMEM((subcarriers // (sub * 32) * order * 2 * syms, sub * 32), f32),
        ],
        compiler_params=params(16),
        cost_estimate=pl.CostEstimate(flops=10**9, bytes_accessed=8 * 10**6, transcendentals=0),
        name="arrange",
    )(far(symbols), near(parts[0]), near(parts[lanes // 2]))
    parts = [pair] + [part for s, part in enumerate(parts) if s not in (0, lanes // 2)]

    packed = pl.pallas_call(
        functools.partial(solve_kernel, count=lanes - 1),
        out_shape=pltpu.VMEM((order * ROWS + 2 * order, WIDE), jnp.int16),
        in_specs=[VMEM] * (1 + lanes),
        out_specs=VMEM,
        scratch_shapes=[pltpu.VMEM((order * order, WIDE), f32)] * 8,
        compiler_params=params(16),
        name="solve",
    )(near(transmit), near(mix), *map(near, parts))
    packs = swap([packed] * lanes)
    packs = [packs[mirrored(i, lanes)] for i in range(lanes)]

    per_tile = WIDE // chunk
    height = syms * antennas
    count = NFFT // WIDE // 4
    out = ()
    for which in range(tiles):
        last = which == tiles - 1
        result = (count, 4, 2, height, WIDE)
        final = (antennas, 2, NFFT // WIDE, syms, WIDE)
        out = pl.pallas_call(
            functools.partial(
                transmit_kernel, which=which, last=last, lanes_count=lanes, chunk=chunk
            ),
            out_shape=[shape(final, f32) if last else pltpu.VMEM(result, f32)],
            in_specs=[VMEM] * (per_tile + 3) + [HBM, VMEM] + [VMEM] * which,
            out_specs=[HBM if last else VMEM],
            scratch_shapes=[
                pltpu.VMEM((per_tile, order * ROWS + 2 * order, WIDE), jnp.int16),
                pltpu.VMEM((order * order, WIDE), f32),
                pltpu.VMEM((order, WIDE), f32),
                pltpu.VMEM((order, WIDE), f32),
                pltpu.VMEM((order, WIDE), f32),
                pltpu.VMEM((2, order, antennas, WIDE), f32),
                pltpu.VMEM((2, order, antennas, WIDE), f32),
                pltpu.VMEM((2, height, WIDE), f32),
                pltpu.VMEM((sub, height, 4 * WIDE), bf16),
                pltpu.VMEM((count, 4 * WIDE, 2 * WIDE), bf16),
                pltpu.VMEM((sub * height, 2 * WIDE), f32),
                pltpu.VMEM((sub * height, 2 * WIDE), f32),
                dma((2,)),
            ]
            + [pltpu.VMEM(result, f32), dma((count, 4, 2))] * last,
            compiler_params=params(16),
            cost_estimate=pl.CostEstimate(
                flops=10**9, bytes_accessed=4 * 10**6, transcendentals=0
            ),
            name="transmit",
        )(
            *map(near, packs[which * per_tile : (which + 1) * per_tile]),
            near(amp),
            near(turned),
            near(sym),
            far(table),
            near(twist),
            *map(near, out),
        )
    out = out[0].transpose(0, 1, 3, 2, 4)
    return out.reshape(1, antennas, 2, syms, NFFT)


def solution(mesh):
    in_specs = (
        P("cell", "lane", None, None, None),
        P("cell", None, None, None, None),
        P("cell", None),
        P("cell", None, None),
        P("cell", None),
        P(),
        P(),
    )
    out_specs = P("cell", "lane", None, None, None)
    return jax.shard_map(
        per_device, mesh=mesh, in_specs=in_specs, out_specs=out_specs, check_vma=False
    )
```

```python
import functools
import math

import jax
import jax.numpy as jnp
import numpy as np
from jax import lax
from jax.experimental import pallas as pl
from jax.experimental.pallas import tpu as pltpu
from jax.sharding import PartitionSpec as P

NFFT = 4096
NS_STEPS = 6
NORM_EPS = 1e-06
NOISE_FLOOR = 0.05
WIDE = 128
HALF = WIDE // 2
ROWS = 8
FULL = 32760.0
OFFSET = 32768
ROOT_UNIT = 2.0**24
LOG_UNIT = 2.0**23

VMEM = pl.BlockSpec(memory_space=pltpu.VMEM)
HBM = pl.BlockSpec(memory_space=pltpu.HBM)


def lane_iota():
    return lax.broadcasted_iota(jnp.int32, (ROWS, WIDE), 1)


def row_iota():
    return lax.broadcasted_iota(jnp.int32, (ROWS, WIDE), 0)


def turn(value, shift):
    shift = shift % WIDE
    return value if shift == 0 else pltpu.roll(value, shift, 1)


def mirrored(index, lanes):
    bits = lanes.bit_length() - 1
    total = 0
    for b in range(bits):
        total = total + ((index >> b) % 2) * (1 << (bits - 1 - b))
    return total


def split(value, unit):
    whole = jnp.round(value * unit).astype(jnp.int32)
    high = whole >> 16
    return jnp.concatenate([high, whole - (high << 16) - OFFSET], 0).astype(jnp.int16)


def joined(halves, unit):
    high = halves[:ROWS].astype(jnp.float32) * (65536.0 / unit)
    return high + (halves[ROWS:] + OFFSET).astype(jnp.float32) * (1.0 / unit)


def unpacked(piece):
    order = 2 * ROWS
    low, rows = lane_iota() < HALF, row_iota()
    root = joined(piece[pl.ds(order * ROWS, order), :].astype(jnp.int32), ROOT_UNIT)
    other = pltpu.roll(root, HALF, 1)
    both = (jnp.where(low, root, other), jnp.where(low, other, root))
    values = {}
    for l in range(ROWS):
        held = piece[pl.ds(l * order, order), :].astype(jnp.int32).astype(jnp.float32)
        for h in range(2):
            whole = jnp.logical_and(rows == l, low if h == 0 else ~low)
            part = jnp.where(whole, 1.0, held[h * ROWS : (h + 1) * ROWS] * (1.0 / FULL))
            values[l, h] = root[l : l + 1] * both[h] * part
    return values


def params(mib):
    return pltpu.CompilerParams(vmem_limit_bytes=mib * 1024 * 1024)


def gram_kernel(*refs, lanes, chunk):
    ins, outs = refs[:6], refs[9 : 9 + lanes]
    amp_all, own, mix = refs[6:9]
    channel, layers, ids_all, power, neigh, coup, pieces, inverses, sems = refs[9 + lanes :]
    antennas, _, order, blocks = channel.shape
    users = power.shape[1]
    tiles = blocks // WIDE
    small = [
        pltpu.make_async_copy(src, dst, sems.at[i])
        for i, (src, dst) in enumerate(
            (
                (ins[1], layers),
                (ins[2].at[0], ids_all),
                (ins[3], power),
                (ins[4], neigh),
                (ins[5], coup),
            )
        )
    ]
    large = [
        pltpu.make_async_copy(
            ins[0].at[0, :, :, :, pl.ds(t * WIDE, WIDE)],
            channel.at[:, :, :, pl.ds(t * WIDE, WIDE)],
            sems.at[5 + t],
        )
        for t in range(tiles)
    ]
    for copy in small + large:
        copy.start()
    for copy in small:
        copy.wait()

    rooted = jnp.sqrt(power[...])
    sums = []
    for t in range(tiles):
        spot = pl.ds(t * WIDE, WIDE)
        granted = layers[:, spot]
        total = jnp.zeros((ROWS, WIDE), jnp.float32)
        for h in range(order // ROWS):
            ids = ids_all[pl.ds(h * ROWS, ROWS), spot]
            picked = jnp.zeros((ROWS, WIDE), jnp.float32)
            for u in range(users // WIDE):
                table = jnp.broadcast_to(rooted[:, u * WIDE : (u + 1) * WIDE], (ROWS, WIDE))
                found = jnp.take_along_axis(table, ids % WIDE, axis=1, mode="promise_in_bounds")
                picked = jnp.where(ids // WIDE == u, found, picked)
            amp = jnp.where(row_iota() + h * ROWS < granted, picked, 0.0)
            amp_all[t, pl.ds(h * ROWS, ROWS), :] = amp
            total = total + amp * amp
        sums.append(jnp.sum(total, axis=0, keepdims=True) / order)
    lane = lax.axis_index("lane")
    start = mirrored(lane, lanes) * chunk
    mine = jnp.broadcast_to(sums[0], (ROWS, WIDE))
    for t in range(1, tiles):
        mine = jnp.where(start // WIDE == t, jnp.broadcast_to(sums[t], (ROWS, WIDE)), mine)
    mine = pltpu.roll(mine, lax.rem(WIDE - lax.rem(start, WIDE), WIDE), 1)
    both = jnp.where(lane_iota() < HALF, mine, pltpu.roll(mine, HALF, 1))
    own[...] = jnp.broadcast_to(both[0:1][None], own.shape)
    cell = lax.axis_index("cell")
    mix[...] = jnp.zeros(mix.shape, jnp.float32)
    for k in range(neigh.shape[1]):
        spot = neigh[cell, k]
        mix[spot] = mix[spot] + coup[cell, k]
    low = lane_iota() < HALF
    rows = row_iota()
    for t in range(tiles):
        spot = pl.ds(t * WIDE, WIDE)
        granted = layers[:, spot]
        inside = [rows + h * ROWS < granted for h in range(2)]
        large[t].wait()
        inverse, root = [], []
        for h in range(2):
            part = pl.ds(h * ROWS, ROWS)
            total = jnp.zeros((ROWS, WIDE), jnp.float32)
            for a in range(antennas):
                re, im = channel[a, 0, part, spot], channel[a, 1, part, spot]
                total = total + (re * re + im * im)
            total = jnp.where(inside[h], total, 0.0)
            inverse.append(jnp.where(total > 0.0, lax.rsqrt(total), 0.0))
            root.append(total * inverse[h])
            inverses[part, :] = inverse[h] * FULL
        chunks = range(t * WIDE // chunk, (t + 1) * WIDE // chunk)

        def packed(top, bottom, z):
            off = z * chunk - t * WIDE
            return jnp.where(low, turn(top, -off), turn(bottom, HALF - off))

        for z in chunks:
            pieces[lane ^ mirrored(z, lanes), pl.ds(order * ROWS, order), :] = split(
                packed(root[0], root[1], z), ROOT_UNIT
            )
        for base in range(0, ROWS, 2):
            tops = (base, base + 1)
            acc = {}

            def add(key, value):
                acc[key] = value if key not in acc else acc[key] + value

            for a in range(antennas):
                re = [channel[a, 0, pl.ds(h * ROWS, ROWS), spot] for h in range(2)]
                im = [channel[a, 1, pl.ds(h * ROWS, ROWS), spot] for h in range(2)]
                for l in tops:
                    lre = channel[a, 0, pl.ds(l, 1), spot]
                    lim = channel[a, 1, pl.ds(l, 1), spot]
                    add((l, "re", 0), lre * re[0] + lim * im[0])
                    add((l, "re", 1), lre * re[1] + lim * im[1])
                    add((l, "im", 0), lim * re[0] - lre * im[0])
                    g = l + ROWS
                    gre = channel[a, 0, pl.ds(g, 1), spot]
                    gim = channel[a, 1, pl.ds(g, 1), spot]
                    add((g, "re", 1), gre * re[1] + gim * im[1])
                    add((g, "im", 0), gim * re[0] - gre * im[0])
                    add((g, "im", 1), gim * re[1] - gre * im[1])
            for l in tops:
                g = l + ROWS
                here = granted > l
                there = granted > g
                upper = [
                    jnp.where(rows >= l, acc[l, "re", 0], acc[l, "im", 0]),
                    acc[l, "re", 1],
                ]
                lower = [
                    acc[g, "im", 0],
                    jnp.where(rows >= l, acc[g, "re", 1], acc[g, "im", 1]),
                ]
                tops_out, bottoms_out = [], []
                for h in range(2):
                    top = jnp.where(jnp.logical_and(inside[h], here), upper[h], 0.0)
                    bottom = jnp.where(jnp.logical_and(inside[h], there), lower[h], 0.0)
                    tops_out.append(top * inverses[pl.ds(l, 1), :] * inverse[h])
                    bottoms_out.append(bottom * inverses[pl.ds(g, 1), :] * inverse[h])
                for z in chunks:
                    value = jnp.concatenate(
                        [packed(tops_out[h], bottoms_out[h], z) for h in range(2)], 0
                    )
                    pieces[lane ^ mirrored(z, lanes), pl.ds(l * order, order), :] = (
                        jnp.round(value).astype(jnp.int32).astype(jnp.int16)
                    )
    for s in range(lanes):
        outs[s][...] = pieces[s]


def solve_kernel(*refs, count):
    trans, mix = refs[:2]
    parts, out = refs[2 : 2 + count], refs[2 + count]
    pack, gram, e_a, e_b, s_a, s_b, d_re, d_im = refs[3 + count :]
    order = 2 * ROWS
    low = lane_iota() < HALF
    rows = row_iota()
    sign = jnp.where(low, -1.0, 1.0)

    def at(l, h):
        return pl.ds(l * order + h * ROWS, ROWS)

    def column(l, h):
        return pl.ds(h * ROWS * order + l, ROWS, stride=order)

    def row(ref, l, k):
        return ref[pl.ds(l * order + k, 1), :]

    others = [unpacked(part) for part in parts[1:]]
    for l in range(ROWS):
        for h in range(2):
            value = parts[0][at(l, h), :]
            for other in others:
                value = value + other[l, h]
            other = pltpu.roll(value, HALF, 1)
            pack[at(l, h), :] = jnp.where(low, value, other)
            pack[at(l + ROWS, h), :] = jnp.where(low, other, value)

    sigma = jnp.full((1, WIDE), NOISE_FLOOR, jnp.float32)
    for c in range(trans.shape[0]):
        sigma = sigma + mix[c] * trans[c]

    trace = order * sigma
    for l in range(order):
        trace = trace + row(pack, l, l)
    inverse = 1.0 / trace
    kept = 1.0 - sigma * inverse

    for l in range(order):
        for h in range(2):
            here = pack[at(l, h), :]
            across = pack[column(l, h), :]
            above = jnp.where(low, here, -across)
            below = jnp.where(low, across, here)
            if h * ROWS > l:
                value = above
            elif h * ROWS + ROWS - 1 < l:
                value = below
            else:
                value = jnp.where(rows + h * ROWS >= l, above, below)
                value = jnp.where(jnp.logical_and(rows + h * ROWS == l, ~low), 0.0, value)
            gram[at(l, h), :] = value
            error = -value * inverse
            total = error
            if h * ROWS <= l < h * ROWS + ROWS:
                spot = jnp.logical_and(rows + h * ROWS == l, low)
                error = error + jnp.where(spot, kept, 0.0)
                total = error + jnp.where(spot, 1.0, 0.0)
            e_a[at(l, h), :] = error
            s_a[at(l, h), :] = total

    def spread(ref):
        for l in range(order):
            for h in range(2):
                value = ref[at(l, h), :]
                other = pltpu.roll(value, HALF, 1)
                d_re[at(l, h), :] = jnp.where(low, value, other)
                d_im[at(l, h), :] = jnp.where(low, other, value)

    def products(jobs):
        for base in range(0, order, 2):
            halves = (0, 1) if base < ROWS else (1,)
            plain, crossed = {}, {}
            for l in (base, base + 1):
                for j, (_, _, start) in enumerate(jobs):
                    for h in halves:
                        if start is not None:
                            plain[l, j, h] = start[at(l, h), :]
            for k in range(order):
                right = {
                    (j, h): ref[at(k, h), :] for j, (ref, _, _) in enumerate(jobs) for h in halves
                }
                for l in (base, base + 1):
                    left_re = row(d_re, l, k)
                    left_im = row(d_im, l, k) if k != l else None
                    for (j, h), value in right.items():
                        key = (l, j, h)
                        term = left_re * value
                        plain[key] = plain[key] + term if key in plain else term
                        if left_im is not None:
                            term = left_im * value
                            crossed[key] = crossed[key] + term if key in crossed else term
            for (l, j, h), value in plain.items():
                cross = pltpu.roll(crossed[l, j, h], HALF, 1)
                jobs[j][1][at(l, h), :] = value + sign * cross
        for _, ref, _ in jobs:
            for l in range(ROWS, order):
                ref[at(l, 0), :] = -sign * ref[column(l, 0), :]

    spread(e_a)
    products([(e_a, e_b, None)])

    def two_steps(_, carry):
        spread(e_b)
        products([(e_b, e_a, None), (s_a, s_b, s_a)])
        spread(e_a)
        products([(e_a, e_b, None), (s_b, s_a, s_b)])
        return carry

    lax.fori_loop(0, (NS_STEPS - 2) // 2, two_steps, 0)
    spread(e_b)
    products([(s_a, s_b, s_a)])

    for l in range(order):
        for h in range(2):
            s_a[at(l, h), :] = s_b[at(l, h), :] * inverse
    spread(s_a)
    products([(gram, e_a, None)])

    logs, norms = [], []
    for h in range(2):
        value = s_a[at(0, h), :] * e_a[at(0, h), :]
        for m in range(1, order):
            value = value + s_a[at(m, h), :] * e_a[at(m, h), :]
        energy = value + pltpu.roll(value, HALF, 1)
        norms.append(lax.rsqrt(jnp.maximum(energy, 0.0) + NORM_EPS))
        logs.append(jnp.log2(norms[h]))
        d_re[pl.ds(h * ROWS, ROWS), :] = norms[h]
    peak = jnp.zeros((ROWS, WIDE), jnp.float32)
    diagonal = [peak, peak]
    for l in range(order):
        for h in range(2) if l < ROWS else (1,):
            value = s_a[at(l, h), :] * d_re[pl.ds(l, 1), :] * norms[h]
            if h * ROWS <= l < h * ROWS + ROWS:
                spot = rows + h * ROWS == l
                diagonal[h] = jnp.where(spot, value, diagonal[h])
                value = jnp.where(spot, 0.0, value)
            peak = jnp.maximum(peak, jnp.abs(value))
    peak = jnp.max(peak, axis=0, keepdims=True)
    peak = jnp.maximum(jnp.broadcast_to(peak, (ROWS, WIDE)), 1e-18)
    level = jnp.ceil(jnp.log2(jnp.maximum(peak, pltpu.roll(peak, HALF, 1))) * 128.0) + 1.0
    shrink = jnp.exp2(level * (-1.0 / 128.0))
    norms = [norm * shrink for norm in norms]
    for l in range(ROWS):
        values = []
        for h in range(2):
            first = s_a[at(l, h), :]
            second = s_a[at(l + ROWS, h), :]
            where = rows + h * ROWS
            first = jnp.where(where >= l, first, pltpu.roll(first, HALF, 1))
            second = jnp.where(where >= l + ROWS, pltpu.roll(second, HALF, 1), second)
            value = jnp.where(
                low, first * d_re[pl.ds(l, 1), :], second * d_re[pl.ds(l + ROWS, 1), :]
            )
            value = jnp.round(value * norms[h] * FULL)
            here = jnp.logical_and(rows == l, low if h == 0 else ~low)
            values.append(jnp.where(here, level, value))
        out[pl.ds(l * order, order), :] = (
            jnp.concatenate(values, 0).astype(jnp.int32).astype(jnp.int16)
        )
    diagonal = [jnp.where(low, d, pltpu.roll(d, HALF, 1)) for d in diagonal]
    diagonal = [jnp.log2(jnp.maximum(d * shrink, 1e-30)) for d in diagonal]
    out[pl.ds(order * ROWS, order), :] = split(jnp.where(low, *diagonal), LOG_UNIT)
    out[pl.ds(order * ROWS + order, order), :] = split(jnp.where(low, *logs), LOG_UNIT)


def arrange_kernel(
    far_ref,
    channel_ref,
    own_ref,
    other_ref,
    sym_ref,
    both_ref,
    turned_ref,
    sum_ref,
    symbols_ref,
    channel,
    sems,
    flat,
    stacked,
    moved,
    stage,
):
    copies = [
        pltpu.make_async_copy(far_ref, symbols_ref, sems.at[0]),
        pltpu.make_async_copy(channel_ref, channel, sems.at[1]),
    ]
    for copy in copies:
        copy.start()
    copies[0].wait()
    _, layers, parts, syms, subcarriers = symbols_ref.shape
    tiles, sub, height, _ = sym_ref.shape
    few = 32
    span = sub * few
    quads = WIDE // few
    lanes = lane_iota()
    for l in range(layers):
        for r in range(parts):
            flat[pl.ds((l * parts + r) * syms, syms), :] = symbols_ref[0, l, r].astype(jnp.float32)
    for i in range(tiles * quads):
        stacked[pl.ds(i * height, height), :] = flat[:, pl.ds(i * span, span)].astype(jnp.bfloat16)
    source = lax.broadcasted_iota(jnp.int32, (span, span), 0)
    target = lax.broadcasted_iota(jnp.int32, (span, span), 1)
    table = jnp.where(source == target % few * sub + target // few, 1.0, 0.0).astype(jnp.bfloat16)
    moved[...] = jnp.dot(stacked[...], table, preferred_element_type=jnp.float32)
    for t in range(tiles):
        for k in range(sub):
            for g in range(height // ROWS):
                value = None
                for b in range(quads):
                    rows = pl.ds((t * quads + b) * height + g * ROWS, ROWS)
                    piece = moved[rows, pl.ds(k // quads * WIDE, WIDE)]
                    piece = turn(piece, (b - k % quads) * few)
                    value = piece if b == 0 else jnp.where(lanes >= b * few, piece, value)
                sym_ref[t, k, pl.ds(g * ROWS, ROWS), :] = value
                both_ref[t, k, pl.ds(g * ROWS, ROWS), :] = value + pltpu.roll(
                    value, ROWS - syms, 0
                )
    copies[1].wait()
    antennas = channel.shape[1]
    for t in range(tiles):
        for a in range(antennas):
            for r in range(2):
                for h in range(layers // ROWS):
                    stage[t, pl.ds((a * 2 + r) * layers + h * ROWS, ROWS), :] = channel[
                        0, a, r, pl.ds(h * ROWS, ROWS), pl.ds(t * WIDE, WIDE)
                    ]
        for r in range(2):
            for m in range(layers):
                for h in range(antennas // ROWS):
                    first = h * ROWS * 2 * layers + r * layers + m
                    turned_ref[t, r, m, pl.ds(h * ROWS, ROWS), :] = stage[
                        t, pl.ds(first, ROWS, stride=2 * layers), :
                    ]
    own, other = unpacked(own_ref), unpacked(other_ref)
    for (l, h), value in own.items():
        sum_ref[pl.ds((l * 2 + h) * ROWS, ROWS), :] = value + other[l, h]


def transmit_kernel(*refs, which, last, lanes_count, chunk):
    per_tile = WIDE // chunk
    ins, rest = refs[:per_tile], refs[per_tile:]
    amp, chan, sym, sums, table_ref, twist = rest[:6]
    before = rest[6] if which else None
    out_ref = out = rest[6 + which]
    packs, pack, whole, norm, scale, scaled, weight, grid, table, spec_a, spec_b, sems = rest[
        7 + which : 19 + which
    ]
    if last:
        out, out_sems = rest[19 + which :]
    tiles, _, order, antennas, _ = chan.shape
    per_block, syms = sym.shape[1], sym.shape[2] // (2 * order)
    groups = antennas // ROWS
    lanes = lane_iota()
    lane = mirrored(lax.axis_index("lane"), lanes_count)
    tile = (lane // per_tile) ^ which
    halves = [
        pltpu.make_async_copy(
            table_ref.at[tile], table.at[:, pl.ds(h * 2 * WIDE, 2 * WIDE), :], sems.at[h]
        )
        for h in range(2)
    ]
    for copy in halves:
        copy.start()

    for s, ref in enumerate(ins):
        packs[lane % per_tile ^ s] = ref[...]

    def merged(values):
        first, second = values[0], pltpu.roll(values[0], HALF, 1)
        for z in range(1, per_tile):
            off = z * chunk
            first = jnp.where(lanes >= off, turn(values[z], off), first)
            second = jnp.where(lanes >= off, turn(values[z], off - HALF), second)
        return first, second

    for l in range(ROWS):
        held = [
            packs[z, pl.ds(l * order, order), :].astype(jnp.int32).astype(jnp.float32)
            for z in range(per_tile)
        ]
        for h in range(2):
            both = merged([value[h * ROWS : (h + 1) * ROWS] for value in held])
            for i, value in enumerate(both):
                pack[pl.ds((l + i * ROWS) * order + h * ROWS, ROWS), :] = value
    grow = jnp.exp2(pack[pl.ds(0, 1), :] * (1.0 / 128.0)) * (1.0 / FULL)
    tails = [
        merged(
            [
                joined(
                    packs[z, pl.ds(order * ROWS + i * order, order), :].astype(jnp.int32), LOG_UNIT
                )
                for z in range(per_tile)
            ]
        )
        for i in range(2)
    ]
    for h in range(2):
        spot = pl.ds(h * ROWS, ROWS)
        whole[spot, :] = jnp.exp2(tails[0][h]) * FULL
        norm[spot, :] = jnp.exp2(-tails[1][h])
        scale[spot, :] = amp[tile, spot, :] * grow
    for m in range(order):
        for g in range(groups):
            spot = pl.ds(g * ROWS, ROWS)
            re, im = [chan[tile, r, m, spot, :] * norm[pl.ds(m, 1), :] for r in range(2)]
            scaled[0, m, spot, :] = re
            scaled[1, m, spot, :] = im
            scaled[2, m, spot, :] = re - im

    def row(l, m):
        return pack[pl.ds(l * order + m, 1), :]

    for base in range(0, order, 4):
        acc = {}

        def add(key, value):
            acc[key] = value if key not in acc else acc[key] + value

        for m in range(order):
            here = [
                [scaled[r, m, pl.ds(g * ROWS, ROWS), :] for g in range(groups)] for r in range(3)
            ]
            for l in range(base, base + 4):
                if l == m:
                    inv = whole[pl.ds(l, 1), :]
                    for g in range(groups):
                        add((l, 0, g), here[0][g] * inv)
                        add((l, 2, g), here[2][g] * inv)
                    continue
                inv_re, inv_im = row(min(l, m), max(l, m)), row(max(l, m), min(l, m))
                if l > m:
                    inv_im = -inv_im
                total = inv_re + inv_im
                for g in range(groups):
                    add((l, 0, g), here[0][g] * inv_re)
                    add((l, 1, g), here[1][g] * inv_im)
                    add((l, 2, g), here[2][g] * total)
        for l in range(base, base + 4):
            for g in range(groups):
                first, second, third = [acc[l, i, g] for i in range(3)]
                grown = scale[pl.ds(l, 1), :]
                spot = pl.ds(g * ROWS, ROWS)
                re = ((first + second) * grown).astype(jnp.bfloat16).astype(jnp.float32)
                im = ((third - first + second) * grown).astype(jnp.bfloat16).astype(jnp.float32)
                weight[0, l, spot, :] = re
                weight[1, l, spot, :] = im
                weight[2, l, spot, :] = re + im

    def precode(k, carry):
        acc = {}
        for l in range(order):
            held = [
                [weight[i, l, pl.ds(g * ROWS, ROWS), :] for g in range(groups)] for i in range(3)
            ]
            for s in range(syms):
                parts = (
                    sym[tile, k, pl.ds(l * 2 * syms + s, 1), :],
                    sym[tile, k, pl.ds((l * 2 + 1) * syms + s, 1), :],
                    sums[tile, k, pl.ds(l * 2 * syms + s, 1), :],
                )
                for i in range(3):
                    for g in range(groups):
                        term = held[i][g] * parts[i]
                        acc[s, g, i] = term if l == 0 else acc[s, g, i] + term
        for r in range(2):
            values = []
            for s in range(syms):
                for g in range(groups):
                    first, second, third = [acc[s, g, i] for i in range(3)]
                    values.append(first - second if r == 0 else third - first - second)
            exact = jnp.concatenate(values, axis=0)
            high = exact.astype(jnp.bfloat16)
            grid[k, :, pl.ds(r * WIDE, WIDE)] = high
            grid[k, :, pl.ds((2 + r) * WIDE, WIDE)] = (exact - high.astype(jnp.float32)).astype(
                jnp.bfloat16
            )
        return carry

    lax.fori_loop(0, per_block, precode, 0)

    height = syms * antennas
    count = NFFT // WIDE // 4
    for copy in halves:
        copy.wait()
    left = grid[...].reshape(per_block * height, 4 * WIDE)
    specs = (spec_a, spec_b)

    def product(n):
        specs[n % 2][...] = jnp.dot(left, table[n], preferred_element_type=jnp.float32)

    def combine(n):
        spec = specs[n % 2]
        for g in range(height // ROWS):
            part = [None] * 4
            for k in range(per_block):
                rows = pl.ds(k * height + g * ROWS, ROWS)
                re = spec[rows, pl.ds(0, WIDE)]
                im = spec[rows, pl.ds(WIDE, WIDE)]
                if k > 0:
                    cos = twist[n, pl.ds(2 * k, 1), :]
                    sin = twist[n, pl.ds(2 * k + 1, 1), :]
                    re, im = re * cos - im * sin, re * sin + im * cos
                old = part[k % 4]
                part[k % 4] = (re, im) if old is None else (old[0] + re, old[1] + im)
            (r0, i0), (r1, i1), (r2, i2), (r3, i3) = part
            even_re, even_im, odd_re, odd_im = r0 + r2, i0 + i2, r1 + r3, i1 + i3
            gap_re, gap_im, far_re, far_im = r0 - r2, i0 - i2, r1 - r3, i1 - i3
            outs = (
                (even_re + odd_re, even_im + odd_im),
                (gap_re - far_im, gap_im + far_re),
                (even_re - odd_re, even_im - odd_im),
                (gap_re + far_im, gap_im - far_re),
            )
            s, first = g // groups, g % groups * ROWS
            for q, pair in enumerate(outs):
                for r in range(2):
                    value = pair[r]
                    spot = pl.ds(g * ROWS, ROWS)
                    if which:
                        value = value + before[n, q, r, spot, :]
                    if last:
                        start = (first * 2 + r) * syms + s
                        out[n, q, pl.ds(start, ROWS, stride=2 * syms), :] = value
                    else:
                        out[n, q, r, spot, :] = value

    done = []
    product(0)
    for n in range(count):
        if n + 1 < count:
            product(n + 1)
        combine(n)
        if not last:
            continue
        for q in range(4):
            copy = pltpu.make_async_copy(
                out.at[n, q].reshape(antennas, 2, syms, WIDE),
                out_ref.at[:, :, q * count + n],
                out_sems.at[n, q],
            )
            copy.start()
            done.append(copy)
    for copy in done:
        copy.wait()


def transform_tables(blocks, subcarriers):
    sub = subcarriers // blocks
    tiles = blocks // WIDE
    quarter = NFFT // 4
    p = np.arange(blocks)[:, None]
    n = np.arange(quarter)[None, :]
    angle = 2.0 * np.pi / NFFT * ((sub * p - subcarriers // 2) * n % NFFT)
    cos = np.cos(angle) / math.sqrt(NFFT)
    sin = np.sin(angle) / math.sqrt(NFFT)
    count = quarter // WIDE
    table = np.stack([np.stack([cos, sin]), np.stack([-sin, cos])])
    table = table.reshape(2, 2, tiles, WIDE, count, WIDE).transpose(2, 4, 0, 3, 1, 5)
    table = table.reshape(tiles, count, 2 * WIDE, 2 * WIDE).astype(jnp.bfloat16)
    turns = 2.0 * np.pi / NFFT * (np.arange(sub)[:, None] * n)
    twist = np.stack([np.cos(turns), np.sin(turns)], 1).astype(np.float32)
    twist = twist.reshape(2 * sub, count, WIDE).transpose(1, 0, 2)
    return table, np.ascontiguousarray(twist)


def far(value):
    return pltpu.with_memory_space_constraint(value, pltpu.HBM)


def near(value):
    return pltpu.with_memory_space_constraint(value, pltpu.VMEM)


def swap(pieces):
    lanes = lax.axis_size("lane")
    return [pieces[0]] + [
        lax.ppermute(pieces[s], "lane", [(j, j ^ s) for j in range(lanes)]) for s in range(1, lanes)
    ]


def per_device(channel, symbols, layers, user_ids, user_power, neighbours, coupling):
    lanes = lax.axis_size("lane")
    cells = lax.axis_size("cell")
    _, antennas, _, order, blocks = channel.shape
    syms, subcarriers = symbols.shape[3:]
    sub = subcarriers // blocks
    chunk = blocks // lanes
    tiles = blocks // WIDE
    f32, bf16 = jnp.float32, jnp.bfloat16
    shape = jax.ShapeDtypeStruct
    table, twist = transform_tables(blocks, subcarriers)
    table, twist = jnp.asarray(table), jnp.asarray(twist)
    dma = pltpu.SemaphoreType.DMA

    amp, own, mix, *pieces = pl.pallas_call(
        functools.partial(gram_kernel, lanes=lanes, chunk=chunk),
        out_shape=[pltpu.VMEM((tiles, order, WIDE), f32)]
        + [pltpu.VMEM((cells, 1, WIDE), f32)] * 2
        + [pltpu.VMEM((order * ROWS + order, WIDE), jnp.int16)] * lanes,
        in_specs=[HBM] * 6,
        out_specs=[VMEM] * (3 + lanes),
        scratch_shapes=[
            pltpu.VMEM((antennas, 2, order, blocks), f32),
            pltpu.VMEM((1, blocks), jnp.int32),
            pltpu.VMEM((order, blocks), jnp.int32),
            pltpu.VMEM(user_power.shape, f32),
            pltpu.SMEM(neighbours.shape, jnp.int32),
            pltpu.SMEM(coupling.shape, f32),
            pltpu.VMEM((lanes, order * ROWS + order, WIDE), jnp.int16),
            pltpu.VMEM((order, WIDE), f32),
            dma((5 + tiles,)),
        ],
        compiler_params=params(16),
        name="gram",
    )(*map(far, (channel, layers, user_ids, user_power, neighbours, coupling)))
    parts = swap(pieces)
    transmit = lax.all_to_all(own, "cell", 0, 0, tiled=True)

    sym, both, turned, pair = pl.pallas_call(
        arrange_kernel,
        out_shape=(
            pltpu.VMEM((tiles, sub, order * 2 * syms, WIDE), f32),
            pltpu.VMEM((tiles, sub, order * 2 * syms, WIDE), f32),
            pltpu.VMEM((tiles, 2, order, antennas, WIDE), f32),
            pltpu.VMEM((order * ROWS, WIDE), f32),
        ),
        in_specs=[HBM, HBM, VMEM, VMEM],
        out_specs=(VMEM,) * 4,
        scratch_shapes=[
            pltpu.VMEM(symbols.shape, bf16),
            pltpu.VMEM(channel.shape, f32),
            dma((2,)),
            pltpu.VMEM((order * 2 * syms, subcarriers), f32),
            pltpu.VMEM((subcarriers // (sub * 32) * order * 2 * syms, sub * 32), bf16),
            pltpu.VMEM((subcarriers // (sub * 32) * order * 2 * syms, sub * 32), f32),
            pltpu.VMEM((tiles, antennas * 2 * order, WIDE), f32),
        ],
        compiler_params=params(16),
        cost_estimate=pl.CostEstimate(flops=10**9, bytes_accessed=8 * 10**6, transcendentals=0),
        name="arrange",
    )(far(symbols), far(channel), near(parts[0]), near(parts[lanes - 1]))
    parts = [pair] + parts[1 : lanes - 1]

    packed = pl.pallas_call(
        functools.partial(solve_kernel, count=lanes - 1),
        out_shape=pltpu.VMEM((order * ROWS + 2 * order, WIDE), jnp.int16),
        in_specs=[VMEM] * (1 + lanes),
        out_specs=VMEM,
        scratch_shapes=[pltpu.VMEM((order * order, WIDE), f32)] * 8,
        compiler_params=params(16),
        name="solve",
    )(near(transmit), near(mix), *map(near, parts))
    packs = swap([packed] * lanes)
    packs = [packs[mirrored(i, lanes)] for i in range(lanes)]

    per_tile = WIDE // chunk
    height = syms * antennas
    count = NFFT // WIDE // 4
    out = ()
    for which in range(tiles):
        last = which == tiles - 1
        result = (count, 4, 2, height, WIDE)
        final = (antennas, 2, NFFT // WIDE, syms, WIDE)
        out = pl.pallas_call(
            functools.partial(
                transmit_kernel, which=which, last=last, lanes_count=lanes, chunk=chunk
            ),
            out_shape=[shape(final, f32) if last else pltpu.VMEM(result, f32)],
            in_specs=[VMEM] * (per_tile + 4) + [HBM, VMEM] + [VMEM] * which,
            out_specs=[HBM if last else VMEM],
            scratch_shapes=[
                pltpu.VMEM((per_tile, order * ROWS + 2 * order, WIDE), jnp.int16),
                pltpu.VMEM((order * order, WIDE), f32),
                pltpu.VMEM((order, WIDE), f32),
                pltpu.VMEM((order, WIDE), f32),
                pltpu.VMEM((order, WIDE), f32),
                pltpu.VMEM((3, order, antennas, WIDE), f32),
                pltpu.VMEM((3, order, antennas, WIDE), f32),
                pltpu.VMEM((sub, height, 4 * WIDE), bf16),
                pltpu.VMEM((count, 4 * WIDE, 2 * WIDE), bf16),
                pltpu.VMEM((sub * height, 2 * WIDE), f32),
                pltpu.VMEM((sub * height, 2 * WIDE), f32),
                dma((2,)),
            ]
            + [pltpu.VMEM((count, 4, 2 * height, WIDE), f32), dma((count, 4))] * last,
            compiler_params=params(16),
            cost_estimate=pl.CostEstimate(
                flops=10**9, bytes_accessed=4 * 10**6, transcendentals=0
            ),
            name="transmit",
        )(
            *map(near, packs[which * per_tile : (which + 1) * per_tile]),
            near(amp),
            near(turned),
            near(sym),
            near(both),
            far(table),
            near(twist),
            *map(near, out),
        )
    out = out[0].transpose(0, 1, 3, 2, 4)
    return out.reshape(1, antennas, 2, syms, NFFT)


def solution(mesh):
    in_specs = (
        P("cell", "lane", None, None, None),
        P("cell", None, None, None, None),
        P("cell", None),
        P("cell", None, None),
        P("cell", None),
        P(),
        P(),
    )
    out_specs = P("cell", "lane", None, None, None)
    return jax.shard_map(
        per_device, mesh=mesh, in_specs=in_specs, out_specs=out_specs, check_vma=False
    )
```

```python
import functools
import math

import jax
import jax.numpy as jnp
import numpy as np
from jax import lax
from jax.experimental import pallas as pl
from jax.experimental.pallas import tpu as pltpu
from jax.sharding import PartitionSpec as P

NFFT = 4096
NS_STEPS = 6
NORM_EPS = 1e-06
NOISE_FLOOR = 0.05
WIDE = 128
HALF = WIDE // 2
ROWS = 8
FULL = 32760.0
OFFSET = 32768
ROOT_UNIT = 2.0**24
LOG_UNIT = 2.0**23

VMEM = pl.BlockSpec(memory_space=pltpu.VMEM)
HBM = pl.BlockSpec(memory_space=pltpu.HBM)


def lane_iota():
    return lax.broadcasted_iota(jnp.int32, (ROWS, WIDE), 1)


def row_iota():
    return lax.broadcasted_iota(jnp.int32, (ROWS, WIDE), 0)


def turn(value, shift):
    shift = shift % WIDE
    return value if shift == 0 else pltpu.roll(value, shift, 1)


def mirrored(index, lanes):
    bits = lanes.bit_length() - 1
    total = 0
    for b in range(bits):
        total = total + ((index >> b) % 2) * (1 << (bits - 1 - b))
    return total


def split(value, unit):
    whole = jnp.round(value * unit).astype(jnp.int32)
    high = whole >> 16
    return jnp.concatenate([high, whole - (high << 16) - OFFSET], 0).astype(jnp.int16)


def joined(halves, unit):
    high = halves[:ROWS].astype(jnp.float32) * (65536.0 / unit)
    return high + (halves[ROWS:] + OFFSET).astype(jnp.float32) * (1.0 / unit)


def unpacked(piece):
    order = 2 * ROWS
    low, rows = lane_iota() < HALF, row_iota()
    root = joined(piece[pl.ds(order * ROWS, order), :].astype(jnp.int32), ROOT_UNIT)
    other = pltpu.roll(root, HALF, 1)
    both = (jnp.where(low, root, other), jnp.where(low, other, root))
    values = {}
    for l in range(ROWS):
        held = piece[pl.ds(l * order, order), :].astype(jnp.int32).astype(jnp.float32)
        for h in range(2):
            whole = jnp.logical_and(rows == l, low if h == 0 else ~low)
            part = jnp.where(whole, 1.0, held[h * ROWS : (h + 1) * ROWS] * (1.0 / FULL))
            values[l, h] = root[l : l + 1] * both[h] * part
    return values


def params(mib):
    return pltpu.CompilerParams(vmem_limit_bytes=mib * 1024 * 1024)


def gram_kernel(*refs, lanes, chunk):
    ins, outs = refs[:6], refs[9 : 9 + lanes]
    amp_all, own, mix = refs[6:9]
    channel, layers, ids_all, power, neigh, coup, pieces, inverses, sems = refs[9 + lanes :]
    antennas, _, order, blocks = channel.shape
    users = power.shape[1]
    tiles = blocks // WIDE
    small = [
        pltpu.make_async_copy(src, dst, sems.at[i])
        for i, (src, dst) in enumerate(
            (
                (ins[1], layers),
                (ins[2].at[0], ids_all),
                (ins[3], power),
                (ins[4], neigh),
                (ins[5], coup),
            )
        )
    ]
    large = [
        pltpu.make_async_copy(
            ins[0].at[0, :, :, :, pl.ds(t * WIDE, WIDE)],
            channel.at[:, :, :, pl.ds(t * WIDE, WIDE)],
            sems.at[5 + t],
        )
        for t in range(tiles)
    ]
    for copy in small + large:
        copy.start()
    for copy in small:
        copy.wait()

    rooted = jnp.sqrt(power[...])
    sums = []
    for t in range(tiles):
        spot = pl.ds(t * WIDE, WIDE)
        granted = layers[:, spot]
        total = jnp.zeros((ROWS, WIDE), jnp.float32)
        for h in range(order // ROWS):
            ids = ids_all[pl.ds(h * ROWS, ROWS), spot]
            picked = jnp.zeros((ROWS, WIDE), jnp.float32)
            for u in range(users // WIDE):
                table = jnp.broadcast_to(rooted[:, u * WIDE : (u + 1) * WIDE], (ROWS, WIDE))
                found = jnp.take_along_axis(table, ids % WIDE, axis=1, mode="promise_in_bounds")
                picked = jnp.where(ids // WIDE == u, found, picked)
            amp = jnp.where(row_iota() + h * ROWS < granted, picked, 0.0)
            amp_all[t, pl.ds(h * ROWS, ROWS), :] = amp
            total = total + amp * amp
        sums.append(jnp.sum(total, axis=0, keepdims=True) / order)
    lane = lax.axis_index("lane")
    start = mirrored(lane, lanes) * chunk
    mine = jnp.broadcast_to(sums[0], (ROWS, WIDE))
    for t in range(1, tiles):
        mine = jnp.where(start // WIDE == t, jnp.broadcast_to(sums[t], (ROWS, WIDE)), mine)
    mine = pltpu.roll(mine, lax.rem(WIDE - lax.rem(start, WIDE), WIDE), 1)
    both = jnp.where(lane_iota() < HALF, mine, pltpu.roll(mine, HALF, 1))
    own[...] = jnp.broadcast_to(both[0:1][None], own.shape)
    cell = lax.axis_index("cell")
    mix[...] = jnp.zeros(mix.shape, jnp.float32)
    for k in range(neigh.shape[1]):
        spot = neigh[cell, k]
        mix[spot] = mix[spot] + coup[cell, k]
    low = lane_iota() < HALF
    rows = row_iota()
    for t in range(tiles):
        spot = pl.ds(t * WIDE, WIDE)
        granted = layers[:, spot]
        inside = [rows + h * ROWS < granted for h in range(2)]
        large[t].wait()
        inverse, root = [], []
        for h in range(2):
            part = pl.ds(h * ROWS, ROWS)
            total = jnp.zeros((ROWS, WIDE), jnp.float32)
            for a in range(antennas):
                re, im = channel[a, 0, part, spot], channel[a, 1, part, spot]
                total = total + (re * re + im * im)
            total = jnp.where(inside[h], total, 0.0)
            inverse.append(jnp.where(total > 0.0, lax.rsqrt(total), 0.0))
            root.append(total * inverse[h])
            inverses[part, :] = inverse[h] * FULL
        chunks = range(t * WIDE // chunk, (t + 1) * WIDE // chunk)

        def packed(top, bottom, z):
            off = z * chunk - t * WIDE
            return jnp.where(low, turn(top, -off), turn(bottom, HALF - off))

        for z in chunks:
            pieces[lane ^ mirrored(z, lanes), pl.ds(order * ROWS, order), :] = split(
                packed(root[0], root[1], z), ROOT_UNIT
            )
        for base in range(0, ROWS, 2):
            tops = (base, base + 1)
            acc = {}

            def add(key, value):
                acc[key] = value if key not in acc else acc[key] + value

            for a in range(antennas):
                re = [channel[a, 0, pl.ds(h * ROWS, ROWS), spot] for h in range(2)]
                im = [channel[a, 1, pl.ds(h * ROWS, ROWS), spot] for h in range(2)]
                for l in tops:
                    lre = channel[a, 0, pl.ds(l, 1), spot]
                    lim = channel[a, 1, pl.ds(l, 1), spot]
                    add((l, "re", 0), lre * re[0] + lim * im[0])
                    add((l, "re", 1), lre * re[1] + lim * im[1])
                    add((l, "im", 0), lim * re[0] - lre * im[0])
                    g = l + ROWS
                    gre = channel[a, 0, pl.ds(g, 1), spot]
                    gim = channel[a, 1, pl.ds(g, 1), spot]
                    add((g, "re", 1), gre * re[1] + gim * im[1])
                    add((g, "im", 0), gim * re[0] - gre * im[0])
                    add((g, "im", 1), gim * re[1] - gre * im[1])
            for l in tops:
                g = l + ROWS
                here = granted > l
                there = granted > g
                upper = [
                    jnp.where(rows >= l, acc[l, "re", 0], acc[l, "im", 0]),
                    acc[l, "re", 1],
                ]
                lower = [
                    acc[g, "im", 0],
                    jnp.where(rows >= l, acc[g, "re", 1], acc[g, "im", 1]),
                ]
                tops_out, bottoms_out = [], []
                for h in range(2):
                    top = jnp.where(jnp.logical_and(inside[h], here), upper[h], 0.0)
                    bottom = jnp.where(jnp.logical_and(inside[h], there), lower[h], 0.0)
                    tops_out.append(top * inverses[pl.ds(l, 1), :] * inverse[h])
                    bottoms_out.append(bottom * inverses[pl.ds(g, 1), :] * inverse[h])
                for z in chunks:
                    value = jnp.concatenate(
                        [packed(tops_out[h], bottoms_out[h], z) for h in range(2)], 0
                    )
                    pieces[lane ^ mirrored(z, lanes), pl.ds(l * order, order), :] = (
                        jnp.round(value).astype(jnp.int32).astype(jnp.int16)
                    )
    for s in range(lanes):
        outs[s][...] = pieces[s]


def solve_kernel(*refs, count):
    trans, mix = refs[:2]
    parts, out = refs[2 : 2 + count], refs[2 + count]
    pack, gram, e_a, e_b, s_a, s_b, d_re, d_im = refs[3 + count :]
    order = 2 * ROWS
    low = lane_iota() < HALF
    rows = row_iota()
    sign = jnp.where(low, -1.0, 1.0)

    def at(l, h):
        return pl.ds(l * order + h * ROWS, ROWS)

    def column(l, h):
        return pl.ds(h * ROWS * order + l, ROWS, stride=order)

    def row(ref, l, k):
        return ref[pl.ds(l * order + k, 1), :]

    others = [unpacked(part) for part in parts[1:]]
    for l in range(ROWS):
        for h in range(2):
            value = parts[0][at(l, h), :]
            for other in others:
                value = value + other[l, h]
            other = pltpu.roll(value, HALF, 1)
            pack[at(l, h), :] = jnp.where(low, value, other)
            pack[at(l + ROWS, h), :] = jnp.where(low, other, value)

    sigma = jnp.full((1, WIDE), NOISE_FLOOR, jnp.float32)
    for c in range(trans.shape[0]):
        sigma = sigma + mix[c] * trans[c]

    trace = order * sigma
    for l in range(order):
        trace = trace + row(pack, l, l)
    inverse = 1.0 / trace
    kept = 1.0 - sigma * inverse

    for l in range(order):
        for h in range(2):
            here = pack[at(l, h), :]
            across = pack[column(l, h), :]
            above = jnp.where(low, here, -across)
            below = jnp.where(low, across, here)
            if h * ROWS > l:
                value = above
            elif h * ROWS + ROWS - 1 < l:
                value = below
            else:
                value = jnp.where(rows + h * ROWS >= l, above, below)
                value = jnp.where(jnp.logical_and(rows + h * ROWS == l, ~low), 0.0, value)
            gram[at(l, h), :] = value
            error = -value * inverse
            total = error
            if h * ROWS <= l < h * ROWS + ROWS:
                spot = jnp.logical_and(rows + h * ROWS == l, low)
                error = error + jnp.where(spot, kept, 0.0)
                total = error + jnp.where(spot, 1.0, 0.0)
            e_a[at(l, h), :] = error
            s_a[at(l, h), :] = total

    def spread(ref):
        for l in range(order):
            for h in range(2):
                value = ref[at(l, h), :]
                other = pltpu.roll(value, HALF, 1)
                d_re[at(l, h), :] = jnp.where(low, value, other)
                d_im[at(l, h), :] = jnp.where(low, other, value)

    def products(jobs):
        for base in range(0, order, 2):
            halves = (0, 1) if base < ROWS else (1,)
            plain, crossed = {}, {}
            for l in (base, base + 1):
                for j, (_, _, start) in enumerate(jobs):
                    for h in halves:
                        if start is not None:
                            plain[l, j, h] = start[at(l, h), :]
            for k in range(order):
                right = {
                    (j, h): ref[at(k, h), :] for j, (ref, _, _) in enumerate(jobs) for h in halves
                }
                for l in (base, base + 1):
                    left_re = row(d_re, l, k)
                    left_im = row(d_im, l, k) if k != l else None
                    for (j, h), value in right.items():
                        key = (l, j, h)
                        term = left_re * value
                        plain[key] = plain[key] + term if key in plain else term
                        if left_im is not None:
                            term = left_im * value
                            crossed[key] = crossed[key] + term if key in crossed else term
            for (l, j, h), value in plain.items():
                cross = pltpu.roll(crossed[l, j, h], HALF, 1)
                jobs[j][1][at(l, h), :] = value + sign * cross
        for _, ref, _ in jobs:
            for l in range(ROWS, order):
                ref[at(l, 0), :] = -sign * ref[column(l, 0), :]

    def pair(error, squared, total, grown):
        for l in range(order):
            for h in range(2):
                value, other = error[at(l, h), :], total[at(l, h), :]
                value = value + pltpu.roll(value, HALF, 1)
                d_re[at(l, h), :] = value
                d_im[at(l, h), :] = jnp.where(low, value, other + pltpu.roll(other, HALF, 1))
        for base in range(0, order, 2):
            halves = (0, 1) if base < ROWS else (1,)
            acc = {}
            for k in range(order):
                right = [
                    (i, h, ref[at(k, h), :])
                    for i, ref in enumerate((error, total, d_im))
                    for h in halves
                ]
                for l in (base, base + 1):
                    left = row(error, l, k)
                    lefts = (left, left, row(d_re, l, k))
                    for i, h, value in right:
                        term = lefts[i] * value
                        acc[l, i, h] = acc[l, i, h] + term if k else term
            for l in (base, base + 1):
                for h in halves:
                    first, second, third = [acc[l, i, h] for i in range(3)]
                    other = pltpu.roll(first, HALF, 1)
                    squared[at(l, h), :] = jnp.where(
                        low, first - other, pltpu.roll(third, HALF, 1) - first - other
                    )
                    other = pltpu.roll(second, HALF, 1)
                    grown[at(l, h), :] = total[at(l, h), :] + jnp.where(
                        low, second - other, third - second - other
                    )
        for ref in (squared, grown):
            for l in range(ROWS, order):
                ref[at(l, 0), :] = -sign * ref[column(l, 0), :]

    spread(e_a)
    products([(e_a, e_b, None)])

    def two_steps(_, carry):
        pair(e_b, e_a, s_a, s_b)
        pair(e_a, e_b, s_b, s_a)
        return carry

    lax.fori_loop(0, (NS_STEPS - 2) // 2, two_steps, 0)
    spread(e_b)
    products([(s_a, s_b, s_a)])

    for l in range(order):
        for h in range(2):
            s_a[at(l, h), :] = s_b[at(l, h), :] * inverse
    spread(s_a)
    products([(gram, e_a, None)])

    logs, norms = [], []
    for h in range(2):
        value = s_a[at(0, h), :] * e_a[at(0, h), :]
        for m in range(1, order):
            value = value + s_a[at(m, h), :] * e_a[at(m, h), :]
        energy = value + pltpu.roll(value, HALF, 1)
        norms.append(lax.rsqrt(jnp.maximum(energy, 0.0) + NORM_EPS))
        logs.append(jnp.log2(norms[h]))
        d_re[pl.ds(h * ROWS, ROWS), :] = norms[h]
    peak = jnp.zeros((ROWS, WIDE), jnp.float32)
    diagonal = [peak, peak]
    for l in range(order):
        for h in range(2) if l < ROWS else (1,):
            value = s_a[at(l, h), :] * d_re[pl.ds(l, 1), :] * norms[h]
            if h * ROWS <= l < h * ROWS + ROWS:
                spot = rows + h * ROWS == l
                diagonal[h] = jnp.where(spot, value, diagonal[h])
                value = jnp.where(spot, 0.0, value)
            peak = jnp.maximum(peak, jnp.abs(value))
    peak = jnp.max(peak, axis=0, keepdims=True)
    peak = jnp.maximum(jnp.broadcast_to(peak, (ROWS, WIDE)), 1e-18)
    level = jnp.ceil(jnp.log2(jnp.maximum(peak, pltpu.roll(peak, HALF, 1))) * 128.0) + 1.0
    shrink = jnp.exp2(level * (-1.0 / 128.0))
    norms = [norm * shrink for norm in norms]
    for l in range(ROWS):
        values = []
        for h in range(2):
            first = s_a[at(l, h), :]
            second = s_a[at(l + ROWS, h), :]
            where = rows + h * ROWS
            first = jnp.where(where >= l, first, pltpu.roll(first, HALF, 1))
            second = jnp.where(where >= l + ROWS, pltpu.roll(second, HALF, 1), second)
            value = jnp.where(
                low, first * d_re[pl.ds(l, 1), :], second * d_re[pl.ds(l + ROWS, 1), :]
            )
            value = jnp.round(value * norms[h] * FULL)
            here = jnp.logical_and(rows == l, low if h == 0 else ~low)
            values.append(jnp.where(here, level, value))
        out[pl.ds(l * order, order), :] = (
            jnp.concatenate(values, 0).astype(jnp.int32).astype(jnp.int16)
        )
    diagonal = [jnp.where(low, d, pltpu.roll(d, HALF, 1)) for d in diagonal]
    diagonal = [jnp.log2(jnp.maximum(d * shrink, 1e-30)) for d in diagonal]
    out[pl.ds(order * ROWS, order), :] = split(jnp.where(low, *diagonal), LOG_UNIT)
    out[pl.ds(order * ROWS + order, order), :] = split(jnp.where(low, *logs), LOG_UNIT)


def arrange_kernel(
    far_ref,
    channel_ref,
    own_ref,
    other_ref,
    sym_ref,
    both_ref,
    turned_ref,
    sum_ref,
    symbols_ref,
    channel,
    sems,
    flat,
    stacked,
    moved,
    stage,
):
    copies = [
        pltpu.make_async_copy(far_ref, symbols_ref, sems.at[0]),
        pltpu.make_async_copy(channel_ref, channel, sems.at[1]),
    ]
    for copy in copies:
        copy.start()
    copies[0].wait()
    _, layers, parts, syms, subcarriers = symbols_ref.shape
    tiles, sub, height, _ = sym_ref.shape
    few = 32
    span = sub * few
    quads = WIDE // few
    lanes = lane_iota()
    for l in range(layers):
        for r in range(parts):
            flat[pl.ds((l * parts + r) * syms, syms), :] = symbols_ref[0, l, r].astype(jnp.float32)
    for i in range(tiles * quads):
        stacked[pl.ds(i * height, height), :] = flat[:, pl.ds(i * span, span)].astype(jnp.bfloat16)
    source = lax.broadcasted_iota(jnp.int32, (span, span), 0)
    target = lax.broadcasted_iota(jnp.int32, (span, span), 1)
    table = jnp.where(source == target % few * sub + target // few, 1.0, 0.0).astype(jnp.bfloat16)
    moved[...] = jnp.dot(stacked[...], table, preferred_element_type=jnp.float32)
    for t in range(tiles):
        for k in range(sub):
            for g in range(height // ROWS):
                value = None
                for b in range(quads):
                    rows = pl.ds((t * quads + b) * height + g * ROWS, ROWS)
                    piece = moved[rows, pl.ds(k // quads * WIDE, WIDE)]
                    piece = turn(piece, (b - k % quads) * few)
                    value = piece if b == 0 else jnp.where(lanes >= b * few, piece, value)
                sym_ref[t, k, pl.ds(g * ROWS, ROWS), :] = value
                both_ref[t, k, pl.ds(g * ROWS, ROWS), :] = value + pltpu.roll(
                    value, ROWS - syms, 0
                )
    copies[1].wait()
    antennas = channel.shape[1]
    for t in range(tiles):
        for a in range(antennas):
            for r in range(2):
                for h in range(layers // ROWS):
                    stage[t, pl.ds((a * 2 + r) * layers + h * ROWS, ROWS), :] = channel[
                        0, a, r, pl.ds(h * ROWS, ROWS), pl.ds(t * WIDE, WIDE)
                    ]
        for r in range(2):
            for m in range(layers):
                for h in range(antennas // ROWS):
                    first = h * ROWS * 2 * layers + r * layers + m
                    turned_ref[t, r, m, pl.ds(h * ROWS, ROWS), :] = stage[
                        t, pl.ds(first, ROWS, stride=2 * layers), :
                    ]
    own, other = unpacked(own_ref), unpacked(other_ref)
    for (l, h), value in own.items():
        sum_ref[pl.ds((l * 2 + h) * ROWS, ROWS), :] = value + other[l, h]


def transmit_kernel(*refs, which, last, lanes_count, chunk):
    per_tile = WIDE // chunk
    ins, rest = refs[:per_tile], refs[per_tile:]
    amp, chan, sym, sums, table_ref, twist = rest[:6]
    before = rest[6] if which else None
    out_ref = out = rest[6 + which]
    packs, pack, whole, norm, scale, scaled, weight, grid, table, spec_a, spec_b, sems = rest[
        7 + which : 19 + which
    ]
    if last:
        out, out_sems = rest[19 + which :]
    tiles, _, order, antennas, _ = chan.shape
    per_block, syms = sym.shape[1], sym.shape[2] // (2 * order)
    groups = antennas // ROWS
    lanes = lane_iota()
    lane = mirrored(lax.axis_index("lane"), lanes_count)
    tile = (lane // per_tile) ^ which
    halves = [
        pltpu.make_async_copy(
            table_ref.at[tile], table.at[:, pl.ds(h * 2 * WIDE, 2 * WIDE), :], sems.at[h]
        )
        for h in range(2)
    ]
    for copy in halves:
        copy.start()

    for s, ref in enumerate(ins):
        packs[lane % per_tile ^ s] = ref[...]

    def merged(values):
        first, second = values[0], pltpu.roll(values[0], HALF, 1)
        for z in range(1, per_tile):
            off = z * chunk
            first = jnp.where(lanes >= off, turn(values[z], off), first)
            second = jnp.where(lanes >= off, turn(values[z], off - HALF), second)
        return first, second

    for l in range(ROWS):
        held = [
            packs[z, pl.ds(l * order, order), :].astype(jnp.int32).astype(jnp.float32)
            for z in range(per_tile)
        ]
        for h in range(2):
            both = merged([value[h * ROWS : (h + 1) * ROWS] for value in held])
            for i, value in enumerate(both):
                pack[pl.ds((l + i * ROWS) * order + h * ROWS, ROWS), :] = value
    grow = jnp.exp2(pack[pl.ds(0, 1), :] * (1.0 / 128.0)) * (1.0 / FULL)
    tails = [
        merged(
            [
                joined(
                    packs[z, pl.ds(order * ROWS + i * order, order), :].astype(jnp.int32), LOG_UNIT
                )
                for z in range(per_tile)
            ]
        )
        for i in range(2)
    ]
    for h in range(2):
        spot = pl.ds(h * ROWS, ROWS)
        whole[spot, :] = jnp.exp2(tails[0][h]) * FULL
        norm[spot, :] = jnp.exp2(-tails[1][h])
        scale[spot, :] = amp[tile, spot, :] * grow
    for m in range(order):
        for g in range(groups):
            spot = pl.ds(g * ROWS, ROWS)
            re, im = [chan[tile, r, m, spot, :] * norm[pl.ds(m, 1), :] for r in range(2)]
            scaled[0, m, spot, :] = re
            scaled[1, m, spot, :] = im
            scaled[2, m, spot, :] = re - im

    def row(l, m):
        return pack[pl.ds(l * order + m, 1), :]

    for base in range(0, order, 4):
        acc = {}

        def add(key, value):
            acc[key] = value if key not in acc else acc[key] + value

        for m in range(order):
            here = [
                [scaled[r, m, pl.ds(g * ROWS, ROWS), :] for g in range(groups)] for r in range(3)
            ]
            for l in range(base, base + 4):
                if l == m:
                    inv = whole[pl.ds(l, 1), :]
                    for g in range(groups):
                        add((l, 0, g), here[0][g] * inv)
                        add((l, 2, g), here[2][g] * inv)
                    continue
                inv_re, inv_im = row(min(l, m), max(l, m)), row(max(l, m), min(l, m))
                if l > m:
                    inv_im = -inv_im
                total = inv_re + inv_im
                for g in range(groups):
                    add((l, 0, g), here[0][g] * inv_re)
                    add((l, 1, g), here[1][g] * inv_im)
                    add((l, 2, g), here[2][g] * total)
        for l in range(base, base + 4):
            for g in range(groups):
                first, second, third = [acc[l, i, g] for i in range(3)]
                grown = scale[pl.ds(l, 1), :]
                spot = pl.ds(g * ROWS, ROWS)
                re = ((first + second) * grown).astype(jnp.bfloat16).astype(jnp.float32)
                im = ((third - first + second) * grown).astype(jnp.bfloat16).astype(jnp.float32)
                weight[0, l, spot, :] = re
                weight[1, l, spot, :] = im
                weight[2, l, spot, :] = re + im

    def precode(k, carry):
        acc = {}
        for l in range(order):
            held = [
                [weight[i, l, pl.ds(g * ROWS, ROWS), :] for g in range(groups)] for i in range(3)
            ]
            for s in range(syms):
                parts = (
                    sym[tile, k, pl.ds(l * 2 * syms + s, 1), :],
                    sym[tile, k, pl.ds((l * 2 + 1) * syms + s, 1), :],
                    sums[tile, k, pl.ds(l * 2 * syms + s, 1), :],
                )
                for i in range(3):
                    for g in range(groups):
                        term = held[i][g] * parts[i]
                        acc[s, g, i] = term if l == 0 else acc[s, g, i] + term
        for r in range(2):
            values = []
            for s in range(syms):
                for g in range(groups):
                    first, second, third = [acc[s, g, i] for i in range(3)]
                    values.append(first - second if r == 0 else third - first - second)
            exact = jnp.concatenate(values, axis=0)
            high = exact.astype(jnp.bfloat16)
            grid[k, :, pl.ds(r * WIDE, WIDE)] = high
            grid[k, :, pl.ds((2 + r) * WIDE, WIDE)] = (exact - high.astype(jnp.float32)).astype(
                jnp.bfloat16
            )
        return carry

    lax.fori_loop(0, per_block, precode, 0)

    height = syms * antennas
    count = NFFT // WIDE // 4
    for copy in halves:
        copy.wait()
    left = grid[...].reshape(per_block * height, 4 * WIDE)
    specs = (spec_a, spec_b)

    def product(n):
        specs[n % 2][...] = jnp.dot(left, table[n], preferred_element_type=jnp.float32)

    def combine(n):
        spec = specs[n % 2]
        for g in range(height // ROWS):
            part = [None] * 4
            for k in range(per_block):
                rows = pl.ds(k * height + g * ROWS, ROWS)
                re = spec[rows, pl.ds(0, WIDE)]
                im = spec[rows, pl.ds(WIDE, WIDE)]
                if k > 0:
                    cos = twist[n, pl.ds(2 * k, 1), :]
                    sin = twist[n, pl.ds(2 * k + 1, 1), :]
                    re, im = re * cos - im * sin, re * sin + im * cos
                old = part[k % 4]
                part[k % 4] = (re, im) if old is None else (old[0] + re, old[1] + im)
            (r0, i0), (r1, i1), (r2, i2), (r3, i3) = part
            even_re, even_im, odd_re, odd_im = r0 + r2, i0 + i2, r1 + r3, i1 + i3
            gap_re, gap_im, far_re, far_im = r0 - r2, i0 - i2, r1 - r3, i1 - i3
            outs = (
                (even_re + odd_re, even_im + odd_im),
                (gap_re - far_im, gap_im + far_re),
                (even_re - odd_re, even_im - odd_im),
                (gap_re + far_im, gap_im - far_re),
            )
            s, first = g // groups, g % groups * ROWS
            for q, pair in enumerate(outs):
                for r in range(2):
                    value = pair[r]
                    spot = pl.ds(g * ROWS, ROWS)
                    if which:
                        value = value + before[n, q, r, spot, :]
                    if last:
                        start = (first * 2 + r) * syms + s
                        out[n, q, pl.ds(start, ROWS, stride=2 * syms), :] = value
                    else:
                        out[n, q, r, spot, :] = value

    done = []
    product(0)
    for n in range(count):
        if n + 1 < count:
            product(n + 1)
        combine(n)
        if not last:
            continue
        for q in range(4):
            copy = pltpu.make_async_copy(
                out.at[n, q].reshape(antennas, 2, syms, WIDE),
                out_ref.at[:, :, q * count + n],
                out_sems.at[n, q],
            )
            copy.start()
            done.append(copy)
    for copy in done:
        copy.wait()


def transform_tables(blocks, subcarriers):
    sub = subcarriers // blocks
    tiles = blocks // WIDE
    quarter = NFFT // 4
    p = np.arange(blocks)[:, None]
    n = np.arange(quarter)[None, :]
    angle = 2.0 * np.pi / NFFT * ((sub * p - subcarriers // 2) * n % NFFT)
    cos = np.cos(angle) / math.sqrt(NFFT)
    sin = np.sin(angle) / math.sqrt(NFFT)
    count = quarter // WIDE
    table = np.stack([np.stack([cos, sin]), np.stack([-sin, cos])])
    table = table.reshape(2, 2, tiles, WIDE, count, WIDE).transpose(2, 4, 0, 3, 1, 5)
    table = table.reshape(tiles, count, 2 * WIDE, 2 * WIDE).astype(jnp.bfloat16)
    turns = 2.0 * np.pi / NFFT * (np.arange(sub)[:, None] * n)
    twist = np.stack([np.cos(turns), np.sin(turns)], 1).astype(np.float32)
    twist = twist.reshape(2 * sub, count, WIDE).transpose(1, 0, 2)
    return table, np.ascontiguousarray(twist)


def far(value):
    return pltpu.with_memory_space_constraint(value, pltpu.HBM)


def near(value):
    return pltpu.with_memory_space_constraint(value, pltpu.VMEM)


def swap(pieces):
    lanes = lax.axis_size("lane")
    return [pieces[0]] + [
        lax.ppermute(pieces[s], "lane", [(j, j ^ s) for j in range(lanes)]) for s in range(1, lanes)
    ]


def per_device(channel, symbols, layers, user_ids, user_power, neighbours, coupling):
    lanes = lax.axis_size("lane")
    cells = lax.axis_size("cell")
    _, antennas, _, order, blocks = channel.shape
    syms, subcarriers = symbols.shape[3:]
    sub = subcarriers // blocks
    chunk = blocks // lanes
    tiles = blocks // WIDE
    f32, bf16 = jnp.float32, jnp.bfloat16
    shape = jax.ShapeDtypeStruct
    table, twist = transform_tables(blocks, subcarriers)
    table, twist = jnp.asarray(table), jnp.asarray(twist)
    dma = pltpu.SemaphoreType.DMA

    amp, own, mix, *pieces = pl.pallas_call(
        functools.partial(gram_kernel, lanes=lanes, chunk=chunk),
        out_shape=[pltpu.VMEM((tiles, order, WIDE), f32)]
        + [pltpu.VMEM((cells, 1, WIDE), f32)] * 2
        + [pltpu.VMEM((order * ROWS + order, WIDE), jnp.int16)] * lanes,
        in_specs=[HBM] * 6,
        out_specs=[VMEM] * (3 + lanes),
        scratch_shapes=[
            pltpu.VMEM((antennas, 2, order, blocks), f32),
            pltpu.VMEM((1, blocks), jnp.int32),
            pltpu.VMEM((order, blocks), jnp.int32),
            pltpu.VMEM(user_power.shape, f32),
            pltpu.SMEM(neighbours.shape, jnp.int32),
            pltpu.SMEM(coupling.shape, f32),
            pltpu.VMEM((lanes, order * ROWS + order, WIDE), jnp.int16),
            pltpu.VMEM((order, WIDE), f32),
            dma((5 + tiles,)),
        ],
        compiler_params=params(16),
        name="gram",
    )(*map(far, (channel, layers, user_ids, user_power, neighbours, coupling)))
    parts = swap(pieces)
    transmit = lax.all_to_all(own, "cell", 0, 0, tiled=True)

    sym, both, turned, pair = pl.pallas_call(
        arrange_kernel,
        out_shape=(
            pltpu.VMEM((tiles, sub, order * 2 * syms, WIDE), f32),
            pltpu.VMEM((tiles, sub, order * 2 * syms, WIDE), f32),
            pltpu.VMEM((tiles, 2, order, antennas, WIDE), f32),
            pltpu.VMEM((order * ROWS, WIDE), f32),
        ),
        in_specs=[HBM, HBM, VMEM, VMEM],
        out_specs=(VMEM,) * 4,
        scratch_shapes=[
            pltpu.VMEM(symbols.shape, bf16),
            pltpu.VMEM(channel.shape, f32),
            dma((2,)),
            pltpu.VMEM((order * 2 * syms, subcarriers), f32),
            pltpu.VMEM((subcarriers // (sub * 32) * order * 2 * syms, sub * 32), bf16),
            pltpu.VMEM((subcarriers // (sub * 32) * order * 2 * syms, sub * 32), f32),
            pltpu.VMEM((tiles, antennas * 2 * order, WIDE), f32),
        ],
        compiler_params=params(16),
        cost_estimate=pl.CostEstimate(flops=10**9, bytes_accessed=8 * 10**6, transcendentals=0),
        name="arrange",
    )(far(symbols), far(channel), near(parts[0]), near(parts[lanes - 1]))
    parts = [pair] + parts[1 : lanes - 1]

    packed = pl.pallas_call(
        functools.partial(solve_kernel, count=lanes - 1),
        out_shape=pltpu.VMEM((order * ROWS + 2 * order, WIDE), jnp.int16),
        in_specs=[VMEM] * (1 + lanes),
        out_specs=VMEM,
        scratch_shapes=[pltpu.VMEM((order * order, WIDE), f32)] * 8,
        compiler_params=params(16),
        name="solve",
    )(near(transmit), near(mix), *map(near, parts))
    packs = swap([packed] * lanes)
    packs = [packs[mirrored(i, lanes)] for i in range(lanes)]

    per_tile = WIDE // chunk
    height = syms * antennas
    count = NFFT // WIDE // 4
    out = ()
    for which in range(tiles):
        last = which == tiles - 1
        result = (count, 4, 2, height, WIDE)
        final = (antennas, 2, NFFT // WIDE, syms, WIDE)
        out = pl.pallas_call(
            functools.partial(
                transmit_kernel, which=which, last=last, lanes_count=lanes, chunk=chunk
            ),
            out_shape=[shape(final, f32) if last else pltpu.VMEM(result, f32)],
            in_specs=[VMEM] * (per_tile + 4) + [HBM, VMEM] + [VMEM] * which,
            out_specs=[HBM if last else VMEM],
            scratch_shapes=[
                pltpu.VMEM((per_tile, order * ROWS + 2 * order, WIDE), jnp.int16),
                pltpu.VMEM((order * order, WIDE), f32),
                pltpu.VMEM((order, WIDE), f32),
                pltpu.VMEM((order, WIDE), f32),
                pltpu.VMEM((order, WIDE), f32),
                pltpu.VMEM((3, order, antennas, WIDE), f32),
                pltpu.VMEM((3, order, antennas, WIDE), f32),
                pltpu.VMEM((sub, height, 4 * WIDE), bf16),
                pltpu.VMEM((count, 4 * WIDE, 2 * WIDE), bf16),
                pltpu.VMEM((sub * height, 2 * WIDE), f32),
                pltpu.VMEM((sub * height, 2 * WIDE), f32),
                dma((2,)),
            ]
            + [pltpu.VMEM((count, 4, 2 * height, WIDE), f32), dma((count, 4))] * last,
            compiler_params=params(16),
            cost_estimate=pl.CostEstimate(
                flops=10**9, bytes_accessed=4 * 10**6, transcendentals=0
            ),
            name="transmit",
        )(
            *map(near, packs[which * per_tile : (which + 1) * per_tile]),
            near(amp),
            near(turned),
            near(sym),
            near(both),
            far(table),
            near(twist),
            *map(near, out),
        )
    out = out[0].transpose(0, 1, 3, 2, 4)
    return out.reshape(1, antennas, 2, syms, NFFT)


def solution(mesh):
    in_specs = (
        P("cell", "lane", None, None, None),
        P("cell", None, None, None, None),
        P("cell", None),
        P("cell", None, None),
        P("cell", None),
        P(),
        P(),
    )
    out_specs = P("cell", "lane", None, None, None)
    return jax.shard_map(
        per_device, mesh=mesh, in_specs=in_specs, out_specs=out_specs, check_vma=False
    )
```

```python
import functools
import math

import jax
import jax.numpy as jnp
import numpy as np
from jax import lax
from jax.experimental import pallas as pl
from jax.experimental.pallas import tpu as pltpu
from jax.sharding import PartitionSpec as P

NFFT = 4096
NS_STEPS = 6
NORM_EPS = 1e-06
NOISE_FLOOR = 0.05
WIDE = 128
HALF = WIDE // 2
ROWS = 8
FULL = 32760.0
OFFSET = 32768
ROOT_UNIT = 2.0**24
LOG_UNIT = 2.0**23

VMEM = pl.BlockSpec(memory_space=pltpu.VMEM)
HBM = pl.BlockSpec(memory_space=pltpu.HBM)


def lane_iota():
    return lax.broadcasted_iota(jnp.int32, (ROWS, WIDE), 1)


def row_iota():
    return lax.broadcasted_iota(jnp.int32, (ROWS, WIDE), 0)


def turn(value, shift):
    shift = shift % WIDE
    return value if shift == 0 else pltpu.roll(value, shift, 1)


def split(value, unit):
    whole = jnp.round(value * unit).astype(jnp.int32)
    high = whole >> 16
    return jnp.concatenate([high, whole - (high << 16) - OFFSET], 0).astype(jnp.int16)


def joined(halves, unit):
    high = halves[:ROWS].astype(jnp.float32) * (65536.0 / unit)
    return high + (halves[ROWS:] + OFFSET).astype(jnp.float32) * (1.0 / unit)


def unpacked(piece):
    order = 2 * ROWS
    low, rows = lane_iota() < HALF, row_iota()
    root = joined(piece[pl.ds(order * ROWS, order), :].astype(jnp.int32), ROOT_UNIT)
    other = pltpu.roll(root, HALF, 1)
    both = (jnp.where(low, root, other), jnp.where(low, other, root))
    values = {}
    for l in range(ROWS):
        held = piece[pl.ds(l * order, order), :].astype(jnp.int32).astype(jnp.float32)
        for h in range(2):
            whole = jnp.logical_and(rows == l, low if h == 0 else ~low)
            part = jnp.where(whole, 1.0, held[h * ROWS : (h + 1) * ROWS] * (1.0 / FULL))
            values[l, h] = root[l : l + 1] * both[h] * part
    return values


def params(mib):
    return pltpu.CompilerParams(vmem_limit_bytes=mib * 1024 * 1024)


def gram_kernel(*refs, lanes, chunk):
    ins, outs = refs[:6], refs[9 : 9 + lanes]
    amp_all, own, mix = refs[6:9]
    channel, layers, ids_all, power, neigh, coup, pieces, inverses, sems = refs[9 + lanes :]
    antennas, _, order, blocks = channel.shape
    users = power.shape[1]
    tiles = blocks // WIDE
    small = [
        pltpu.make_async_copy(src, dst, sems.at[i])
        for i, (src, dst) in enumerate(
            (
                (ins[1], layers),
                (ins[2].at[0], ids_all),
                (ins[3], power),
                (ins[4], neigh),
                (ins[5], coup),
            )
        )
    ]
    large = [
        pltpu.make_async_copy(
            ins[0].at[0, :, :, :, pl.ds(t * WIDE, WIDE)],
            channel.at[:, :, :, pl.ds(t * WIDE, WIDE)],
            sems.at[5 + t],
        )
        for t in range(tiles)
    ]
    for copy in small + large:
        copy.start()
    for copy in small:
        copy.wait()

    rooted = jnp.sqrt(power[...])
    sums = []
    for t in range(tiles):
        spot = pl.ds(t * WIDE, WIDE)
        granted = layers[:, spot]
        total = jnp.zeros((ROWS, WIDE), jnp.float32)
        for h in range(order // ROWS):
            ids = ids_all[pl.ds(h * ROWS, ROWS), spot]
            picked = jnp.zeros((ROWS, WIDE), jnp.float32)
            for u in range(users // WIDE):
                table = jnp.broadcast_to(rooted[:, u * WIDE : (u + 1) * WIDE], (ROWS, WIDE))
                found = jnp.take_along_axis(table, ids % WIDE, axis=1, mode="promise_in_bounds")
                picked = jnp.where(ids // WIDE == u, found, picked)
            amp = jnp.where(row_iota() + h * ROWS < granted, picked, 0.0)
            amp_all[t, pl.ds(h * ROWS, ROWS), :] = amp
            total = total + amp * amp
        sums.append(jnp.sum(total, axis=0, keepdims=True) / order)
    lane = lax.axis_index("lane")
    start = lane * chunk
    mine = jnp.broadcast_to(sums[0], (ROWS, WIDE))
    for t in range(1, tiles):
        mine = jnp.where(start // WIDE == t, jnp.broadcast_to(sums[t], (ROWS, WIDE)), mine)
    mine = pltpu.roll(mine, lax.rem(WIDE - lax.rem(start, WIDE), WIDE), 1)
    both = jnp.where(lane_iota() < HALF, mine, pltpu.roll(mine, HALF, 1))
    own[...] = jnp.broadcast_to(both[0:1][None], own.shape)
    cell = lax.axis_index("cell")
    mix[...] = jnp.zeros(mix.shape, jnp.float32)
    for k in range(neigh.shape[1]):
        spot = neigh[cell, k]
        mix[spot] = mix[spot] + coup[cell, k]
    low = lane_iota() < HALF
    rows = row_iota()
    for t in range(tiles):
        spot = pl.ds(t * WIDE, WIDE)
        granted = layers[:, spot]
        inside = [rows + h * ROWS < granted for h in range(2)]
        large[t].wait()
        inverse, root = [], []
        for h in range(2):
            part = pl.ds(h * ROWS, ROWS)
            total = jnp.zeros((ROWS, WIDE), jnp.float32)
            for a in range(antennas):
                re, im = channel[a, 0, part, spot], channel[a, 1, part, spot]
                total = total + (re * re + im * im)
            total = jnp.where(inside[h], total, 0.0)
            inverse.append(jnp.where(total > 0.0, lax.rsqrt(total), 0.0))
            root.append(total * inverse[h])
            inverses[part, :] = inverse[h] * FULL
        chunks = range(t * WIDE // chunk, (t + 1) * WIDE // chunk)

        def packed(top, bottom, z):
            off = z * chunk - t * WIDE
            return jnp.where(low, turn(top, -off), turn(bottom, HALF - off))

        for z in chunks:
            pieces[lane ^ z, pl.ds(order * ROWS, order), :] = split(
                packed(root[0], root[1], z), ROOT_UNIT
            )
        for base in range(0, ROWS, 2):
            tops = (base, base + 1)
            acc = {}

            def add(key, value):
                acc[key] = value if key not in acc else acc[key] + value

            for a in range(antennas):
                re = [channel[a, 0, pl.ds(h * ROWS, ROWS), spot] for h in range(2)]
                im = [channel[a, 1, pl.ds(h * ROWS, ROWS), spot] for h in range(2)]
                for l in tops:
                    lre = channel[a, 0, pl.ds(l, 1), spot]
                    lim = channel[a, 1, pl.ds(l, 1), spot]
                    add((l, "re", 0), lre * re[0] + lim * im[0])
                    add((l, "re", 1), lre * re[1] + lim * im[1])
                    add((l, "im", 0), lim * re[0] - lre * im[0])
                    g = l + ROWS
                    gre = channel[a, 0, pl.ds(g, 1), spot]
                    gim = channel[a, 1, pl.ds(g, 1), spot]
                    add((g, "re", 1), gre * re[1] + gim * im[1])
                    add((g, "im", 0), gim * re[0] - gre * im[0])
                    add((g, "im", 1), gim * re[1] - gre * im[1])
            for l in tops:
                g = l + ROWS
                here = granted > l
                there = granted > g
                upper = [
                    jnp.where(rows >= l, acc[l, "re", 0], acc[l, "im", 0]),
                    acc[l, "re", 1],
                ]
                lower = [
                    acc[g, "im", 0],
                    jnp.where(rows >= l, acc[g, "re", 1], acc[g, "im", 1]),
                ]
                tops_out, bottoms_out = [], []
                for h in range(2):
                    top = jnp.where(jnp.logical_and(inside[h], here), upper[h], 0.0)
                    bottom = jnp.where(jnp.logical_and(inside[h], there), lower[h], 0.0)
                    tops_out.append(top * inverses[pl.ds(l, 1), :] * inverse[h])
                    bottoms_out.append(bottom * inverses[pl.ds(g, 1), :] * inverse[h])
                for z in chunks:
                    value = jnp.concatenate(
                        [packed(tops_out[h], bottoms_out[h], z) for h in range(2)], 0
                    )
                    pieces[lane ^ z, pl.ds(l * order, order), :] = (
                        jnp.round(value).astype(jnp.int32).astype(jnp.int16)
                    )
    for s in range(lanes):
        outs[s][...] = pieces[s]


def solve_kernel(*refs, count):
    trans, mix = refs[:2]
    parts, out = refs[2 : 2 + count], refs[2 + count]
    pack, gram, e_a, e_b, s_a, s_b, d_re, d_im = refs[3 + count :]
    order = 2 * ROWS
    low = lane_iota() < HALF
    rows = row_iota()
    sign = jnp.where(low, -1.0, 1.0)

    def at(l, h):
        return pl.ds(l * order + h * ROWS, ROWS)

    def column(l, h):
        return pl.ds(h * ROWS * order + l, ROWS, stride=order)

    def row(ref, l, k):
        return ref[pl.ds(l * order + k, 1), :]

    others = [unpacked(part) for part in parts[1:]]
    for l in range(ROWS):
        for h in range(2):
            value = parts[0][at(l, h), :]
            for other in others:
                value = value + other[l, h]
            other = pltpu.roll(value, HALF, 1)
            pack[at(l, h), :] = jnp.where(low, value, other)
            pack[at(l + ROWS, h), :] = jnp.where(low, other, value)

    sigma = jnp.full((1, WIDE), NOISE_FLOOR, jnp.float32)
    for c in range(trans.shape[0]):
        sigma = sigma + mix[c] * trans[c]

    trace = order * sigma
    for l in range(order):
        trace = trace + row(pack, l, l)
    inverse = 1.0 / trace
    kept = 1.0 - sigma * inverse

    for l in range(order):
        for h in range(2):
            here = pack[at(l, h), :]
            across = pack[column(l, h), :]
            above = jnp.where(low, here, -across)
            below = jnp.where(low, across, here)
            if h * ROWS > l:
                value = above
            elif h * ROWS + ROWS - 1 < l:
                value = below
            else:
                value = jnp.where(rows + h * ROWS >= l, above, below)
                value = jnp.where(jnp.logical_and(rows + h * ROWS == l, ~low), 0.0, value)
            gram[at(l, h), :] = value
            error = -value * inverse
            total = error
            if h * ROWS <= l < h * ROWS + ROWS:
                spot = jnp.logical_and(rows + h * ROWS == l, low)
                error = error + jnp.where(spot, kept, 0.0)
                total = error + jnp.where(spot, 1.0, 0.0)
            e_a[at(l, h), :] = error
            s_a[at(l, h), :] = total

    def spread(ref):
        for l in range(order):
            for h in range(2):
                value = ref[at(l, h), :]
                other = pltpu.roll(value, HALF, 1)
                d_re[at(l, h), :] = jnp.where(low, value, other)
                d_im[at(l, h), :] = jnp.where(low, other, value)

    def products(jobs):
        for base in range(0, order, 2):
            halves = (0, 1) if base < ROWS else (1,)
            plain, crossed = {}, {}
            for l in (base, base + 1):
                for j, (_, _, start) in enumerate(jobs):
                    for h in halves:
                        if start is not None:
                            plain[l, j, h] = start[at(l, h), :]
            for k in range(order):
                right = {
                    (j, h): ref[at(k, h), :] for j, (ref, _, _) in enumerate(jobs) for h in halves
                }
                for l in (base, base + 1):
                    left_re = row(d_re, l, k)
                    left_im = row(d_im, l, k) if k != l else None
                    for (j, h), value in right.items():
                        key = (l, j, h)
                        term = left_re * value
                        plain[key] = plain[key] + term if key in plain else term
                        if left_im is not None:
                            term = left_im * value
                            crossed[key] = crossed[key] + term if key in crossed else term
            for (l, j, h), value in plain.items():
                cross = pltpu.roll(crossed[l, j, h], HALF, 1)
                jobs[j][1][at(l, h), :] = value + sign * cross
        for _, ref, _ in jobs:
            for l in range(ROWS, order):
                ref[at(l, 0), :] = -sign * ref[column(l, 0), :]

    def pair(error, squared, total, grown):
        for l in range(order):
            for h in range(2):
                value, other = error[at(l, h), :], total[at(l, h), :]
                value = value + pltpu.roll(value, HALF, 1)
                d_re[at(l, h), :] = value
                d_im[at(l, h), :] = jnp.where(low, value, other + pltpu.roll(other, HALF, 1))
        for base in range(0, order, 2):
            halves = (0, 1) if base < ROWS else (1,)
            acc = {}
            for k in range(order):
                right = [
                    (i, h, ref[at(k, h), :])
                    for i, ref in enumerate((error, total, d_im))
                    for h in halves
                ]
                for l in (base, base + 1):
                    left = row(error, l, k)
                    lefts = (left, left, row(d_re, l, k))
                    for i, h, value in right:
                        term = lefts[i] * value
                        acc[l, i, h] = acc[l, i, h] + term if k else term
            for l in (base, base + 1):
                for h in halves:
                    first, second, third = [acc[l, i, h] for i in range(3)]
                    other = pltpu.roll(first, HALF, 1)
                    squared[at(l, h), :] = jnp.where(
                        low, first - other, pltpu.roll(third, HALF, 1) - first - other
                    )
                    other = pltpu.roll(second, HALF, 1)
                    grown[at(l, h), :] = total[at(l, h), :] + jnp.where(
                        low, second - other, third - second - other
                    )
        for ref in (squared, grown):
            for l in range(ROWS, order):
                ref[at(l, 0), :] = -sign * ref[column(l, 0), :]

    spread(e_a)
    products([(e_a, e_b, None)])

    def two_steps(_, carry):
        pair(e_b, e_a, s_a, s_b)
        pair(e_a, e_b, s_b, s_a)
        return carry

    lax.fori_loop(0, (NS_STEPS - 2) // 2, two_steps, 0)
    spread(e_b)
    products([(s_a, s_b, s_a)])

    for l in range(order):
        for h in range(2):
            s_a[at(l, h), :] = s_b[at(l, h), :] * inverse
    spread(s_a)
    products([(gram, e_a, None)])

    logs, norms = [], []
    for h in range(2):
        value = s_a[at(0, h), :] * e_a[at(0, h), :]
        for m in range(1, order):
            value = value + s_a[at(m, h), :] * e_a[at(m, h), :]
        energy = value + pltpu.roll(value, HALF, 1)
        norms.append(lax.rsqrt(jnp.maximum(energy, 0.0) + NORM_EPS))
        logs.append(jnp.log2(norms[h]))
        d_re[pl.ds(h * ROWS, ROWS), :] = norms[h]
    peak = jnp.zeros((ROWS, WIDE), jnp.float32)
    diagonal = [peak, peak]
    for l in range(order):
        for h in range(2) if l < ROWS else (1,):
            value = s_a[at(l, h), :] * d_re[pl.ds(l, 1), :] * norms[h]
            if h * ROWS <= l < h * ROWS + ROWS:
                spot = rows + h * ROWS == l
                diagonal[h] = jnp.where(spot, value, diagonal[h])
                value = jnp.where(spot, 0.0, value)
            peak = jnp.maximum(peak, jnp.abs(value))
    peak = jnp.max(peak, axis=0, keepdims=True)
    peak = jnp.maximum(jnp.broadcast_to(peak, (ROWS, WIDE)), 1e-18)
    level = jnp.ceil(jnp.log2(jnp.maximum(peak, pltpu.roll(peak, HALF, 1))) * 128.0) + 1.0
    shrink = jnp.exp2(level * (-1.0 / 128.0))
    norms = [norm * shrink for norm in norms]
    for l in range(ROWS):
        values = []
        for h in range(2):
            first = s_a[at(l, h), :]
            second = s_a[at(l + ROWS, h), :]
            where = rows + h * ROWS
            first = jnp.where(where >= l, first, pltpu.roll(first, HALF, 1))
            second = jnp.where(where >= l + ROWS, pltpu.roll(second, HALF, 1), second)
            value = jnp.where(
                low, first * d_re[pl.ds(l, 1), :], second * d_re[pl.ds(l + ROWS, 1), :]
            )
            value = jnp.round(value * norms[h] * FULL)
            here = jnp.logical_and(rows == l, low if h == 0 else ~low)
            values.append(jnp.where(here, level, value))
        out[pl.ds(l * order, order), :] = (
            jnp.concatenate(values, 0).astype(jnp.int32).astype(jnp.int16)
        )
    diagonal = [jnp.where(low, d, pltpu.roll(d, HALF, 1)) for d in diagonal]
    diagonal = [jnp.log2(jnp.maximum(d * shrink, 1e-30)) for d in diagonal]
    out[pl.ds(order * ROWS, order), :] = split(jnp.where(low, *diagonal), LOG_UNIT)
    out[pl.ds(order * ROWS + order, order), :] = split(jnp.where(low, *logs), LOG_UNIT)


def arrange_kernel(
    far_ref,
    channel_ref,
    own_ref,
    other_ref,
    sym_ref,
    both_ref,
    turned_ref,
    sum_ref,
    symbols_ref,
    channel,
    sems,
    flat,
    stacked,
    moved,
    stage,
):
    copies = [
        pltpu.make_async_copy(far_ref, symbols_ref, sems.at[0]),
        pltpu.make_async_copy(channel_ref, channel, sems.at[1]),
    ]
    for copy in copies:
        copy.start()
    copies[0].wait()
    _, layers, parts, syms, subcarriers = symbols_ref.shape
    tiles, sub, height, _ = sym_ref.shape
    few = 32
    span = sub * few
    quads = WIDE // few
    lanes = lane_iota()
    for l in range(layers):
        for r in range(parts):
            flat[pl.ds((l * parts + r) * syms, syms), :] = symbols_ref[0, l, r].astype(jnp.float32)
    for i in range(tiles * quads):
        stacked[pl.ds(i * height, height), :] = flat[:, pl.ds(i * span, span)].astype(jnp.bfloat16)
    source = lax.broadcasted_iota(jnp.int32, (span, span), 0)
    target = lax.broadcasted_iota(jnp.int32, (span, span), 1)
    table = jnp.where(source == target % few * sub + target // few, 1.0, 0.0).astype(jnp.bfloat16)
    moved[...] = jnp.dot(stacked[...], table, preferred_element_type=jnp.float32)
    for t in range(tiles):
        for k in range(sub):
            for g in range(height // ROWS):
                value = None
                for b in range(quads):
                    rows = pl.ds((t * quads + b) * height + g * ROWS, ROWS)
                    piece = moved[rows, pl.ds(k // quads * WIDE, WIDE)]
                    piece = turn(piece, (b - k % quads) * few)
                    value = piece if b == 0 else jnp.where(lanes >= b * few, piece, value)
                sym_ref[t, k, pl.ds(g * ROWS, ROWS), :] = value
                both_ref[t, k, pl.ds(g * ROWS, ROWS), :] = value + pltpu.roll(
                    value, ROWS - syms, 0
                )
    copies[1].wait()
    antennas = channel.shape[1]
    for t in range(tiles):
        for a in range(antennas):
            for r in range(2):
                for h in range(layers // ROWS):
                    stage[t, pl.ds((a * 2 + r) * layers + h * ROWS, ROWS), :] = channel[
                        0, a, r, pl.ds(h * ROWS, ROWS), pl.ds(t * WIDE, WIDE)
                    ]
        for r in range(2):
            for m in range(layers):
                for h in range(antennas // ROWS):
                    first = h * ROWS * 2 * layers + r * layers + m
                    turned_ref[t, r, m, pl.ds(h * ROWS, ROWS), :] = stage[
                        t, pl.ds(first, ROWS, stride=2 * layers), :
                    ]
    own, other = unpacked(own_ref), unpacked(other_ref)
    for (l, h), value in own.items():
        sum_ref[pl.ds((l * 2 + h) * ROWS, ROWS), :] = value + other[l, h]


def transmit_kernel(*refs, which, last, chunk):
    per_tile = WIDE // chunk
    ins, rest = refs[:per_tile], refs[per_tile:]
    amp, chan, sym, sums, table_ref, twist = rest[:6]
    before = rest[6] if which else None
    out_ref = out = rest[6 + which]
    packs, pack, whole, norm, scale, scaled, weight, grid, table, spec_a, spec_b, sems = rest[
        7 + which : 19 + which
    ]
    if last:
        out, out_sems = rest[19 + which :]
    tiles, _, order, antennas, _ = chan.shape
    per_block, syms = sym.shape[1], sym.shape[2] // (2 * order)
    groups = antennas // ROWS
    lanes = lane_iota()
    lane = lax.axis_index("lane")
    tile = (lane // per_tile) ^ which
    halves = [
        pltpu.make_async_copy(
            table_ref.at[tile], table.at[:, pl.ds(h * 2 * WIDE, 2 * WIDE), :], sems.at[h]
        )
        for h in range(2)
    ]
    for copy in halves:
        copy.start()

    for s, ref in enumerate(ins):
        packs[lane % per_tile ^ s] = ref[...]

    def merged(values):
        first, second = values[0], pltpu.roll(values[0], HALF, 1)
        for z in range(1, per_tile):
            off = z * chunk
            first = jnp.where(lanes >= off, turn(values[z], off), first)
            second = jnp.where(lanes >= off, turn(values[z], off - HALF), second)
        return first, second

    for l in range(ROWS):
        held = [
            packs[z, pl.ds(l * order, order), :].astype(jnp.int32).astype(jnp.float32)
            for z in range(per_tile)
        ]
        for h in range(2):
            both = merged([value[h * ROWS : (h + 1) * ROWS] for value in held])
            for i, value in enumerate(both):
                pack[pl.ds((l + i * ROWS) * order + h * ROWS, ROWS), :] = value
    grow = jnp.exp2(pack[pl.ds(0, 1), :] * (1.0 / 128.0)) * (1.0 / FULL)
    tails = [
        merged(
            [
                joined(
                    packs[z, pl.ds(order * ROWS + i * order, order), :].astype(jnp.int32), LOG_UNIT
                )
                for z in range(per_tile)
            ]
        )
        for i in range(2)
    ]
    for h in range(2):
        spot = pl.ds(h * ROWS, ROWS)
        whole[spot, :] = jnp.exp2(tails[0][h]) * FULL
        norm[spot, :] = jnp.exp2(-tails[1][h])
        scale[spot, :] = amp[tile, spot, :] * grow
    for m in range(order):
        for g in range(groups):
            spot = pl.ds(g * ROWS, ROWS)
            re, im = [chan[tile, r, m, spot, :] * norm[pl.ds(m, 1), :] for r in range(2)]
            scaled[0, m, spot, :] = re
            scaled[1, m, spot, :] = im
            scaled[2, m, spot, :] = re - im

    def row(l, m):
        return pack[pl.ds(l * order + m, 1), :]

    for base in range(0, order, 4):
        acc = {}

        def add(key, value):
            acc[key] = value if key not in acc else acc[key] + value

        for m in range(order):
            here = [
                [scaled[r, m, pl.ds(g * ROWS, ROWS), :] for g in range(groups)] for r in range(3)
            ]
            for l in range(base, base + 4):
                if l == m:
                    inv = whole[pl.ds(l, 1), :]
                    for g in range(groups):
                        add((l, 0, g), here[0][g] * inv)
                        add((l, 2, g), here[2][g] * inv)
                    continue
                inv_re, inv_im = row(min(l, m), max(l, m)), row(max(l, m), min(l, m))
                if l > m:
                    inv_im = -inv_im
                total = inv_re + inv_im
                for g in range(groups):
                    add((l, 0, g), here[0][g] * inv_re)
                    add((l, 1, g), here[1][g] * inv_im)
                    add((l, 2, g), here[2][g] * total)
        for l in range(base, base + 4):
            for g in range(groups):
                first, second, third = [acc[l, i, g] for i in range(3)]
                grown = scale[pl.ds(l, 1), :]
                spot = pl.ds(g * ROWS, ROWS)
                re = ((first + second) * grown).astype(jnp.bfloat16).astype(jnp.float32)
                im = ((third - first + second) * grown).astype(jnp.bfloat16).astype(jnp.float32)
                weight[0, l, spot, :] = re
                weight[1, l, spot, :] = im
                weight[2, l, spot, :] = re + im

    def precode(k, carry):
        acc = {}
        for l in range(order):
            held = [
                [weight[i, l, pl.ds(g * ROWS, ROWS), :] for g in range(groups)] for i in range(3)
            ]
            for s in range(syms):
                parts = (
                    sym[tile, k, pl.ds(l * 2 * syms + s, 1), :],
                    sym[tile, k, pl.ds((l * 2 + 1) * syms + s, 1), :],
                    sums[tile, k, pl.ds(l * 2 * syms + s, 1), :],
                )
                for i in range(3):
                    for g in range(groups):
                        term = held[i][g] * parts[i]
                        acc[s, g, i] = term if l == 0 else acc[s, g, i] + term
        for r in range(2):
            values = []
            for s in range(syms):
                for g in range(groups):
                    first, second, third = [acc[s, g, i] for i in range(3)]
                    values.append(first - second if r == 0 else third - first - second)
            exact = jnp.concatenate(values, axis=0)
            high = exact.astype(jnp.bfloat16)
            grid[k, :, pl.ds(r * WIDE, WIDE)] = high
            grid[k, :, pl.ds((2 + r) * WIDE, WIDE)] = (exact - high.astype(jnp.float32)).astype(
                jnp.bfloat16
            )
        return carry

    lax.fori_loop(0, per_block, precode, 0)

    height = syms * antennas
    count = NFFT // WIDE // 4
    for copy in halves:
        copy.wait()
    left = grid[...].reshape(per_block * height, 4 * WIDE)
    specs = (spec_a, spec_b)

    def product(n):
        specs[n % 2][...] = jnp.dot(left, table[n], preferred_element_type=jnp.float32)

    def combine(n):
        spec = specs[n % 2]
        for g in range(height // ROWS):
            part = [None] * 4
            for k in range(per_block):
                rows = pl.ds(k * height + g * ROWS, ROWS)
                re = spec[rows, pl.ds(0, WIDE)]
                im = spec[rows, pl.ds(WIDE, WIDE)]
                if k > 0:
                    cos = twist[n, pl.ds(2 * k, 1), :]
                    sin = twist[n, pl.ds(2 * k + 1, 1), :]
                    re, im = re * cos - im * sin, re * sin + im * cos
                old = part[k % 4]
                part[k % 4] = (re, im) if old is None else (old[0] + re, old[1] + im)
            (r0, i0), (r1, i1), (r2, i2), (r3, i3) = part
            even_re, even_im, odd_re, odd_im = r0 + r2, i0 + i2, r1 + r3, i1 + i3
            gap_re, gap_im, far_re, far_im = r0 - r2, i0 - i2, r1 - r3, i1 - i3
            outs = (
                (even_re + odd_re, even_im + odd_im),
                (gap_re - far_im, gap_im + far_re),
                (even_re - odd_re, even_im - odd_im),
                (gap_re + far_im, gap_im - far_re),
            )
            s, first = g // groups, g % groups * ROWS
            for q, pair in enumerate(outs):
                for r in range(2):
                    value = pair[r]
                    spot = pl.ds(g * ROWS, ROWS)
                    if which:
                        value = value + before[n, q, r, spot, :]
                    if last:
                        start = (first * 2 + r) * syms + s
                        out[n, q, pl.ds(start, ROWS, stride=2 * syms), :] = value
                    else:
                        out[n, q, r, spot, :] = value

    done = []
    product(0)
    for n in range(count):
        if n + 1 < count:
            product(n + 1)
        combine(n)
        if not last:
            continue
        for q in range(4):
            copy = pltpu.make_async_copy(
                out.at[n, q].reshape(antennas, 2, syms, WIDE),
                out_ref.at[:, :, q * count + n],
                out_sems.at[n, q],
            )
            copy.start()
            done.append(copy)
    for copy in done:
        copy.wait()


def transform_tables(blocks, subcarriers):
    sub = subcarriers // blocks
    tiles = blocks // WIDE
    quarter = NFFT // 4
    p = np.arange(blocks)[:, None]
    n = np.arange(quarter)[None, :]
    angle = 2.0 * np.pi / NFFT * ((sub * p - subcarriers // 2) * n % NFFT)
    cos = np.cos(angle) / math.sqrt(NFFT)
    sin = np.sin(angle) / math.sqrt(NFFT)
    count = quarter // WIDE
    table = np.stack([np.stack([cos, sin]), np.stack([-sin, cos])])
    table = table.reshape(2, 2, tiles, WIDE, count, WIDE).transpose(2, 4, 0, 3, 1, 5)
    table = table.reshape(tiles, count, 2 * WIDE, 2 * WIDE).astype(jnp.bfloat16)
    turns = 2.0 * np.pi / NFFT * (np.arange(sub)[:, None] * n)
    twist = np.stack([np.cos(turns), np.sin(turns)], 1).astype(np.float32)
    twist = twist.reshape(2 * sub, count, WIDE).transpose(1, 0, 2)
    return table, np.ascontiguousarray(twist)


def far(value):
    return pltpu.with_memory_space_constraint(value, pltpu.HBM)


def near(value):
    return pltpu.with_memory_space_constraint(value, pltpu.VMEM)


def swap(pieces):
    lanes = lax.axis_size("lane")
    return [pieces[0]] + [
        lax.ppermute(pieces[s], "lane", [(j, j ^ s) for j in range(lanes)]) for s in range(1, lanes)
    ]


def per_device(channel, symbols, layers, user_ids, user_power, neighbours, coupling):
    lanes = lax.axis_size("lane")
    cells = lax.axis_size("cell")
    _, antennas, _, order, blocks = channel.shape
    syms, subcarriers = symbols.shape[3:]
    sub = subcarriers // blocks
    chunk = blocks // lanes
    tiles = blocks // WIDE
    f32, bf16 = jnp.float32, jnp.bfloat16
    shape = jax.ShapeDtypeStruct
    table, twist = transform_tables(blocks, subcarriers)
    table, twist = jnp.asarray(table), jnp.asarray(twist)
    dma = pltpu.SemaphoreType.DMA

    amp, own, mix, *pieces = pl.pallas_call(
        functools.partial(gram_kernel, lanes=lanes, chunk=chunk),
        out_shape=[pltpu.VMEM((tiles, order, WIDE), f32)]
        + [pltpu.VMEM((cells, 1, WIDE), f32)] * 2
        + [pltpu.VMEM((order * ROWS + order, WIDE), jnp.int16)] * lanes,
        in_specs=[HBM] * 6,
        out_specs=[VMEM] * (3 + lanes),
        scratch_shapes=[
            pltpu.VMEM((antennas, 2, order, blocks), f32),
            pltpu.VMEM((1, blocks), jnp.int32),
            pltpu.VMEM((order, blocks), jnp.int32),
            pltpu.VMEM(user_power.shape, f32),
            pltpu.SMEM(neighbours.shape, jnp.int32),
            pltpu.SMEM(coupling.shape, f32),
            pltpu.VMEM((lanes, order * ROWS + order, WIDE), jnp.int16),
            pltpu.VMEM((order, WIDE), f32),
            dma((5 + tiles,)),
        ],
        compiler_params=params(16),
        name="gram",
    )(*map(far, (channel, layers, user_ids, user_power, neighbours, coupling)))
    parts = swap(pieces)
    transmit = lax.all_to_all(own, "cell", 0, 0, tiled=True)

    sym, both, turned, pair = pl.pallas_call(
        arrange_kernel,
        out_shape=(
            pltpu.VMEM((tiles, sub, order * 2 * syms, WIDE), f32),
            pltpu.VMEM((tiles, sub, order * 2 * syms, WIDE), f32),
            pltpu.VMEM((tiles, 2, order, antennas, WIDE), f32),
            pltpu.VMEM((order * ROWS, WIDE), f32),
        ),
        in_specs=[HBM, HBM, VMEM, VMEM],
        out_specs=(VMEM,) * 4,
        scratch_shapes=[
            pltpu.VMEM(symbols.shape, bf16),
            pltpu.VMEM(channel.shape, f32),
            dma((2,)),
            pltpu.VMEM((order * 2 * syms, subcarriers), f32),
            pltpu.VMEM((subcarriers // (sub * 32) * order * 2 * syms, sub * 32), bf16),
            pltpu.VMEM((subcarriers // (sub * 32) * order * 2 * syms, sub * 32), f32),
            pltpu.VMEM((tiles, antennas * 2 * order, WIDE), f32),
        ],
        compiler_params=params(16),
        cost_estimate=pl.CostEstimate(flops=10**9, bytes_accessed=8 * 10**6, transcendentals=0),
        name="arrange",
    )(far(symbols), far(channel), near(parts[0]), near(parts[lanes - 1]))
    parts = [pair] + parts[1 : lanes - 1]

    packed = pl.pallas_call(
        functools.partial(solve_kernel, count=lanes - 1),
        out_shape=pltpu.VMEM((order * ROWS + 2 * order, WIDE), jnp.int16),
        in_specs=[VMEM] * (1 + lanes),
        out_specs=VMEM,
        scratch_shapes=[pltpu.VMEM((order * order, WIDE), f32)] * 8,
        compiler_params=params(16),
        name="solve",
    )(near(transmit), near(mix), *map(near, parts))
    packs = swap([packed] * lanes)

    per_tile = WIDE // chunk
    height = syms * antennas
    count = NFFT // WIDE // 4
    out = ()
    for which in range(tiles):
        last = which == tiles - 1
        result = (count, 4, 2, height, WIDE)
        final = (antennas, 2, NFFT // WIDE, syms, WIDE)
        out = pl.pallas_call(
            functools.partial(transmit_kernel, which=which, last=last, chunk=chunk),
            out_shape=[shape(final, f32) if last else pltpu.VMEM(result, f32)],
            in_specs=[VMEM] * (per_tile + 4) + [HBM, VMEM] + [VMEM] * which,
            out_specs=[HBM if last else VMEM],
            scratch_shapes=[
                pltpu.VMEM((per_tile, order * ROWS + 2 * order, WIDE), jnp.int16),
                pltpu.VMEM((order * order, WIDE), f32),
                pltpu.VMEM((order, WIDE), f32),
                pltpu.VMEM((order, WIDE), f32),
                pltpu.VMEM((order, WIDE), f32),
                pltpu.VMEM((3, order, antennas, WIDE), f32),
                pltpu.VMEM((3, order, antennas, WIDE), f32),
                pltpu.VMEM((sub, height, 4 * WIDE), bf16),
                pltpu.VMEM((count, 4 * WIDE, 2 * WIDE), bf16),
                pltpu.VMEM((sub * height, 2 * WIDE), f32),
                pltpu.VMEM((sub * height, 2 * WIDE), f32),
                dma((2,)),
            ]
            + [pltpu.VMEM((count, 4, 2 * height, WIDE), f32), dma((count, 4))] * last,
            compiler_params=params(16),
            cost_estimate=pl.CostEstimate(
                flops=10**9, bytes_accessed=4 * 10**6, transcendentals=0
            ),
            name="transmit",
        )(
            *map(near, packs[which * per_tile : (which + 1) * per_tile]),
            near(amp),
            near(turned),
            near(sym),
            near(both),
            far(table),
            near(twist),
            *map(near, out),
        )
    out = out[0].transpose(0, 1, 3, 2, 4)
    return out.reshape(1, antennas, 2, syms, NFFT)


def solution(mesh):
    in_specs = (
        P("cell", "lane", None, None, None),
        P("cell", None, None, None, None),
        P("cell", None),
        P("cell", None, None),
        P("cell", None),
        P(),
        P(),
    )
    out_specs = P("cell", "lane", None, None, None)
    return jax.shard_map(
        per_device, mesh=mesh, in_specs=in_specs, out_specs=out_specs, check_vma=False
    )
```
